32 devices in a mesh: samp: 4 (over y, core), sp: 8 (over z, x).
Axes of the slice: x: 2, y: 2, z: 4, core: 2. Of those that a mesh axis runs over, the one named last changes fastest.
Arguments:
- tokens: bfloat16 [4, 96, 160, 768], P('samp', 'sp'), may hold values from -6 to 6
- cotangent: bfloat16 [4, 96, 160, 768], P('samp', 'sp'), may hold values from -6 to 6
- storm_weight: int32 [4], P('samp'), may hold values from 16 to 192
- filter_master: float32 [768, 384], P(('samp', 'sp')), may hold values from -0.4375 to 0.4375
- in_master: float32 [768, 3072], P(('samp', 'sp')), may hold values from -0.21875 to 0.21875
- out_master: float32 [3072, 768], P(('samp', 'sp')), may hold values from -0.109375 to 0.109375
- small_master: float32 [9984], P(('samp', 'sp')), may hold values from -1.2 to 1.6, as said below
- filter_m: float32 [768, 384], P(('samp', 'sp')), may hold values from -128 to 128
- filter_v: float32 [768, 384], P(('samp', 'sp')), may hold values from 1536 to 6144
- in_m: float32 [768, 3072], P(('samp', 'sp')), may hold values from -96 to 96
- in_v: float32 [768, 3072], P(('samp', 'sp')), may hold values from 921.6 to 3686.4
- out_m: float32 [3072, 768], P(('samp', 'sp')), may hold values from -192 to 192
- out_v: float32 [3072, 768], P(('samp', 'sp')), may hold values from 4300.8 to 17203.2
- small_m: float32 [9984], P(('samp', 'sp')), may hold values from -160 to 160
- small_v: float32 [9984], P(('samp', 'sp')), may hold values from 3072 to 12288
- filter_ema: float32 [768, 384], P(('samp', 'sp')), may hold values from -0.4375 to 0.4375
- in_ema: float32 [768, 3072], P(('samp', 'sp')), may hold values from -0.21875 to 0.21875
- out_ema: float32 [3072, 768], P(('samp', 'sp')), may hold values from -0.109375 to 0.109375
- small_ema: float32 [9984], P(('samp', 'sp')), may hold values from 0.5 to 1.5
Outputs:
- result: bfloat16 [4, 96, 160, 768], P('samp', 'sp')
- input_grad: float32 [4, 96, 160, 768], P('samp', 'sp')
- filter_grad: float32 [768, 384], P(('samp', 'sp'))
- in_grad: float32 [768, 3072], P(('samp', 'sp'))
- out_grad: float32 [3072, 768], P(('samp', 'sp'))
- small_grad: float32 [9984], P(('samp', 'sp'))
- filter_new: float32 [768, 384], P(('samp', 'sp'))
- in_new: float32 [768, 3072], P(('samp', 'sp'))
- out_new: float32 [3072, 768], P(('samp', 'sp'))
- small_new: float32 [9984], P(('samp', 'sp'))
- filter_m_new: float32 [768, 384], P(('samp', 'sp'))
- filter_v_new: float32 [768, 384], P(('samp', 'sp'))
- in_m_new: float32 [768, 3072], P(('samp', 'sp'))
- in_v_new: float32 [768, 3072], P(('samp', 'sp'))
- out_m_new: float32 [3072, 768], P(('samp', 'sp'))
- out_v_new: float32 [3072, 768], P(('samp', 'sp'))
- small_m_new: float32 [9984], P(('samp', 'sp'))
- small_v_new: float32 [9984], P(('samp', 'sp'))
- filter_ema_new: float32 [768, 384], P(('samp', 'sp'))
- in_ema_new: float32 [768, 3072], P(('samp', 'sp'))
- out_ema_new: float32 [3072, 768], P(('samp', 'sp'))
- small_ema_new: float32 [9984], P(('samp', 'sp'))
The draws below stay inside these ranges and needn't reach their ends.
Inputs may be any that keep to these rules, and one draw needn't show every extreme that they name: `small_master`: rows 0 and 2 of the small vector are gains, the others biases.
All inputs are finite; a program needn't handle non-finite values.
Results may differ from the reference program's by a relative error of at most 0.014.
Values may be sent and summed in bfloat16 or wider, within the bound.
No kernel may reach another device: no remote copies, remote signals or barrier semaphores. Data moves between devices by JAX's collectives and lax.ppermute only.
A program may use at most 320 MiB of HBM per device.

```python
import math
import jax
import jax.numpy as jnp
from jax import lax

D = 768
FF = 3072
NB = 8
H = 96
W = 160
STEP = 10
BS = 96
S = 4
TOKENS = 61440


def draw_small_master(key, part):
    key = jax.random.fold_in(key, 7)
    noise_draw = jnp.clip(jax.random.normal(key, (13, D), jnp.float32), -4.0, 4.0)
    row_index = jnp.arange(13, dtype=jnp.int32)[:, None]
    gain_rows = (row_index == 0) | (row_index == 2)
    values = jnp.where(gain_rows, 1.0 + 0.15 * noise_draw, 0.3 * noise_draw)
    return values.reshape(13 * D)


def plant(array, rng, least, high):
    longest = array.shape.index(max(array.shape))
    spots = []
    for shift in (0, 1):
        where = [jax.random.randint(jax.random.fold_in(rng, axis), (), 0, length) for axis, length in enumerate(array.shape)]
        where[longest] = (where[longest] + shift) % array.shape[longest]
        spots.append(tuple(where))
    return array.at[spots[0]].set(least).at[spots[1]].set(high)


def levels(rng, dims, cuts, least, top_value):
    def one(dim, parts):
        steps = jax.random.uniform(jax.random.fold_in(jax.random.fold_in(rng, 6), dim), (parts,), jnp.float32, least / len(cuts), top_value / len(cuts))
        return jnp.repeat(jnp.exp(steps), dims[dim] // parts).reshape((-1,) + (1,) * (len(dims) - dim - 1))

    factor_of = one(*cuts[0])
    for cut in cuts[1:]:
        factor_of = factor_of * one(*cut)
    return factor_of


def centred(stream_key, extent, deviation, bound, cuts=(), kind=jnp.bfloat16):
    factor_of = levels(stream_key, extent, cuts, -0.22, 0.18) if cuts else 1.0
    values = jax.random.normal(stream_key, extent, jnp.float32) * deviation * factor_of
    return jnp.minimum(jnp.maximum(values, -bound), bound).astype(kind)


def setup_inputs(seed: int = 0) -> dict:
    key_list = jax.random.split(jax.random.key(seed), 20)
    return {
        "tokens": centred(key_list[0], (S, H, W, D), 1.0, 6.0, ((0, 4), (1, 8))),
        "cotangent": centred(key_list[1], (S, H, W, D), 1.0, 6.0, ((0, 4), (1, 8))),
        "storm_weight": plant(jax.random.randint(key_list[2], (S,), 16, 193), jax.random.fold_in(key_list[2], 1), 16, 192).astype(jnp.int32),
        "filter_master": centred(key_list[3], (D, 4 * BS), (2 * BS) ** -0.5, 0.4375, ((0, 32),), jnp.float32),
        "in_master": centred(key_list[4], (D, FF), D ** -0.5, 0.21875, ((0, 32),), jnp.float32),
        "out_master": centred(key_list[5], (FF, D), FF ** -0.5, 0.109375, ((0, 32),), jnp.float32),
        "small_master": draw_small_master(jax.random.fold_in(key_list[19], 71), 0),
        "filter_m": centred(key_list[7], (D, 4 * BS), (0.08 * TOKENS ** 0.5), 128.0, ((0, 32),), jnp.float32),
        "filter_v": jnp.clip(jnp.exp(math.log(6144.0) - 1.3862944 * jax.random.uniform(key_list[8], (D, 4 * BS), jnp.float32) ** levels(key_list[8], (D, 4 * BS), ((0, 32),), -0.2, 0.2)), 1536.0, 6144.0),
        "in_m": centred(key_list[9], (D, FF), (0.06 * TOKENS ** 0.5), 96.0, ((0, 32),), jnp.float32),
        "in_v": jnp.clip(jnp.exp(math.log(3686.4) - 1.3862944 * jax.random.uniform(key_list[10], (D, FF), jnp.float32) ** levels(key_list[10], (D, FF), ((0, 32),), -0.2, 0.2)), 921.6, 3686.4),
        "out_m": centred(key_list[11], (FF, D), (0.13 * TOKENS ** 0.5), 192.0, ((0, 32),), jnp.float32),
        "out_v": jnp.clip(jnp.exp(math.log(17203.2) - 1.3862944 * jax.random.uniform(key_list[12], (FF, D), jnp.float32) ** levels(key_list[12], (FF, D), ((0, 32),), -0.2, 0.2)), 4300.8, 17203.2),
        "small_m": centred(key_list[13], (13 * D,), (0.11 * TOKENS ** 0.5), 160.0, ((0, 32),), jnp.float32),
        "small_v": jnp.clip(jnp.exp(math.log(12288.0) - 1.3862944 * jax.random.uniform(key_list[14], (13 * D,), jnp.float32) ** levels(key_list[14], (13 * D,), ((0, 32),), -0.2, 0.2)), 3072.0, 12288.0),
        "filter_ema": centred(key_list[15], (D, 4 * BS), (2 * BS) ** -0.5, 0.4375, ((0, 32),), jnp.float32),
        "in_ema": centred(key_list[16], (D, FF), D ** -0.5, 0.21875, ((0, 32),), jnp.float32),
        "out_ema": centred(key_list[17], (FF, D), FF ** -0.5, 0.109375, ((0, 32),), jnp.float32),
        "small_ema": jnp.clip(1.0 + 0.1 * jax.random.normal(key_list[18], (13 * D,), jnp.float32), 0.5, 1.5),
    }


HIGHEST = lax.Precision.HIGHEST
NORM_EPS = 1e-05
BETA_ONE = 0.9
BETA_TWO = 0.95
ADAM_EPS = 1e-08
DECAY = 0.05
EMA_KEEP = 0.75

@jax.custom_vjp
def low(v):
    return lax.optimization_barrier(v.astype(jnp.bfloat16)).astype(jnp.float32)

@jax.custom_vjp
def low_back(v):
    return v

def low_keep(v):
    return (low(v), None)

def low_pass(kept, grad):
    return (grad,)

def back_keep(v):
    return (v, None)

def back_low(kept, grad):
    return (low(grad),)
low.defvjp(low_keep, low_pass)
low_back.defvjp(back_keep, back_low)

def gelu_exact(values):
    return jax.nn.gelu(values, approximate=False)

def layer_norm(values, gain, shift):
    center = values - lax.optimization_barrier(jnp.mean(values, axis=-1, keepdims=True))
    spread = lax.optimization_barrier(jnp.mean(center * center, axis=-1, keepdims=True))
    return center * lax.rsqrt(spread + NORM_EPS) * gain + shift

def block_mix(part_re, part_im, weight_re, weight_im):
    grouped_re = part_re.reshape(part_re.shape[:-1] + (NB, BS))
    grouped_im = part_im.reshape(part_im.shape[:-1] + (NB, BS))
    matrix_re = weight_re.reshape(NB, BS, BS)
    matrix_im = weight_im.reshape(NB, BS, BS)

    def product(left, right):
        return jnp.einsum('hwbi,bio->hwbo', left, right, precision=HIGHEST).reshape(part_re.shape)
    out_re = product(grouped_re, matrix_re) - product(grouped_im, matrix_im)
    out_im = product(grouped_im, matrix_re) + product(grouped_re, matrix_im)
    return (out_re, out_im)

def sample_forward(inputs, filter_master, in_master, out_master, small_master):
    filter_w = low(filter_master)
    in_w = low(in_master)
    out_w = low(out_master)
    params = low(small_master).reshape(13, D)
    first = layer_norm(inputs, params[0], params[1])
    spectrum = jnp.fft.fft(first, axis=1, norm='ortho')
    spec_re = low_back(low(jnp.real(spectrum)))
    spec_im = low_back(low(jnp.imag(spectrum)))
    modes = jnp.fft.fft(lax.complex(spec_re, spec_im), axis=0, norm='ortho')
    modes_re = low(jnp.real(modes))
    modes_im = low(jnp.imag(modes))
    pre_re, pre_im = block_mix(modes_re, modes_im, filter_w[:, 0:BS], filter_w[:, BS:2 * BS])
    pre_re = low_back(pre_re + params[4])
    pre_im = low_back(pre_im + params[5])
    hidden_re = low(gelu_exact(pre_re))
    hidden_im = low(gelu_exact(pre_im))
    two_re, two_im = block_mix(hidden_re, hidden_im, filter_w[:, 2 * BS:3 * BS], filter_w[:, 3 * BS:4 * BS])
    two_re = low_back(two_re + params[6])
    two_im = low_back(two_im + params[7])
    back = jnp.fft.ifft(lax.complex(two_re, two_im), axis=0, norm='ortho')
    back_re = low_back(low(jnp.real(back)))
    back_im = low_back(low(jnp.imag(back)))
    spatial = jnp.real(jnp.fft.ifft(lax.complex(back_re, back_im), axis=1, norm='ortho'))
    mixed = spatial + first + inputs
    second = low(layer_norm(mixed, params[2], params[3]))
    pre_dense = low_back(jnp.einsum('hwd,df->hwf', second, in_w, precision=HIGHEST) + params[9:13].reshape(FF))
    act_dense = low(gelu_exact(pre_dense))
    branch = low_back(jnp.einsum('hwf,fd->hwd', act_dense, out_w, precision=HIGHEST) + params[8])
    return mixed + branch

def adam_update(master, gradient, moment, second, average, step_rate):
    moment_new = BETA_ONE * moment + (1.0 - BETA_ONE) * gradient
    second_new = BETA_TWO * second + (1.0 - BETA_TWO) * gradient * gradient
    scaled_moment = moment_new / (1.0 - BETA_ONE ** STEP)
    scaled_second = second_new / (1.0 - BETA_TWO ** STEP)
    master_new = master - step_rate * (scaled_moment / (jnp.sqrt(scaled_second) + ADAM_EPS) + DECAY * master)
    average_new = EMA_KEEP * average + (1.0 - EMA_KEEP) * master_new
    return (master_new, moment_new, second_new, average_new)

def reference(tokens, cotangent, storm_weight, filter_master, in_master, out_master, small_master, filter_m, filter_v, in_m, in_v, out_m, out_v, small_m, small_v, filter_ema, in_ema, out_ema, small_ema):
    masters = (filter_master, in_master, out_master, small_master)

    def one_sample(running, sample_items):
        sample_tokens, sample_cot, sample_storm = sample_items
        values, pull_back = jax.vjp(sample_forward, sample_tokens.astype(jnp.float32), filter_master, in_master, out_master, small_master)
        scale_value = sample_storm.astype(jnp.float32) / 64.0
        gradients = pull_back(sample_cot.astype(jnp.float32) * scale_value)
        running = tuple((summed + piece_grad for summed, piece_grad in zip(running, gradients[1:])))
        return (running, (values.astype(jnp.bfloat16), gradients[0]))
    zeros_init = tuple((jnp.zeros_like(master) for master in masters))
    totals, outputs = lax.scan(one_sample, zeros_init, (tokens, cotangent, storm_weight))
    result, input_grad = outputs
    filter_grad, in_grad, out_grad, small_grad = totals
    filter_new, filter_m_new, filter_v_new, filter_ema_new = adam_update(filter_master, filter_grad, filter_m, filter_v, filter_ema, 0.2)
    in_new, in_m_new, in_v_new, in_ema_new = adam_update(in_master, in_grad, in_m, in_v, in_ema, 0.1)
    out_new, out_m_new, out_v_new, out_ema_new = adam_update(out_master, out_grad, out_m, out_v, out_ema, 0.05)
    small_new, small_m_new, small_v_new, small_ema_new = adam_update(small_master, small_grad, small_m, small_v, small_ema, 0.5)
    return (result, input_grad, filter_grad, in_grad, out_grad, small_grad, filter_new, in_new, out_new, small_new, filter_m_new, filter_v_new, in_m_new, in_v_new, out_m_new, out_v_new, small_m_new, small_v_new, filter_ema_new, in_ema_new, out_ema_new, small_ema_new)
```

```python
import functools
import math

import jax
import jax.numpy as jnp
import numpy as np
from jax import lax
from jax.experimental import pallas as pl
from jax.experimental.pallas import tpu as pltpu
from jax.sharding import PartitionSpec as P

NB = 8
STEP = 10


HIGHEST = lax.Precision.HIGHEST
NORM_EPS = 1e-05
BETA_ONE = 0.9
BETA_TWO = 0.95
ADAM_EPS = 1e-08
DECAY = 0.05
EMA_KEEP = 0.75


def gelu_exact(values):
    return jax.nn.gelu(values, approximate=False)


def norm_forward(values):
    center = values - jnp.mean(values, axis=-1, keepdims=True)
    inv_std = lax.rsqrt(jnp.mean(center * center, axis=-1, keepdims=True) + NORM_EPS)
    return (center * inv_std, inv_std)


def norm_back(upstream, normed, inv_std, gain):
    scaled = upstream * gain
    first_mean = jnp.mean(scaled, axis=-1, keepdims=True)
    second_mean = jnp.mean(scaled * normed, axis=-1, keepdims=True)
    leading = tuple(range(upstream.ndim - 1))
    input_part = inv_std * (scaled - first_mean - normed * second_mean)
    return (input_part, jnp.sum(upstream * normed, axis=leading), jnp.sum(upstream, axis=leading))


def dft_table(points):
    positions = jnp.arange(points, dtype=jnp.int32)
    phases = positions[:, None] * positions[None, :] % points
    angles = phases.astype(jnp.float32) * (2.0 * math.pi / points)
    factor = 1.0 / math.sqrt(points)
    return (jnp.cos(angles) * factor, jnp.sin(angles) * factor)


def lat_table(cosine, sine_part, sign_value):
    upper_rows = jnp.stack([cosine, -sign_value * sine_part], axis=-1)
    lower_rows = jnp.stack([sign_value * sine_part, cosine], axis=-1)
    return jnp.stack([upper_rows, lower_rows], axis=1)


def split_table(table):
    upper_part = table.astype(jnp.bfloat16)
    lower_part = (table - upper_part.astype(jnp.float32)).astype(jnp.bfloat16)
    return (upper_part, lower_part)


def table_first(form, table, values):
    upper_part, lower_part = split_table(table)
    return jnp.einsum(form, upper_part, values, preferred_element_type=jnp.float32) + jnp.einsum(
        form, lower_part, values, preferred_element_type=jnp.float32
    )


def table_second(form, values, table):
    upper_part, lower_part = split_table(table)
    return jnp.einsum(form, values, upper_part, preferred_element_type=jnp.float32) + jnp.einsum(
        form, values, lower_part, preferred_element_type=jnp.float32
    )


def complex_mix(inputs, weight):
    shape_in = inputs.shape
    size_block = weight.shape[1] // 2
    grouped = inputs.reshape(shape_in[:4] + (NB, size_block))
    matrices = weight.reshape(NB, size_block, 2, size_block)
    product = jnp.einsum(
        "sgckbi,bieo->sgcekbo", grouped, matrices, preferred_element_type=jnp.float32
    )
    real_part = product[:, :, 0, 0] - product[:, :, 1, 1]
    imag_part = product[:, :, 1, 0] + product[:, :, 0, 1]
    return jnp.stack([real_part, imag_part], axis=2).reshape(shape_in)


def mix_back(upstream, inputs, weight):
    shape_in = inputs.shape
    size_block = weight.shape[1] // 2
    grouped = inputs.reshape(shape_in[:4] + (NB, size_block))
    upstream_grouped = upstream.reshape(shape_in[:4] + (NB, size_block))
    matrices = weight.reshape(NB, size_block, 2, size_block)
    toward = jnp.einsum(
        "sgekbo,bico->sgeckbi", upstream_grouped, matrices, preferred_element_type=jnp.float32
    )
    grad_real = toward[:, :, 0, 0] + toward[:, :, 1, 1]
    grad_imag = toward[:, :, 1, 0] - toward[:, :, 0, 1]
    grad_inputs = jnp.stack([grad_real, grad_imag], axis=2).reshape(shape_in)
    outer_sums = jnp.einsum(
        "sgckbi,sgekbo->cebio", grouped, upstream_grouped, preferred_element_type=jnp.float32
    )
    weight_real = outer_sums[0, 0] + outer_sums[1, 1]
    weight_imag = outer_sums[0, 1] - outer_sums[1, 0]
    weight_grad = jnp.stack([weight_real, weight_imag], axis=2).reshape(weight.shape)
    bias_grad = jnp.sum(upstream, axis=(0, 1, 3), dtype=jnp.float32)
    return (grad_inputs, weight_grad, bias_grad)


def adam_update(master, gradient, moment, second, average, step_rate):
    moment_new = BETA_ONE * moment + (1.0 - BETA_ONE) * gradient
    second_new = BETA_TWO * second + (1.0 - BETA_TWO) * gradient * gradient
    scaled_moment = moment_new / (1.0 - BETA_ONE**STEP)
    scaled_second = second_new / (1.0 - BETA_TWO**STEP)
    master_new = master - step_rate * (
        scaled_moment / (jnp.sqrt(scaled_second) + ADAM_EPS) + DECAY * master
    )
    average_new = EMA_KEEP * average + (1.0 - EMA_KEEP) * master_new
    return (master_new, moment_new, second_new, average_new)


def plain_shards(
    tokens,
    cotangent,
    storm_weight,
    filter_master,
    in_master,
    out_master,
    small_master,
    filter_m,
    filter_v,
    in_m,
    in_v,
    out_m,
    out_v,
    small_m,
    small_v,
    filter_ema,
    in_ema,
    out_ema,
    small_ema,
):
    filter_work, small_work = (
        lax.all_gather(filter_master.astype(jnp.bfloat16), ("samp", "sp"), axis=0, tiled=True),
        lax.all_gather(small_master.astype(jnp.bfloat16), ("samp", "sp"), axis=0, tiled=True),
    )
    width = filter_work.shape[0]
    size_block = width // NB
    params = small_work.astype(jnp.float32).reshape(13, width)
    inputs = tokens.astype(jnp.float32)
    normed_one, inv_one = norm_forward(inputs)
    first = normed_one * params[0] + params[1]
    lon_cos, lon_sin = dft_table(tokens.shape[2])
    lon_forward = jnp.stack([lon_cos, -lon_sin], axis=1)
    lon_inverse = jnp.stack([lon_cos, -lon_sin], axis=0)
    spectrum = jnp.einsum("shwd,wck->shckd", first, lon_forward, precision=HIGHEST).astype(
        jnp.bfloat16
    )
    arrived = lax.all_to_all(spectrum, "sp", split_axis=3, concat_axis=1, tiled=True)
    lat_cos, lat_sin = dft_table(arrived.shape[1])
    lat_forward = lat_table(lat_cos, lat_sin, -1.0)
    lat_inverse = lat_table(lat_cos, lat_sin, 1.0)
    modes = table_first("gohc,shckd->sgokd", lat_forward, arrived).astype(jnp.bfloat16)
    bias_one = params[4:6][:, None, :]
    bias_two = params[6:8][:, None, :]
    pre_one = complex_mix(modes, filter_work[:, : 2 * size_block]) + bias_one
    hidden_one = gelu_exact(pre_one).astype(jnp.bfloat16)
    pre_two = complex_mix(hidden_one, filter_work[:, 2 * size_block :]) + bias_two
    leaving = jnp.einsum("gohc,shckd->sgokd", lat_inverse, pre_two, precision=HIGHEST).astype(
        jnp.bfloat16
    )
    returned = lax.all_to_all(leaving, "sp", split_axis=1, concat_axis=3, tiled=True)
    spatial = table_second("shckd,ckw->shwd", returned, lon_inverse)
    mixed = spatial + first + inputs
    in_work, out_work = (
        lax.all_gather(in_master.astype(jnp.bfloat16), ("samp", "sp"), axis=0, tiled=True),
        lax.all_gather(out_master.astype(jnp.bfloat16), ("samp", "sp"), axis=0, tiled=True),
    )
    normed_two, inv_two = norm_forward(mixed)
    second = (normed_two * params[2] + params[3]).astype(jnp.bfloat16).reshape(-1, width)
    pre_dense = jnp.dot(second, in_work, preferred_element_type=jnp.float32) + params[9:13].reshape(
        -1
    )
    act_dense = gelu_exact(pre_dense).astype(jnp.bfloat16)
    branch = jnp.dot(act_dense, out_work, preferred_element_type=jnp.float32) + params[8]
    result = (mixed + branch.reshape(mixed.shape)).astype(jnp.bfloat16)
    filter_back = lax.all_gather(
        filter_master.astype(jnp.bfloat16), ("samp", "sp"), axis=0, tiled=True
    )
    in_back, out_back = (
        lax.all_gather(in_master.astype(jnp.bfloat16), ("samp", "sp"), axis=0, tiled=True),
        lax.all_gather(out_master.astype(jnp.bfloat16), ("samp", "sp"), axis=0, tiled=True),
    )
    sample_scale = storm_weight.astype(jnp.float32)[:, None, None, None] / 64.0
    grad_out = cotangent.astype(jnp.float32) * sample_scale
    grad_low = grad_out.astype(jnp.bfloat16).reshape(-1, width)
    out_local = jnp.einsum("tf,td->fd", act_dense, grad_low, preferred_element_type=jnp.float32)
    out_bias_grad = jnp.sum(grad_low, axis=0, dtype=jnp.float32)
    grad_act = jnp.einsum("td,fd->tf", grad_low, out_back, preferred_element_type=jnp.float32)
    dense_values, dense_pull = jax.vjp(gelu_exact, pre_dense)
    grad_pre = dense_pull(grad_act)[0].astype(jnp.bfloat16)
    in_local = jnp.einsum("td,tf->df", second, grad_pre, preferred_element_type=jnp.float32)
    in_bias_grad = jnp.sum(grad_pre, axis=0, dtype=jnp.float32)
    grad_second = jnp.einsum(
        "tf,df->td", grad_pre, in_back, preferred_element_type=jnp.float32
    ).reshape(mixed.shape)
    grad_norm_two, gain_two_grad, shift_two_grad = norm_back(
        grad_second, normed_two, inv_two, params[2]
    )
    grad_mixed = grad_out + grad_norm_two
    grad_leaving = jnp.einsum("shwd,ckw->shckd", grad_mixed, lon_inverse, precision=HIGHEST).astype(
        jnp.bfloat16
    )
    grad_arrived = lax.all_to_all(grad_leaving, "sp", split_axis=3, concat_axis=1, tiled=True)
    grad_pre_two = table_first("gohc,sgokd->shckd", lat_inverse, grad_arrived).astype(jnp.bfloat16)
    grad_hidden, weight_two_grad, bias_two_grad = mix_back(
        grad_pre_two, hidden_one, filter_back[:, 2 * size_block :]
    )
    gelu_values, gelu_pull = jax.vjp(gelu_exact, pre_one)
    grad_pre_one = gelu_pull(grad_hidden)[0].astype(jnp.bfloat16)
    grad_modes, weight_one_grad, bias_one_grad = mix_back(
        grad_pre_one, modes, filter_back[:, : 2 * size_block]
    )
    grad_spectrum = jnp.einsum(
        "gohc,sgokd->shckd", lat_forward, grad_modes, precision=HIGHEST
    ).astype(jnp.bfloat16)
    grad_sent = lax.all_to_all(grad_spectrum, "sp", split_axis=1, concat_axis=3, tiled=True)
    grad_first = grad_mixed + table_second("shckd,wck->shwd", grad_sent, lon_forward)
    grad_norm_one, gain_one_grad, shift_one_grad = norm_back(
        grad_first, normed_one, inv_one, params[0]
    )
    input_grad = grad_mixed + grad_norm_one
    norm_rows = jnp.stack([gain_one_grad, shift_one_grad, gain_two_grad, shift_two_grad])
    small_local = jnp.concatenate(
        [
            norm_rows,
            bias_one_grad,
            bias_two_grad,
            out_bias_grad[None, :],
            in_bias_grad.reshape(-1, width),
        ],
        axis=0,
    ).reshape(-1)
    filter_local = jnp.concatenate([weight_one_grad, weight_two_grad], axis=1)
    filter_grad, in_grad, out_grad, small_grad = (
        lax.psum_scatter(filter_local, ("samp", "sp"), scatter_dimension=0, tiled=True),
        lax.psum_scatter(in_local, ("samp", "sp"), scatter_dimension=0, tiled=True),
        lax.psum_scatter(out_local, ("samp", "sp"), scatter_dimension=0, tiled=True),
        lax.psum_scatter(small_local, ("samp", "sp"), scatter_dimension=0, tiled=True),
    )
    filter_new, filter_m_new, filter_v_new, filter_ema_new = adam_update(
        filter_master, filter_grad, filter_m, filter_v, filter_ema, 0.2
    )
    in_new, in_m_new, in_v_new, in_ema_new = adam_update(
        in_master, in_grad, in_m, in_v, in_ema, 0.1
    )
    out_new, out_m_new, out_v_new, out_ema_new = adam_update(
        out_master, out_grad, out_m, out_v, out_ema, 0.05
    )
    small_new, small_m_new, small_v_new, small_ema_new = adam_update(
        small_master, small_grad, small_m, small_v, small_ema, 0.5
    )
    return (
        result,
        input_grad,
        filter_grad,
        in_grad,
        out_grad,
        small_grad,
        filter_new,
        in_new,
        out_new,
        small_new,
        filter_m_new,
        filter_v_new,
        in_m_new,
        in_v_new,
        out_m_new,
        out_v_new,
        small_m_new,
        small_v_new,
        filter_ema_new,
        in_ema_new,
        out_ema_new,
        small_ema_new,
    )


F32 = jnp.float32
BF16 = jnp.bfloat16
LAT = 96
LON = 160
GROUP = 4
HALF = 384
ROWS = 208
FCHUNK = 512
VMEM_BYTES = 56 * 1024 * 1024
SCHED = pltpu.CompilerParams(vmem_limit_bytes=VMEM_BYTES)


def fits(parts):
    return LAT % (parts * GROUP) == 0 and LON // 2 % (2 * parts) == 0


def dot(left, right, left_dim, right_dim):
    return lax.dot_general(
        left, right, (((left_dim,), (right_dim,)), ((), ())), preferred_element_type=F32
    )


def gelu_pair(values):
    cdf = 0.5 + 0.5 * lax.erf(values * math.sqrt(0.5))
    pdf = jnp.exp2(values * values * (-0.5 * math.log2(math.e))) * (1.0 / math.sqrt(2.0 * math.pi))
    return (values * cdf, cdf + values * pdf)


@functools.lru_cache(maxsize=None)
def lon_matrix():
    slots = LON // 2
    points = np.arange(LON)
    table = np.zeros((slots, 2, LON))
    for slot in range(slots):
        angles = 2.0 * np.pi * (slot * points % LON) / LON
        table[slot, 0] = np.cos(angles)
        table[slot, 1] = -np.sin(angles)
    table[0, 1] = np.where(points % 2 == 0, 1.0, -1.0)
    table /= np.sqrt(LON)
    full = np.zeros((slots, 2, GROUP, GROUP, LON))
    for row in range(GROUP):
        full[:, :, row, row, :] = table
    return full.reshape(slots * 2 * GROUP, GROUP * LON)


@functools.lru_cache(maxsize=None)
def lat_matrices(parts):
    per_part = LAT // parts
    groups = per_part // GROUP
    forward = np.zeros((2, 2, ROWS, LAT, 2, 2))
    share = np.zeros((2, ROWS))
    lat = np.arange(LAT)

    def put_plain(variant, start, slot):
        for mode in range(LAT):
            angles = 2.0 * np.pi * (mode * lat % LAT) / LAT
            forward[variant, 0, start + mode, :, slot, 0] = np.cos(angles)
            forward[variant, 0, start + mode, :, slot, 1] = np.sin(angles)
            forward[variant, 1, start + mode, :, slot, 0] = -np.sin(angles)
            forward[variant, 1, start + mode, :, slot, 1] = np.cos(angles)
            share[variant, start + mode] = 1.0

    half = LAT // 2 + 1
    for column in range(2):
        for mode in range(half):
            angles = 2.0 * np.pi * (mode * lat % LAT) / LAT
            row = column * half + mode
            own = mode in (0, LAT // 2)
            forward[0, 0, row, :, 0, column] = np.cos(angles)
            forward[0, 1, row, :, 0, column] = 0.0 if own else -np.sin(angles)
            share[0, row] = 0.5 if own else 1.0
    put_plain(0, 2 * half, 1)
    put_plain(1, 0, 0)
    put_plain(1, LAT, 1)
    forward /= np.sqrt(LAT)
    forward = forward.reshape(2, 2, ROWS, parts, groups, GROUP, 2, 2)
    forward = forward.transpose(0, 1, 2, 3, 4, 6, 7, 5)
    shift_row = np.zeros((2, ROWS, 128))
    shift_row[0, 0] = np.sqrt(LAT * LON)
    return (forward, share, shift_row)


def lat_tables(parts):
    forward, share, shift_row = lat_matrices(parts)
    tall = 2 * ROWS
    wide = forward[0].size // tall
    by_part = forward.reshape(2, tall, wide)
    by_group = forward.transpose(0, 1, 2, 4, 3, 5, 6, 7).reshape(2, tall, wide)
    weights = np.concatenate([share, share], axis=1)[:, :, None]
    tables = (
        by_part,
        (weights * by_group).transpose(0, 2, 1),
        weights * by_group,
        by_part.transpose(0, 2, 1),
    )
    return tuple(jnp.asarray(table, BF16) for table in tables) + (jnp.asarray(shift_row, F32),)


def normalise(values):
    center = values - jnp.mean(values, axis=-1, keepdims=True)
    inv_std = lax.rsqrt(jnp.mean(center * center, axis=-1, keepdims=True) + NORM_EPS)
    return (center * inv_std, inv_std)


def spread_body(tokens_ref, table_ref, low_ref, high_ref):
    values = tokens_ref[...].astype(F32).reshape(GROUP * LON, 2 * HALF)
    normed, _ = normalise(values)
    out = dot(table_ref[...], normed.astype(BF16), 1, 0).astype(BF16)
    low_ref[...] = out[:, :HALF].reshape(low_ref.shape)
    high_ref[...] = out[:, HALF:].reshape(high_ref.shape)


def spread(tokens, table, parts):
    groups = tokens.shape[1] // GROUP
    pairs = LON // 4 // parts
    shape = (parts, groups, pairs, 16, HALF)
    block = pl.BlockSpec((parts, 1, pairs, 16, HALF), lambda r: (0, r, 0, 0, 0))
    return pl.pallas_call(
        spread_body,
        name="norm_and_longitude",
        grid=(groups,),
        in_specs=[
            pl.BlockSpec((1, GROUP, LON, 2 * HALF), lambda r: (0, r, 0, 0)),
            pl.BlockSpec(table.shape, lambda r: (0, 0)),
        ],
        out_specs=[block, block],
        out_shape=[jax.ShapeDtypeStruct(shape, BF16)] * 2,
        compiler_params=SCHED,
    )(tokens, table)


def filter_body(
    groups,
    pick_ref,
    arrived_ref,
    forward_ref,
    inverse_ref,
    shift_row_ref,
    params_ref,
    one_ref,
    two_ref,
    *outs,
):
    back_refs = outs[:groups]
    modes_ref, sums_ref, slopes_ref = outs[groups:]
    columns = forward_ref.shape[-1]
    arrived = arrived_ref[...].reshape(columns, HALF)
    raw = dot(forward_ref[0], arrived, 1, 0)
    gain = params_ref[0:1, :]
    shift = params_ref[1:2, :]
    modes_re = (raw[:ROWS] * gain + shift_row_ref[0, :, 0:1] * shift).astype(BF16)
    modes_im = (raw[ROWS:] * gain).astype(BF16)
    modes_ref[0, :ROWS] = modes_re
    modes_ref[0, ROWS:] = modes_im
    from_re = dot(modes_re, one_ref[0], 1, 0)
    from_im = dot(modes_im, one_ref[0], 1, 0)
    bias_re = params_ref[4:5, :]
    bias_im = params_ref[5:6, :]
    re_a = from_re[:, :HALF] + bias_re
    re_b = from_re[:, HALF:] + bias_im
    im_a = from_im[:, :HALF]
    im_b = from_im[:, HALF:]
    plus_re, slope = gelu_pair(re_a - im_b)
    slopes_ref[0, 0] = slope.astype(BF16)
    minus_re, slope = gelu_pair(re_a + im_b)
    slopes_ref[0, 1] = slope.astype(BF16)
    sums_ref[0, 0, :, :HALF] = (plus_re + minus_re).astype(BF16)
    sums_ref[0, 1, :, HALF:] = (plus_re - minus_re).astype(BF16)
    plus_im, slope = gelu_pair(re_b + im_a)
    slopes_ref[0, 2] = slope.astype(BF16)
    minus_im, slope = gelu_pair(re_b - im_a)
    slopes_ref[0, 3] = slope.astype(BF16)
    sums_ref[0, 0, :, HALF:] = (-plus_im - minus_im).astype(BF16)
    sums_ref[0, 1, :, :HALF] = (plus_im - minus_im).astype(BF16)
    two_bias_re = params_ref[6:7, :]
    two_bias_im = params_ref[7:8, :]
    two_re = dot(sums_ref[0, 0], two_ref[0], 1, 0) + (two_bias_re + two_bias_re)
    two_im = dot(sums_ref[0, 1], two_ref[0], 1, 0) + (two_bias_im - two_bias_im)
    both = jnp.concatenate([two_re.astype(BF16), two_im.astype(BF16)], axis=0)
    back = dot(inverse_ref[0], both, 1, 0).astype(BF16)
    step = columns // groups
    for group in range(groups):
        ref = back_refs[group]
        ref[...] = back[group * step : (group + 1) * step].reshape(ref.shape)


def filter_forward(pick, arrived, tables, params, one, two, part_of_channels):
    parts, groups, pairs = arrived.shape[:3]
    forward, inverse, _, _, shift_row = tables
    q = part_of_channels
    tall = 2 * ROWS

    def chosen(*shape):
        return pl.BlockSpec((1,) + shape, lambda b, pick_ref: (pick_ref[b], 0, 0))

    def fixed(*shape):
        return pl.BlockSpec((1,) + shape, lambda b, pick_ref: (q, 0, 0))

    def stepped(*shape):
        zeros = (0,) * len(shape)
        return pl.BlockSpec((1,) + shape, lambda b, pick_ref: (b,) + zeros)

    back_block = pl.BlockSpec((parts, 1, 16, HALF), lambda b, pick_ref: (0, b, 0, 0))
    columns = forward.shape[-1]
    return pl.pallas_call(
        functools.partial(filter_body, groups),
        name="filter_forward",
        grid_spec=pltpu.PrefetchScalarGridSpec(
            num_scalar_prefetch=1,
            grid=(pairs,),
            in_specs=[
                pl.BlockSpec((parts, groups, 1, 16, HALF), lambda b, pick_ref: (0, 0, b, 0, 0)),
                chosen(tall, columns),
                chosen(columns, tall),
                chosen(ROWS, 128),
                pl.BlockSpec((16, HALF), lambda b, pick_ref: (0, q)),
                fixed(HALF, 2 * HALF),
                fixed(2 * HALF, HALF),
            ],
            out_specs=[back_block] * groups
            + [stepped(tall, HALF), stepped(2, ROWS, 2 * HALF), stepped(4, ROWS, HALF)],
        ),
        out_shape=[jax.ShapeDtypeStruct((parts, pairs, 16, HALF), BF16)] * groups
        + [
            jax.ShapeDtypeStruct((pairs, tall, HALF), BF16),
            jax.ShapeDtypeStruct((pairs, 2, ROWS, 2 * HALF), BF16),
            jax.ShapeDtypeStruct((pairs, 4, ROWS, HALF), BF16),
        ],
        compiler_params=SCHED,
    )(pick, arrived, forward, inverse, shift_row, params, one, two)


def filter_back_body(
    groups,
    pick_ref,
    *refs,
):
    arrived_refs = refs[:groups]
    adjoint_ref, inverse_ref, one_ref, two_ref, modes_ref, sums_ref, slopes_ref = refs[
        groups : groups + 7
    ]
    sent_ref, one_grad_ref, two_grad_ref, bias_ref = refs[groups + 7 :]
    columns = adjoint_ref.shape[-1]
    step = columns // groups
    arrived = jnp.concatenate([ref[...].reshape(step, HALF) for ref in arrived_refs], axis=0)
    grad = dot(adjoint_ref[0], arrived, 1, 0)
    grad_re = grad[:ROWS].astype(BF16)
    grad_im = grad[ROWS:].astype(BF16)
    from_re = dot(grad_re, two_ref[0], 1, 1)
    from_im = dot(grad_im, two_ref[0], 1, 1)
    du = from_re[:, :HALF]
    dv = -from_re[:, HALF:]
    dw = from_im[:, :HALF]
    dx = from_im[:, HALF:]
    plus_re = (du + dx) * slopes_ref[0, 0].astype(F32)
    minus_re = (du - dx) * slopes_ref[0, 1].astype(F32)
    plus_im = (dv + dw) * slopes_ref[0, 2].astype(F32)
    minus_im = (dv - dw) * slopes_ref[0, 3].astype(F32)
    re_a = plus_re + minus_re
    im_b = minus_re - plus_re
    im_a = plus_im - minus_im
    re_b = plus_im + minus_im
    out_re = jnp.concatenate([re_a.astype(BF16), re_b.astype(BF16)], axis=1)
    out_im = jnp.concatenate([im_a.astype(BF16), im_b.astype(BF16)], axis=1)
    modes_re = dot(out_re, one_ref[0], 1, 1)
    modes_im = dot(out_im, one_ref[0], 1, 1)
    both = jnp.concatenate([modes_re.astype(BF16), modes_im.astype(BF16)], axis=0)
    sent = dot(inverse_ref[0], both, 1, 0).astype(BF16)
    sent_ref[...] = sent.reshape(sent_ref.shape)
    one_part = dot(modes_ref[0, :ROWS], out_re, 0, 0) + dot(modes_ref[0, ROWS:], out_im, 0, 0)
    two_part = dot(sums_ref[0, 0], grad_re, 0, 0) + dot(sums_ref[0, 1], grad_im, 0, 0)
    rows = [jnp.sum(part, axis=0, keepdims=True) for part in (re_a, re_b, grad[:ROWS], grad[ROWS:])]
    bias_part = jnp.concatenate(rows + [jnp.zeros((4, HALF), F32)], axis=0)
    first = pl.program_id(0) == 0

    @pl.when(first)
    def _():
        one_grad_ref[...] = one_part
        two_grad_ref[...] = two_part
        bias_ref[...] = bias_part

    @pl.when(jnp.logical_not(first))
    def _():
        one_grad_ref[...] += one_part
        two_grad_ref[...] += two_part
        bias_ref[...] += bias_part


def filter_backward(pick, arrived, tables, one, two, modes, sums, slopes, part_of_channels):
    groups = len(arrived)
    parts, pairs = arrived[0].shape[:2]
    _, _, adjoint, inverse, _ = tables
    q = part_of_channels
    tall = 2 * ROWS
    columns = adjoint.shape[-1]

    def chosen(*shape):
        return pl.BlockSpec((1,) + shape, lambda b, pick_ref: (pick_ref[b], 0, 0))

    def fixed(*shape):
        return pl.BlockSpec((1,) + shape, lambda b, pick_ref: (q, 0, 0))

    def stepped(*shape):
        zeros = (0,) * len(shape)
        return pl.BlockSpec((1,) + shape, lambda b, pick_ref: (b,) + zeros)

    def whole(*shape):
        return pl.BlockSpec(shape, lambda b, pick_ref: (0,) * len(shape))

    arrived_block = pl.BlockSpec((parts, 1, 16, HALF), lambda b, pick_ref: (0, b, 0, 0))
    return pl.pallas_call(
        functools.partial(filter_back_body, groups),
        name="filter_backward",
        grid_spec=pltpu.PrefetchScalarGridSpec(
            num_scalar_prefetch=1,
            grid=(pairs,),
            in_specs=[arrived_block] * groups
            + [
                chosen(tall, columns),
                chosen(columns, tall),
                fixed(HALF, 2 * HALF),
                fixed(2 * HALF, HALF),
                stepped(tall, HALF),
                stepped(2, ROWS, 2 * HALF),
                stepped(4, ROWS, HALF),
            ],
            out_specs=[
                pl.BlockSpec((parts, groups, 1, 16, HALF), lambda b, pick_ref: (0, 0, b, 0, 0)),
                whole(HALF, 2 * HALF),
                whole(2 * HALF, HALF),
                whole(8, HALF),
            ],
        ),
        out_shape=[
            jax.ShapeDtypeStruct((parts, groups, pairs, 16, HALF), BF16),
            jax.ShapeDtypeStruct((HALF, 2 * HALF), F32),
            jax.ShapeDtypeStruct((2 * HALF, HALF), F32),
            jax.ShapeDtypeStruct((8, HALF), F32),
        ],
        compiler_params=SCHED,
    )(pick, *arrived, adjoint, inverse, one, two, modes, sums, slopes)


def dense_body(
    tokens_ref,
    cotangent_ref,
    low_ref,
    high_ref,
    inverse_ref,
    table_ref,
    params_ref,
    in_bias_ref,
    in_ref,
    out_ref,
    result_ref,
    mixed_grad_ref,
    low_sent_ref,
    high_sent_ref,
    second_ref,
    grad_low_ref,
    act_ref,
    grad_pre_ref,
    in_bias_grad_ref,
    rows_ref,
    mixed_ref,
    branch_ref,
    grad_second_ref,
):
    chunk = pl.program_id(0)
    count = GROUP * LON
    wide = 2 * HALF

    @pl.when(chunk == 0)
    def _():
        inputs = tokens_ref[...].astype(F32).reshape(count, wide)
        normed, _ = normalise(inputs)
        base = normed * params_ref[0:1, :] + params_ref[1:2, :] + inputs
        mixed_ref[:, :HALF] = (
            dot(inverse_ref[...], low_ref[...].reshape(count, HALF), 1, 0) + base[:, :HALF]
        )
        mixed_ref[:, HALF:] = (
            dot(inverse_ref[...], high_ref[...].reshape(count, HALF), 1, 0) + base[:, HALF:]
        )
        normed_two, _ = normalise(mixed_ref[...])
        second_ref[...] = (normed_two * params_ref[2:3, :] + params_ref[3:4, :]).astype(BF16)
        grad_low_ref[...] = (
            cotangent_ref[...].astype(F32).reshape(count, wide) * params_ref[13:14, :]
        ).astype(BF16)
        branch_ref[...] = jnp.zeros_like(branch_ref)
        grad_second_ref[...] = jnp.zeros_like(grad_second_ref)

    pre = dot(second_ref[...], in_ref[...], 1, 0) + in_bias_ref[...]
    grad_act = dot(grad_low_ref[...], out_ref[...], 1, 1)
    act, slope = gelu_pair(pre)
    act = act.astype(BF16)
    grad_pre = grad_act * slope
    in_bias_grad_ref[...] = jnp.sum(grad_pre, axis=0, keepdims=True)
    grad_pre = grad_pre.astype(BF16)
    act_ref[...] = act
    grad_pre_ref[...] = grad_pre
    branch_ref[...] += dot(act, out_ref[...], 1, 0)
    grad_second_ref[...] += dot(grad_pre, in_ref[...], 1, 1)

    @pl.when(chunk == pl.num_programs(0) - 1)
    def _():
        mixed = mixed_ref[...]
        result = (mixed + branch_ref[...] + params_ref[8:9, :]).astype(BF16)
        result_ref[...] = result.reshape(result_ref.shape)
        normed_two, inv_two = normalise(mixed)
        upstream = grad_second_ref[...]
        scaled = upstream * params_ref[2:3, :]
        first_mean = jnp.mean(scaled, axis=-1, keepdims=True)
        second_mean = jnp.mean(scaled * normed_two, axis=-1, keepdims=True)
        grad_out = cotangent_ref[...].astype(F32).reshape(count, wide) * params_ref[13:14, :]
        mixed_grad = grad_out + inv_two * (scaled - first_mean - normed_two * second_mean)
        mixed_grad_ref[...] = mixed_grad.reshape(mixed_grad_ref.shape)
        rows = [
            jnp.sum(part, axis=0, keepdims=True)
            for part in (upstream * normed_two, upstream, grad_low_ref[...].astype(F32))
        ]
        rows_ref[...] = jnp.concatenate(rows + [jnp.zeros((5, wide), F32)], axis=0)
        sent = dot(table_ref[...], mixed_grad.astype(BF16), 1, 0).astype(BF16)
        low_sent_ref[...] = sent[:, :HALF].reshape(low_sent_ref.shape)
        high_sent_ref[...] = sent[:, HALF:].reshape(high_sent_ref.shape)


def dense(tokens, cotangent, low, high, inverse, table, params, in_bias, in_work, out_work, group):
    parts, pairs = low.shape[:2]
    count = GROUP * LON
    wide = 2 * HALF
    hidden = in_work.shape[1]

    def whole(*shape):
        return pl.BlockSpec(shape, lambda f: (0,) * len(shape))

    rows_in = pl.BlockSpec((1, GROUP, LON, wide), lambda f: (0, group, 0, 0))
    sent = whole(parts, pairs, 16, HALF)
    return pl.pallas_call(
        dense_body,
        name="dense_group",
        grid=(hidden // FCHUNK,),
        in_specs=[
            rows_in,
            rows_in,
            sent,
            sent,
            whole(*inverse.shape),
            whole(*table.shape),
            whole(16, wide),
            pl.BlockSpec((1, FCHUNK), lambda f: (0, f)),
            pl.BlockSpec((wide, FCHUNK), lambda f: (0, f)),
            pl.BlockSpec((FCHUNK, wide), lambda f: (f, 0)),
        ],
        out_specs=[
            whole(GROUP, LON, wide),
            whole(GROUP, LON, wide),
            sent,
            sent,
            whole(count, wide),
            whole(count, wide),
            pl.BlockSpec((count, FCHUNK), lambda f: (0, f)),
            pl.BlockSpec((count, FCHUNK), lambda f: (0, f)),
            pl.BlockSpec((1, FCHUNK), lambda f: (0, f)),
            whole(8, wide),
        ],
        out_shape=[
            jax.ShapeDtypeStruct((GROUP, LON, wide), BF16),
            jax.ShapeDtypeStruct((GROUP, LON, wide), F32),
            jax.ShapeDtypeStruct((parts, pairs, 16, HALF), BF16),
            jax.ShapeDtypeStruct((parts, pairs, 16, HALF), BF16),
            jax.ShapeDtypeStruct((count, wide), BF16),
            jax.ShapeDtypeStruct((count, wide), BF16),
            jax.ShapeDtypeStruct((count, hidden), BF16),
            jax.ShapeDtypeStruct((count, hidden), BF16),
            jax.ShapeDtypeStruct((1, hidden), F32),
            jax.ShapeDtypeStruct((8, wide), F32),
        ],
        scratch_shapes=[pltpu.VMEM((count, wide), F32)] * 3,
        compiler_params=SCHED,
    )(tokens, cotangent, low, high, inverse, table, params, in_bias, in_work, out_work)


def gather_grad_body(groups, *refs):
    tokens_ref = refs[0]
    mixed_grad_refs = refs[1 : 1 + groups]
    low_ref, high_ref, inverse_ref, params_ref, grad_ref, rows_ref = refs[1 + groups :]
    step = pl.program_id(0)
    count = GROUP * LON
    wide = 2 * HALF
    mixed_grad = mixed_grad_refs[0][...]
    for group in range(1, groups):
        mixed_grad = jnp.where(step == group, mixed_grad_refs[group][...], mixed_grad)
    mixed_grad = mixed_grad.reshape(count, wide)
    low = dot(inverse_ref[...], low_ref[...].reshape(count, HALF), 1, 0)
    high = dot(inverse_ref[...], high_ref[...].reshape(count, HALF), 1, 0)
    upstream = mixed_grad + jnp.concatenate([low, high], axis=1)
    normed, inv_std = normalise(tokens_ref[...].astype(F32).reshape(count, wide))
    scaled = upstream * params_ref[0:1, :]
    first_mean = jnp.mean(scaled, axis=-1, keepdims=True)
    second_mean = jnp.mean(scaled * normed, axis=-1, keepdims=True)
    out = mixed_grad + inv_std * (scaled - first_mean - normed * second_mean)
    grad_ref[...] = out.reshape(grad_ref.shape)
    rows = [jnp.sum(part, axis=0, keepdims=True) for part in (upstream * normed, upstream)]
    part = jnp.concatenate(rows + [jnp.zeros((6, wide), F32)], axis=0)

    @pl.when(step == 0)
    def _():
        rows_ref[...] = part

    @pl.when(step > 0)
    def _():
        rows_ref[...] += part


def gather_grad(tokens, mixed_grads, low, high, inverse, params):
    parts, groups, pairs = low.shape[:3]
    wide = 2 * HALF

    def whole(*shape):
        return pl.BlockSpec(shape, lambda r: (0,) * len(shape))

    rows = pl.BlockSpec((1, GROUP, LON, wide), lambda r: (0, r, 0, 0))
    arrived = pl.BlockSpec((parts, 1, pairs, 16, HALF), lambda r: (0, r, 0, 0, 0))
    return pl.pallas_call(
        functools.partial(gather_grad_body, groups),
        name="longitude_and_norm_grad",
        grid=(groups,),
        in_specs=[rows]
        + [whole(GROUP, LON, wide)] * groups
        + [arrived, arrived, whole(*inverse.shape), whole(16, wide)],
        out_specs=[rows, whole(8, wide)],
        out_shape=[
            jax.ShapeDtypeStruct((1, groups * GROUP, LON, wide), F32),
            jax.ShapeDtypeStruct((8, wide), F32),
        ],
        compiler_params=SCHED,
    )(tokens, *mixed_grads, low, high, inverse, params)


def block_matrices(weight):
    size = weight.shape[1] // 2
    count = HALF // size
    grouped = weight.reshape(2, count, size, 2, size)
    eye = jnp.eye(count, dtype=weight.dtype)
    full = grouped[:, :, :, :, None, :] * eye[None, :, None, None, :, None]
    return full.reshape(2, HALF, 2, HALF)


def own_blocks(matrix, size):
    count = HALF // size
    return jnp.concatenate(
        [matrix[i * size : (i + 1) * size, i * size : (i + 1) * size] for i in range(count)], axis=0
    )


def exchange(values):
    return lax.all_to_all(values, "sp", split_axis=0, concat_axis=0, tiled=True)


def fast_shards(
    sizes,
    tokens,
    cotangent,
    storm_weight,
    filter_master,
    in_master,
    out_master,
    small_master,
    filter_m,
    filter_v,
    in_m,
    in_v,
    out_m,
    out_v,
    small_m,
    small_v,
    filter_ema,
    in_ema,
    out_ema,
    small_ema,
):
    both = ("samp", "sp")
    parts = sizes[1]
    devices = sizes[0] * sizes[1]
    groups = tokens.shape[1] // GROUP
    pairs = LON // 4 // parts
    width = tokens.shape[-1]
    block = width // NB
    small_share = small_master.shape[0]
    sp_index = lax.axis_index("sp")

    lon = lon_matrix()
    lon_table = jnp.asarray(lon, BF16)
    lon_back = jnp.asarray(lon.T, BF16)
    tables = lat_tables(parts)
    pick = jnp.where((sp_index == 0) & (jnp.arange(pairs) == 0), 0, 1).astype(jnp.int32)

    filter_rows = filter_master.shape[0]
    small_line = jnp.pad(small_master.astype(BF16), (0, 4 * block - small_share)).reshape(1, -1)
    packed = jnp.concatenate([filter_master.astype(BF16), small_line], axis=0)
    sent = spread(tokens, lon_table, parts)
    packed_all = lax.all_gather(packed, both, axis=0, tiled=True).reshape(devices, filter_rows + 1, -1)
    filter_work = packed_all[:, :filter_rows].reshape(width, 4 * block)
    small_work = packed_all[:, filter_rows, :small_share].reshape(-1)
    in_work = lax.all_gather(in_master.astype(BF16), both, axis=0, tiled=True)
    out_work = lax.all_gather(out_master.astype(BF16), both, axis=0, tiled=True)

    params = small_work.astype(F32).reshape(13, width)
    scale = storm_weight.astype(F32)[0] / 64.0
    in_bias = params[9:13].reshape(1, -1)
    params = jnp.concatenate(
        [params, jnp.full((1, width), scale, F32), jnp.zeros((2, width), F32)], axis=0
    )
    one = block_matrices(filter_work[:, : 2 * block]).reshape(2, HALF, 2 * HALF)
    two = block_matrices(filter_work[:, 2 * block :]).transpose(0, 2, 1, 3).reshape(2, 2 * HALF, HALF)

    arrived = [exchange(piece) for piece in sent]
    forward = [
        filter_forward(pick, arrived[q], tables, params, one, two, q) for q in range(2)
    ]
    returned = [[exchange(forward[q][group]) for q in range(2)] for group in range(groups)]
    dense_out = [
        dense(
            tokens,
            cotangent,
            returned[group][0],
            returned[group][1],
            lon_back,
            lon_table,
            params,
            in_bias,
            in_work,
            out_work,
            group,
        )
        for group in range(groups)
    ]
    grad_arrived = [[exchange(dense_out[group][2 + q]) for group in range(groups)] for q in range(2)]
    backward = [
        filter_backward(pick, grad_arrived[q], tables, one, two, *forward[q][groups:], q)
        for q in range(2)
    ]
    grad_returned = [exchange(backward[q][0]) for q in range(2)]
    input_grad, norm_rows = gather_grad(
        tokens, [part[1] for part in dense_out], grad_returned[0], grad_returned[1], lon_back, params
    )
    result = jnp.concatenate([part[0] for part in dense_out], axis=0)[None]

    second, grad_low, act, grad_pre = (
        jnp.concatenate([part[i] for part in dense_out], axis=0) for i in (4, 5, 6, 7)
    )
    out_local = jnp.einsum("tf,td->fd", act, grad_low, preferred_element_type=F32).astype(BF16)
    in_local = jnp.einsum("td,tf->df", second, grad_pre, preferred_element_type=F32).astype(BF16)
    in_grad = lax.psum_scatter(in_local, both, scatter_dimension=0, tiled=True).astype(F32)
    out_grad = lax.psum_scatter(out_local, both, scatter_dimension=0, tiled=True).astype(F32)

    pieces = []
    for q in range(2):
        one_grad = backward[q][1]
        two_grad = backward[q][2]
        pieces.append(
            jnp.concatenate(
                [
                    own_blocks(one_grad[:, :HALF], block),
                    own_blocks(one_grad[:, HALF:], block),
                    own_blocks(two_grad[:HALF], block),
                    own_blocks(two_grad[HALF:], block),
                ],
                axis=1,
            )
        )
    filter_local = jnp.concatenate(pieces, axis=0)
    filter_grad = lax.psum_scatter(filter_local, both, scatter_dimension=0, tiled=True)

    bias_rows = jnp.concatenate([backward[0][3], backward[1][3]], axis=1)
    dense_rows = sum(part[9] for part in dense_out)
    in_bias_grad = sum(part[8] for part in dense_out)
    small_local = jnp.concatenate(
        [
            norm_rows[0:2],
            dense_rows[0:2],
            bias_rows[0:2],
            bias_rows[2:3] + bias_rows[2:3],
            bias_rows[3:4] - bias_rows[3:4],
            dense_rows[2:3],
            in_bias_grad.reshape(4, width),
        ],
        axis=0,
    ).reshape(-1)
    small_grad = lax.psum_scatter(small_local, both, scatter_dimension=0, tiled=True)

    filter_new, filter_m_new, filter_v_new, filter_ema_new = adam_update(
        filter_master, filter_grad, filter_m, filter_v, filter_ema, 0.2
    )
    in_new, in_m_new, in_v_new, in_ema_new = adam_update(
        in_master, in_grad, in_m, in_v, in_ema, 0.1
    )
    out_new, out_m_new, out_v_new, out_ema_new = adam_update(
        out_master, out_grad, out_m, out_v, out_ema, 0.05
    )
    small_new, small_m_new, small_v_new, small_ema_new = adam_update(
        small_master, small_grad, small_m, small_v, small_ema, 0.5
    )
    return (
        result,
        input_grad,
        filter_grad,
        in_grad,
        out_grad,
        small_grad,
        filter_new,
        in_new,
        out_new,
        small_new,
        filter_m_new,
        filter_v_new,
        in_m_new,
        in_v_new,
        out_m_new,
        out_v_new,
        small_m_new,
        small_v_new,
        filter_ema_new,
        in_ema_new,
        out_ema_new,
        small_ema_new,
    )


def solution(mesh):
    sizes = (mesh.shape["samp"], mesh.shape["sp"])
    body = functools.partial(fast_shards, sizes) if fits(sizes[1]) else plain_shards
    return jax.shard_map(
        body,
        mesh=mesh,
        in_specs=(
            P("samp", "sp", None, None),
            P("samp", "sp", None, None),
            P("samp"),
            P(("samp", "sp"), None),
            P(("samp", "sp"), None),
            P(("samp", "sp"), None),
            P(("samp", "sp")),
            P(("samp", "sp"), None),
            P(("samp", "sp"), None),
            P(("samp", "sp"), None),
            P(("samp", "sp"), None),
            P(("samp", "sp"), None),
            P(("samp", "sp"), None),
            P(("samp", "sp")),
            P(("samp", "sp")),
            P(("samp", "sp"), None),
            P(("samp", "sp"), None),
            P(("samp", "sp"), None),
            P(("samp", "sp")),
        ),
        out_specs=(
            P("samp", "sp", None, None),
            P("samp", "sp", None, None),
            P(("samp", "sp"), None),
            P(("samp", "sp"), None),
            P(("samp", "sp"), None),
            P(("samp", "sp")),
            P(("samp", "sp"), None),
            P(("samp", "sp"), None),
            P(("samp", "sp"), None),
            P(("samp", "sp")),
            P(("samp", "sp"), None),
            P(("samp", "sp"), None),
            P(("samp", "sp"), None),
            P(("samp", "sp"), None),
            P(("samp", "sp"), None),
            P(("samp", "sp"), None),
            P(("samp", "sp")),
            P(("samp", "sp")),
            P(("samp", "sp"), None),
            P(("samp", "sp"), None),
            P(("samp", "sp"), None),
            P(("samp", "sp")),
        ),
        check_vma=False,
    )
```

```python
import functools
import math

import jax
import jax.numpy as jnp
import numpy as np
from jax import lax
from jax.experimental import pallas as pl
from jax.experimental.pallas import tpu as pltpu
from jax.sharding import Mesh
from jax.sharding import PartitionSpec as P

NB = 8
STEP = 10


HIGHEST = lax.Precision.HIGHEST
NORM_EPS = 1e-05
BETA_ONE = 0.9
BETA_TWO = 0.95
ADAM_EPS = 1e-08
DECAY = 0.05
EMA_KEEP = 0.75


def gelu_exact(values):
    return jax.nn.gelu(values, approximate=False)


def norm_forward(values):
    center = values - jnp.mean(values, axis=-1, keepdims=True)
    inv_std = lax.rsqrt(jnp.mean(center * center, axis=-1, keepdims=True) + NORM_EPS)
    return (center * inv_std, inv_std)


def norm_back(upstream, normed, inv_std, gain):
    scaled = upstream * gain
    first_mean = jnp.mean(scaled, axis=-1, keepdims=True)
    second_mean = jnp.mean(scaled * normed, axis=-1, keepdims=True)
    leading = tuple(range(upstream.ndim - 1))
    input_part = inv_std * (scaled - first_mean - normed * second_mean)
    return (input_part, jnp.sum(upstream * normed, axis=leading), jnp.sum(upstream, axis=leading))


def dft_table(points):
    positions = jnp.arange(points, dtype=jnp.int32)
    phases = positions[:, None] * positions[None, :] % points
    angles = phases.astype(jnp.float32) * (2.0 * math.pi / points)
    factor = 1.0 / math.sqrt(points)
    return (jnp.cos(angles) * factor, jnp.sin(angles) * factor)


def lat_table(cosine, sine_part, sign_value):
    upper_rows = jnp.stack([cosine, -sign_value * sine_part], axis=-1)
    lower_rows = jnp.stack([sign_value * sine_part, cosine], axis=-1)
    return jnp.stack([upper_rows, lower_rows], axis=1)


def split_table(table):
    upper_part = table.astype(jnp.bfloat16)
    lower_part = (table - upper_part.astype(jnp.float32)).astype(jnp.bfloat16)
    return (upper_part, lower_part)


def table_first(form, table, values):
    upper_part, lower_part = split_table(table)
    return jnp.einsum(form, upper_part, values, preferred_element_type=jnp.float32) + jnp.einsum(
        form, lower_part, values, preferred_element_type=jnp.float32
    )


def table_second(form, values, table):
    upper_part, lower_part = split_table(table)
    return jnp.einsum(form, values, upper_part, preferred_element_type=jnp.float32) + jnp.einsum(
        form, values, lower_part, preferred_element_type=jnp.float32
    )


def complex_mix(inputs, weight):
    shape_in = inputs.shape
    size_block = weight.shape[1] // 2
    grouped = inputs.reshape(shape_in[:4] + (NB, size_block))
    matrices = weight.reshape(NB, size_block, 2, size_block)
    product = jnp.einsum(
        "sgckbi,bieo->sgcekbo", grouped, matrices, preferred_element_type=jnp.float32
    )
    real_part = product[:, :, 0, 0] - product[:, :, 1, 1]
    imag_part = product[:, :, 1, 0] + product[:, :, 0, 1]
    return jnp.stack([real_part, imag_part], axis=2).reshape(shape_in)


def mix_back(upstream, inputs, weight):
    shape_in = inputs.shape
    size_block = weight.shape[1] // 2
    grouped = inputs.reshape(shape_in[:4] + (NB, size_block))
    upstream_grouped = upstream.reshape(shape_in[:4] + (NB, size_block))
    matrices = weight.reshape(NB, size_block, 2, size_block)
    toward = jnp.einsum(
        "sgekbo,bico->sgeckbi", upstream_grouped, matrices, preferred_element_type=jnp.float32
    )
    grad_real = toward[:, :, 0, 0] + toward[:, :, 1, 1]
    grad_imag = toward[:, :, 1, 0] - toward[:, :, 0, 1]
    grad_inputs = jnp.stack([grad_real, grad_imag], axis=2).reshape(shape_in)
    outer_sums = jnp.einsum(
        "sgckbi,sgekbo->cebio", grouped, upstream_grouped, preferred_element_type=jnp.float32
    )
    weight_real = outer_sums[0, 0] + outer_sums[1, 1]
    weight_imag = outer_sums[0, 1] - outer_sums[1, 0]
    weight_grad = jnp.stack([weight_real, weight_imag], axis=2).reshape(weight.shape)
    bias_grad = jnp.sum(upstream, axis=(0, 1, 3), dtype=jnp.float32)
    return (grad_inputs, weight_grad, bias_grad)


def adam_update(master, gradient, moment, second, average, step_rate):
    moment_new = BETA_ONE * moment + (1.0 - BETA_ONE) * gradient
    second_new = BETA_TWO * second + (1.0 - BETA_TWO) * gradient * gradient
    scaled_moment = moment_new / (1.0 - BETA_ONE**STEP)
    scaled_second = second_new / (1.0 - BETA_TWO**STEP)
    master_new = master - step_rate * (
        scaled_moment / (jnp.sqrt(scaled_second) + ADAM_EPS) + DECAY * master
    )
    average_new = EMA_KEEP * average + (1.0 - EMA_KEEP) * master_new
    return (master_new, moment_new, second_new, average_new)


def plain_shards(
    tokens,
    cotangent,
    storm_weight,
    filter_master,
    in_master,
    out_master,
    small_master,
    filter_m,
    filter_v,
    in_m,
    in_v,
    out_m,
    out_v,
    small_m,
    small_v,
    filter_ema,
    in_ema,
    out_ema,
    small_ema,
):
    filter_work, small_work = (
        lax.all_gather(filter_master.astype(jnp.bfloat16), ("samp", "sp"), axis=0, tiled=True),
        lax.all_gather(small_master.astype(jnp.bfloat16), ("samp", "sp"), axis=0, tiled=True),
    )
    width = filter_work.shape[0]
    size_block = width // NB
    params = small_work.astype(jnp.float32).reshape(13, width)
    inputs = tokens.astype(jnp.float32)
    normed_one, inv_one = norm_forward(inputs)
    first = normed_one * params[0] + params[1]
    lon_cos, lon_sin = dft_table(tokens.shape[2])
    lon_forward = jnp.stack([lon_cos, -lon_sin], axis=1)
    lon_inverse = jnp.stack([lon_cos, -lon_sin], axis=0)
    spectrum = jnp.einsum("shwd,wck->shckd", first, lon_forward, precision=HIGHEST).astype(
        jnp.bfloat16
    )
    arrived = lax.all_to_all(spectrum, "sp", split_axis=3, concat_axis=1, tiled=True)
    lat_cos, lat_sin = dft_table(arrived.shape[1])
    lat_forward = lat_table(lat_cos, lat_sin, -1.0)
    lat_inverse = lat_table(lat_cos, lat_sin, 1.0)
    modes = table_first("gohc,shckd->sgokd", lat_forward, arrived).astype(jnp.bfloat16)
    bias_one = params[4:6][:, None, :]
    bias_two = params[6:8][:, None, :]
    pre_one = complex_mix(modes, filter_work[:, : 2 * size_block]) + bias_one
    hidden_one = gelu_exact(pre_one).astype(jnp.bfloat16)
    pre_two = complex_mix(hidden_one, filter_work[:, 2 * size_block :]) + bias_two
    leaving = jnp.einsum("gohc,shckd->sgokd", lat_inverse, pre_two, precision=HIGHEST).astype(
        jnp.bfloat16
    )
    returned = lax.all_to_all(leaving, "sp", split_axis=1, concat_axis=3, tiled=True)
    spatial = table_second("shckd,ckw->shwd", returned, lon_inverse)
    mixed = spatial + first + inputs
    in_work, out_work = (
        lax.all_gather(in_master.astype(jnp.bfloat16), ("samp", "sp"), axis=0, tiled=True),
        lax.all_gather(out_master.astype(jnp.bfloat16), ("samp", "sp"), axis=0, tiled=True),
    )
    normed_two, inv_two = norm_forward(mixed)
    second = (normed_two * params[2] + params[3]).astype(jnp.bfloat16).reshape(-1, width)
    pre_dense = jnp.dot(second, in_work, preferred_element_type=jnp.float32) + params[9:13].reshape(
        -1
    )
    act_dense = gelu_exact(pre_dense).astype(jnp.bfloat16)
    branch = jnp.dot(act_dense, out_work, preferred_element_type=jnp.float32) + params[8]
    result = (mixed + branch.reshape(mixed.shape)).astype(jnp.bfloat16)
    filter_back = lax.all_gather(
        filter_master.astype(jnp.bfloat16), ("samp", "sp"), axis=0, tiled=True
    )
    in_back, out_back = (
        lax.all_gather(in_master.astype(jnp.bfloat16), ("samp", "sp"), axis=0, tiled=True),
        lax.all_gather(out_master.astype(jnp.bfloat16), ("samp", "sp"), axis=0, tiled=True),
    )
    sample_scale = storm_weight.astype(jnp.float32)[:, None, None, None] / 64.0
    grad_out = cotangent.astype(jnp.float32) * sample_scale
    grad_low = grad_out.astype(jnp.bfloat16).reshape(-1, width)
    out_local = jnp.einsum("tf,td->fd", act_dense, grad_low, preferred_element_type=jnp.float32)
    out_bias_grad = jnp.sum(grad_low, axis=0, dtype=jnp.float32)
    grad_act = jnp.einsum("td,fd->tf", grad_low, out_back, preferred_element_type=jnp.float32)
    dense_values, dense_pull = jax.vjp(gelu_exact, pre_dense)
    grad_pre = dense_pull(grad_act)[0].astype(jnp.bfloat16)
    in_local = jnp.einsum("td,tf->df", second, grad_pre, preferred_element_type=jnp.float32)
    in_bias_grad = jnp.sum(grad_pre, axis=0, dtype=jnp.float32)
    grad_second = jnp.einsum(
        "tf,df->td", grad_pre, in_back, preferred_element_type=jnp.float32
    ).reshape(mixed.shape)
    grad_norm_two, gain_two_grad, shift_two_grad = norm_back(
        grad_second, normed_two, inv_two, params[2]
    )
    grad_mixed = grad_out + grad_norm_two
    grad_leaving = jnp.einsum("shwd,ckw->shckd", grad_mixed, lon_inverse, precision=HIGHEST).astype(
        jnp.bfloat16
    )
    grad_arrived = lax.all_to_all(grad_leaving, "sp", split_axis=3, concat_axis=1, tiled=True)
    grad_pre_two = table_first("gohc,sgokd->shckd", lat_inverse, grad_arrived).astype(jnp.bfloat16)
    grad_hidden, weight_two_grad, bias_two_grad = mix_back(
        grad_pre_two, hidden_one, filter_back[:, 2 * size_block :]
    )
    gelu_values, gelu_pull = jax.vjp(gelu_exact, pre_one)
    grad_pre_one = gelu_pull(grad_hidden)[0].astype(jnp.bfloat16)
    grad_modes, weight_one_grad, bias_one_grad = mix_back(
        grad_pre_one, modes, filter_back[:, : 2 * size_block]
    )
    grad_spectrum = jnp.einsum(
        "gohc,sgokd->shckd", lat_forward, grad_modes, precision=HIGHEST
    ).astype(jnp.bfloat16)
    grad_sent = lax.all_to_all(grad_spectrum, "sp", split_axis=1, concat_axis=3, tiled=True)
    grad_first = grad_mixed + table_second("shckd,wck->shwd", grad_sent, lon_forward)
    grad_norm_one, gain_one_grad, shift_one_grad = norm_back(
        grad_first, normed_one, inv_one, params[0]
    )
    input_grad = grad_mixed + grad_norm_one
    norm_rows = jnp.stack([gain_one_grad, shift_one_grad, gain_two_grad, shift_two_grad])
    small_local = jnp.concatenate(
        [
            norm_rows,
            bias_one_grad,
            bias_two_grad,
            out_bias_grad[None, :],
            in_bias_grad.reshape(-1, width),
        ],
        axis=0,
    ).reshape(-1)
    filter_local = jnp.concatenate([weight_one_grad, weight_two_grad], axis=1)
    filter_grad, in_grad, out_grad, small_grad = (
        lax.psum_scatter(filter_local, ("samp", "sp"), scatter_dimension=0, tiled=True),
        lax.psum_scatter(in_local, ("samp", "sp"), scatter_dimension=0, tiled=True),
        lax.psum_scatter(out_local, ("samp", "sp"), scatter_dimension=0, tiled=True),
        lax.psum_scatter(small_local, ("samp", "sp"), scatter_dimension=0, tiled=True),
    )
    filter_new, filter_m_new, filter_v_new, filter_ema_new = adam_update(
        filter_master, filter_grad, filter_m, filter_v, filter_ema, 0.2
    )
    in_new, in_m_new, in_v_new, in_ema_new = adam_update(
        in_master, in_grad, in_m, in_v, in_ema, 0.1
    )
    out_new, out_m_new, out_v_new, out_ema_new = adam_update(
        out_master, out_grad, out_m, out_v, out_ema, 0.05
    )
    small_new, small_m_new, small_v_new, small_ema_new = adam_update(
        small_master, small_grad, small_m, small_v, small_ema, 0.5
    )
    return (
        result,
        input_grad,
        filter_grad,
        in_grad,
        out_grad,
        small_grad,
        filter_new,
        in_new,
        out_new,
        small_new,
        filter_m_new,
        filter_v_new,
        in_m_new,
        in_v_new,
        out_m_new,
        out_v_new,
        small_m_new,
        small_v_new,
        filter_ema_new,
        in_ema_new,
        out_ema_new,
        small_ema_new,
    )


F32 = jnp.float32
BF16 = jnp.bfloat16
LAT = 96
LON = 160
GROUP = 4
HALF = 384
ROWS = 208
FCHUNK = 512
VMEM_BYTES = 56 * 1024 * 1024
SCHED = pltpu.CompilerParams(vmem_limit_bytes=VMEM_BYTES)


def fits(sizes):
    parts = sizes[1]
    return sizes == (4, 8) and LAT % (parts * GROUP) == 0 and LON // 2 % (2 * parts) == 0


def cost(time_us, bytes_moved):
    return pl.CostEstimate(
        flops=int(time_us * 1.15e9), bytes_accessed=bytes_moved, transcendentals=0
    )


def dot(left, right, left_dim, right_dim):
    return lax.dot_general(
        left, right, (((left_dim,), (right_dim,)), ((), ())), preferred_element_type=F32
    )


def gelu_pair(values):
    cdf = 0.5 + 0.5 * lax.erf(values * math.sqrt(0.5))
    pdf = jnp.exp2(values * values * (-0.5 * math.log2(math.e))) * (1.0 / math.sqrt(2.0 * math.pi))
    return (values * cdf, cdf + values * pdf)


@functools.lru_cache(maxsize=None)
def lon_matrix():
    slots = LON // 2
    points = np.arange(LON)
    table = np.zeros((slots, 2, LON))
    for slot in range(slots):
        angles = 2.0 * np.pi * (slot * points % LON) / LON
        table[slot, 0] = np.cos(angles)
        table[slot, 1] = -np.sin(angles)
    table[0, 1] = np.where(points % 2 == 0, 1.0, -1.0)
    table /= np.sqrt(LON)
    full = np.zeros((slots, 2, GROUP, GROUP, LON))
    for row in range(GROUP):
        full[:, :, row, row, :] = table
    return full.reshape(slots * 2 * GROUP, GROUP * LON)


@functools.lru_cache(maxsize=None)
def lat_matrices(parts):
    per_part = LAT // parts
    groups = per_part // GROUP
    forward = np.zeros((2, 2, ROWS, LAT, 2, 2))
    share = np.zeros((2, ROWS))
    lat = np.arange(LAT)

    def put_plain(variant, start, slot):
        for mode in range(LAT):
            angles = 2.0 * np.pi * (mode * lat % LAT) / LAT
            forward[variant, 0, start + mode, :, slot, 0] = np.cos(angles)
            forward[variant, 0, start + mode, :, slot, 1] = np.sin(angles)
            forward[variant, 1, start + mode, :, slot, 0] = -np.sin(angles)
            forward[variant, 1, start + mode, :, slot, 1] = np.cos(angles)
            share[variant, start + mode] = 1.0

    half = LAT // 2 + 1
    for column in range(2):
        for mode in range(half):
            angles = 2.0 * np.pi * (mode * lat % LAT) / LAT
            row = column * half + mode
            own = mode in (0, LAT // 2)
            forward[0, 0, row, :, 0, column] = np.cos(angles)
            forward[0, 1, row, :, 0, column] = 0.0 if own else -np.sin(angles)
            share[0, row] = 0.5 if own else 1.0
    put_plain(0, 2 * half, 1)
    put_plain(1, 0, 0)
    put_plain(1, LAT, 1)
    forward /= np.sqrt(LAT)
    forward = forward.reshape(2, 2, ROWS, parts, groups, GROUP, 2, 2)
    forward = forward.transpose(0, 1, 2, 3, 4, 6, 7, 5)
    shift_row = np.zeros((2, ROWS, 128))
    shift_row[0, 0] = np.sqrt(LAT * LON)
    return (forward, share, shift_row)


def lat_tables(parts):
    forward, share, shift_row = lat_matrices(parts)
    tall = 2 * ROWS
    wide = forward[0].size // tall
    by_part = forward.reshape(2, tall, wide)
    by_group = forward.transpose(0, 1, 2, 4, 3, 5, 6, 7).reshape(2, tall, wide)
    weights = np.concatenate([share, share], axis=1)[:, :, None]
    tables = (
        by_part,
        (weights * by_group).transpose(0, 2, 1),
        weights * by_group,
        by_part.transpose(0, 2, 1),
    )
    return tuple(jnp.asarray(table, BF16) for table in tables) + (jnp.asarray(shift_row, F32),)


def normalise(values):
    center = values - jnp.mean(values, axis=-1, keepdims=True)
    inv_std = lax.rsqrt(jnp.mean(center * center, axis=-1, keepdims=True) + NORM_EPS)
    return (center * inv_std, inv_std)


def spread_body(tokens_ref, table_ref, filter_ref, small_ref, low_ref, high_ref):
    step = pl.program_id(0)
    values = tokens_ref[...].astype(F32).reshape(GROUP * LON, 2 * HALF)
    normed, _ = normalise(values)
    out = dot(table_ref[...], normed.astype(BF16), 1, 0).astype(BF16)
    pairs = high_ref.shape[1]
    parts = high_ref.shape[0]
    units = low_ref.shape[1]
    low_ref[:, pl.ds(step * pairs, pairs)] = out[:, :HALF].reshape(parts, pairs, 16, HALF)
    high_ref[...] = out[:, HALF:].reshape(parts, pairs, 16, HALF)

    @pl.when(step == 0)
    def _():
        rows = filter_ref.shape[0]
        extra = units - pl.num_programs(0) * pairs
        spare = jnp.zeros((16 * extra - rows - 1, HALF), F32)
        own = jnp.concatenate([filter_ref[...], small_ref[...], spare], axis=0).astype(BF16)
        own = own.reshape(1, extra, 16, HALF)
        low_ref[:, units - extra :] = jnp.broadcast_to(own, (parts, extra, 16, HALF))


def spread(tokens, table, filter_rows, small_row, parts):
    groups = tokens.shape[1] // GROUP
    pairs = LON // 4 // parts
    extra = filter_rows.shape[0] // 16 + 1
    low = (parts, groups * pairs + extra, 16, HALF)
    high = (parts, groups * pairs, 16, HALF)

    def whole(*shape):
        return pl.BlockSpec(shape, lambda r: (0,) * len(shape))

    return pl.pallas_call(
        spread_body,
        name="norm_and_longitude",
        grid=(groups,),
        in_specs=[
            pl.BlockSpec((1, GROUP, LON, 2 * HALF), lambda r: (0, r, 0, 0)),
            whole(*table.shape),
            whole(*filter_rows.shape),
            whole(*small_row.shape),
        ],
        out_specs=[
            whole(*low),
            pl.BlockSpec((parts, pairs, 16, HALF), lambda r: (0, r, 0, 0)),
        ],
        out_shape=[jax.ShapeDtypeStruct(low, BF16), jax.ShapeDtypeStruct(high, BF16)],
        compiler_params=SCHED,
        cost_estimate=cost(7, 2 * tokens.size),
    )(tokens, table, filter_rows, small_row)


def unit_specs(parts, groups, pairs):
    return [
        pl.BlockSpec((parts, 1, 16, HALF), lambda b, pick_ref, r=r: (0, r * pairs + b, 0, 0))
        for r in range(groups)
    ]


def stacked(refs):
    return jnp.concatenate([ref[...] for ref in refs], axis=1).reshape(-1, HALF)


def filter_body(
    pieces,
    pick_ref,
    *refs,
):
    arrived_refs = refs[: sum(pieces)]
    forward_ref, inverse_ref, shift_row_ref, params_ref, one_ref, two_ref, *outs = refs[
        sum(pieces) :
    ]
    back_refs = outs[:-3]
    modes_ref, sums_ref, slopes_ref = outs[-3:]
    columns = forward_ref.shape[-1]
    raw = dot(forward_ref[0], stacked(arrived_refs), 1, 0)
    gain = params_ref[0:1, :]
    shift = params_ref[1:2, :]
    modes_re = (raw[:ROWS] * gain + shift_row_ref[0, :, 0:1] * shift).astype(BF16)
    modes_im = (raw[ROWS:] * gain).astype(BF16)
    modes_ref[0, :ROWS] = modes_re
    modes_ref[0, ROWS:] = modes_im
    from_re = dot(modes_re, one_ref[0], 1, 0)
    from_im = dot(modes_im, one_ref[0], 1, 0)
    bias_re = params_ref[4:5, :]
    bias_im = params_ref[5:6, :]
    re_a = from_re[:, :HALF] + bias_re
    re_b = from_re[:, HALF:] + bias_im
    im_a = from_im[:, :HALF]
    im_b = from_im[:, HALF:]
    plus_re, slope = gelu_pair(re_a - im_b)
    slopes_ref[0, 0] = slope.astype(BF16)
    minus_re, slope = gelu_pair(re_a + im_b)
    slopes_ref[0, 1] = slope.astype(BF16)
    sums_ref[0, 0, :, :HALF] = (plus_re + minus_re).astype(BF16)
    sums_ref[0, 1, :, HALF:] = (plus_re - minus_re).astype(BF16)
    plus_im, slope = gelu_pair(re_b + im_a)
    slopes_ref[0, 2] = slope.astype(BF16)
    minus_im, slope = gelu_pair(re_b - im_a)
    slopes_ref[0, 3] = slope.astype(BF16)
    sums_ref[0, 0, :, HALF:] = (-plus_im - minus_im).astype(BF16)
    sums_ref[0, 1, :, :HALF] = (plus_im - minus_im).astype(BF16)
    two_bias_re = params_ref[6:7, :]
    two_bias_im = params_ref[7:8, :]
    two_re = dot(sums_ref[0, 0], two_ref[0], 1, 0) + (two_bias_re + two_bias_re)
    two_im = dot(sums_ref[0, 1], two_ref[0], 1, 0) + (two_bias_im - two_bias_im)
    both = jnp.concatenate([two_re.astype(BF16), two_im.astype(BF16)], axis=0)
    back = dot(inverse_ref[0], both, 1, 0).astype(BF16)
    step = columns // sum(pieces)
    group = 0
    for ref, count in zip(back_refs, pieces):
        for place in range(count):
            rows = back[group * step : (group + 1) * step]
            ref[:, place] = rows.reshape(-1, 1, 16, HALF)
            group += 1


def filter_forward(pick, arrived, tables, params, one, two, part_of_channels, pieces):
    parts = arrived.shape[0]
    groups = sum(pieces)
    pairs = LON // 4 // parts
    forward, inverse, _, _, shift_row = tables
    q = part_of_channels
    tall = 2 * ROWS

    def chosen(*shape):
        return pl.BlockSpec((1,) + shape, lambda b, pick_ref: (pick_ref[b], 0, 0))

    def fixed(*shape):
        return pl.BlockSpec((1,) + shape, lambda b, pick_ref: (q, 0, 0))

    def stepped(*shape):
        zeros = (0,) * len(shape)
        return pl.BlockSpec((1,) + shape, lambda b, pick_ref: (b,) + zeros)

    back_blocks = [
        pl.BlockSpec((parts, count, 1, 16, HALF), lambda b, pick_ref: (0, 0, b, 0, 0))
        for count in pieces
    ]
    back_shapes = [jax.ShapeDtypeStruct((parts, count, pairs, 16, HALF), BF16) for count in pieces]
    columns = forward.shape[-1]
    return pl.pallas_call(
        functools.partial(filter_body, pieces),
        name="filter_forward",
        grid_spec=pltpu.PrefetchScalarGridSpec(
            num_scalar_prefetch=1,
            grid=(pairs,),
            in_specs=unit_specs(parts, groups, pairs)
            + [
                chosen(tall, columns),
                chosen(columns, tall),
                chosen(ROWS, 128),
                pl.BlockSpec((16, HALF), lambda b, pick_ref: (0, q)),
                fixed(HALF, 2 * HALF),
                fixed(2 * HALF, HALF),
            ],
            out_specs=back_blocks
            + [stepped(tall, HALF), stepped(2, ROWS, 2 * HALF), stepped(4, ROWS, HALF)],
        ),
        out_shape=back_shapes
        + [
            jax.ShapeDtypeStruct((pairs, tall, HALF), BF16),
            jax.ShapeDtypeStruct((pairs, 2, ROWS, 2 * HALF), BF16),
            jax.ShapeDtypeStruct((pairs, 4, ROWS, HALF), BF16),
        ],
        compiler_params=SCHED,
        cost_estimate=cost(14, 12 * 1024 * 1024),
    )(pick, *[arrived] * groups, forward, inverse, shift_row, params, one, two)


def filter_back_body(
    groups,
    pick_ref,
    *refs,
):
    arrived_refs = refs[:groups]
    adjoint_ref, inverse_ref, shift_row_ref, one_ref, two_ref = refs[groups : groups + 5]
    normed_refs = refs[groups + 5 : 2 * groups + 5]
    modes_ref, sums_ref, slopes_ref = refs[2 * groups + 5 : 2 * groups + 8]
    sent_ref, one_grad_ref, two_grad_ref, bias_ref = refs[2 * groups + 8 :]
    columns = adjoint_ref.shape[-1]
    step = columns // groups
    arrived = jnp.concatenate([ref[...].reshape(step, HALF) for ref in arrived_refs], axis=0)
    grad = dot(adjoint_ref[0], arrived, 1, 0)
    grad_re = grad[:ROWS].astype(BF16)
    grad_im = grad[ROWS:].astype(BF16)
    from_re = dot(grad_re, two_ref[0], 1, 1)
    from_im = dot(grad_im, two_ref[0], 1, 1)
    du = from_re[:, :HALF]
    dv = -from_re[:, HALF:]
    dw = from_im[:, :HALF]
    dx = from_im[:, HALF:]
    plus_re = (du + dx) * slopes_ref[0, 0].astype(F32)
    minus_re = (du - dx) * slopes_ref[0, 1].astype(F32)
    plus_im = (dv + dw) * slopes_ref[0, 2].astype(F32)
    minus_im = (dv - dw) * slopes_ref[0, 3].astype(F32)
    re_a = plus_re + minus_re
    im_b = minus_re - plus_re
    im_a = plus_im - minus_im
    re_b = plus_im + minus_im
    out_re = jnp.concatenate([re_a.astype(BF16), re_b.astype(BF16)], axis=1)
    out_im = jnp.concatenate([im_a.astype(BF16), im_b.astype(BF16)], axis=1)
    modes_re = dot(out_re, one_ref[0], 1, 1)
    modes_im = dot(out_im, one_ref[0], 1, 1)
    both = jnp.concatenate([modes_re.astype(BF16), modes_im.astype(BF16)], axis=0)
    sent = dot(inverse_ref[0], both, 1, 0).astype(BF16)
    sent_ref[...] = sent.reshape(sent_ref.shape)
    one_part = dot(modes_ref[0, :ROWS], out_re, 0, 0) + dot(modes_ref[0, ROWS:], out_im, 0, 0)
    two_part = dot(sums_ref[0, 0], grad_re, 0, 0) + dot(sums_ref[0, 1], grad_im, 0, 0)
    gain_part = sent.astype(F32) * stacked(normed_refs).astype(F32)
    shift_part = modes_re * shift_row_ref[0, :, 0:1]
    rows = [
        jnp.sum(part, axis=0, keepdims=True)
        for part in (re_a, re_b, grad[:ROWS], grad[ROWS:], gain_part, shift_part)
    ]
    bias_part = jnp.concatenate(rows + [jnp.zeros((2, HALF), F32)], axis=0)
    first = pl.program_id(0) == 0

    @pl.when(first)
    def _():
        one_grad_ref[...] = one_part
        two_grad_ref[...] = two_part
        bias_ref[...] = bias_part

    @pl.when(jnp.logical_not(first))
    def _():
        one_grad_ref[...] += one_part
        two_grad_ref[...] += two_part
        bias_ref[...] += bias_part


def filter_backward(pick, arrived, tables, one, two, normed, modes, sums, slopes, part_of_channels):
    groups = len(arrived)
    parts, pairs = arrived[0].shape[:2]
    _, _, adjoint, inverse, shift_row = tables
    q = part_of_channels
    tall = 2 * ROWS
    columns = adjoint.shape[-1]

    def chosen(*shape):
        return pl.BlockSpec((1,) + shape, lambda b, pick_ref: (pick_ref[b], 0, 0))

    def fixed(*shape):
        return pl.BlockSpec((1,) + shape, lambda b, pick_ref: (q, 0, 0))

    def stepped(*shape):
        zeros = (0,) * len(shape)
        return pl.BlockSpec((1,) + shape, lambda b, pick_ref: (b,) + zeros)

    def whole(*shape):
        return pl.BlockSpec(shape, lambda b, pick_ref: (0,) * len(shape))

    arrived_block = pl.BlockSpec((parts, 1, 16, HALF), lambda b, pick_ref: (0, b, 0, q))
    return pl.pallas_call(
        functools.partial(filter_back_body, groups),
        name="filter_backward",
        grid_spec=pltpu.PrefetchScalarGridSpec(
            num_scalar_prefetch=1,
            grid=(pairs,),
            in_specs=[arrived_block] * groups
            + [
                chosen(tall, columns),
                chosen(columns, tall),
                chosen(ROWS, 128),
                fixed(HALF, 2 * HALF),
                fixed(2 * HALF, HALF),
            ]
            + unit_specs(parts, groups, pairs)
            + [
                stepped(tall, HALF),
                stepped(2, ROWS, 2 * HALF),
                stepped(4, ROWS, HALF),
            ],
            out_specs=[
                pl.BlockSpec((parts, groups, 1, 16, HALF), lambda b, pick_ref: (0, 0, b, 0, 0)),
                whole(HALF, 2 * HALF),
                whole(2 * HALF, HALF),
                whole(8, HALF),
            ],
        ),
        out_shape=[
            jax.ShapeDtypeStruct((parts, groups, pairs, 16, HALF), BF16),
            jax.ShapeDtypeStruct((HALF, 2 * HALF), F32),
            jax.ShapeDtypeStruct((2 * HALF, HALF), F32),
            jax.ShapeDtypeStruct((8, HALF), F32),
        ],
        compiler_params=SCHED,
        cost_estimate=cost(18, 12 * 1024 * 1024),
    )(pick, *arrived, adjoint, inverse, shift_row, one, two, *[normed] * groups, modes, sums, slopes)


def dense_body(
    tokens_ref,
    cotangent_ref,
    low_ref,
    high_ref,
    inverse_ref,
    table_ref,
    params_ref,
    in_bias_ref,
    in_ref,
    out_ref,
    *refs,
):
    (
        result_ref,
        mixed_grad_ref,
        second_ref,
        grad_low_ref,
        act_ref,
        grad_pre_ref,
        sent_ref,
        in_bias_grad_ref,
        rows_ref,
        mixed_ref,
        branch_ref,
        grad_second_ref,
    ) = refs[-12:]
    chunk = pl.program_id(0)
    count = GROUP * LON
    wide = 2 * HALF

    @pl.when(chunk == 0)
    def _():
        inputs = tokens_ref[...].astype(F32).reshape(count, wide)
        normed, _ = normalise(inputs)
        base = normed * params_ref[0:1, :] + params_ref[1:2, :] + inputs
        mixed_ref[:, :HALF] = (
            dot(inverse_ref[...], low_ref[...].reshape(count, HALF), 1, 0) + base[:, :HALF]
        )
        mixed_ref[:, HALF:] = (
            dot(inverse_ref[...], high_ref[...].reshape(count, HALF), 1, 0) + base[:, HALF:]
        )
        normed_two, _ = normalise(mixed_ref[...])
        second_ref[...] = (normed_two * params_ref[2:3, :] + params_ref[3:4, :]).astype(BF16)
        grad_low_ref[...] = (
            cotangent_ref[...].astype(F32).reshape(count, wide) * params_ref[13:14, :]
        ).astype(BF16)
        branch_ref[...] = jnp.zeros_like(branch_ref)
        grad_second_ref[...] = jnp.zeros_like(grad_second_ref)

    pre = dot(second_ref[...], in_ref[...], 1, 0) + in_bias_ref[...]
    grad_act = dot(grad_low_ref[...], out_ref[...], 1, 1)
    act, slope = gelu_pair(pre)
    act = act.astype(BF16)
    grad_pre = grad_act * slope
    in_bias_grad_ref[...] = jnp.sum(grad_pre, axis=0, keepdims=True)
    grad_pre = grad_pre.astype(BF16)
    act_ref[...] = act
    grad_pre_ref[...] = grad_pre
    branch_ref[...] += dot(act, out_ref[...], 1, 0)
    grad_second_ref[...] += dot(grad_pre, in_ref[...], 1, 1)

    @pl.when(chunk == pl.num_programs(0) - 1)
    def _():
        mixed = mixed_ref[...]
        result = (mixed + branch_ref[...] + params_ref[8:9, :]).astype(BF16)
        result_ref[...] = result.reshape(result_ref.shape)
        normed_two, inv_two = normalise(mixed)
        upstream = grad_second_ref[...]
        scaled = upstream * params_ref[2:3, :]
        first_mean = jnp.mean(scaled, axis=-1, keepdims=True)
        second_mean = jnp.mean(scaled * normed_two, axis=-1, keepdims=True)
        grad_out = cotangent_ref[...].astype(F32).reshape(count, wide) * params_ref[13:14, :]
        mixed_grad = grad_out + inv_two * (scaled - first_mean - normed_two * second_mean)
        mixed_grad_ref[...] = mixed_grad.reshape(mixed_grad_ref.shape)
        rows = [
            jnp.sum(part, axis=0, keepdims=True)
            for part in (upstream * normed_two, upstream, grad_low_ref[...].astype(F32))
        ]
        normed_one, _ = normalise(tokens_ref[...].astype(F32).reshape(count, wide))
        rows += [
            jnp.sum(part, axis=0, keepdims=True) for part in (mixed_grad * normed_one, mixed_grad)
        ]
        rows_ref[...] = jnp.concatenate(rows + [jnp.zeros((3, wide), F32)], axis=0)
        sent = dot(table_ref[...], mixed_grad.astype(BF16), 1, 0).astype(BF16)
        sent_ref[...] = sent.reshape(sent_ref.shape)


def dense(
    kept, tokens, cotangent, low, high, places, inverse, table, params, in_bias, in_work, out_work, group
):
    parts, _, pairs = high.shape[:3]
    groups = tokens.shape[1] // GROUP
    count = GROUP * LON
    wide = 2 * HALF
    hidden = in_work.shape[1]

    def whole(*shape):
        return pl.BlockSpec(shape, lambda f: (0,) * len(shape))

    rows = pl.BlockSpec((1, GROUP, LON, wide), lambda f: (0, group, 0, 0))
    low_spec, high_spec = (
        pl.BlockSpec((parts, 1, pairs, 16, HALF), lambda f, place=place: (0, place, 0, 0, 0))
        for place in places
    )
    token_rows = pl.BlockSpec((count, wide), lambda f: (group, 0))
    hidden_rows = pl.BlockSpec((count, FCHUNK), lambda f: (group, f))
    return pl.pallas_call(
        dense_body,
        name="dense_group",
        grid=(hidden // FCHUNK,),
        in_specs=[
            rows,
            rows,
            low_spec,
            high_spec,
            whole(*inverse.shape),
            whole(*table.shape),
            whole(16, wide),
            pl.BlockSpec((1, FCHUNK), lambda f: (0, f)),
            pl.BlockSpec((wide, FCHUNK), lambda f: (0, f)),
            pl.BlockSpec((FCHUNK, wide), lambda f: (f, 0)),
        ]
        + [pl.BlockSpec(memory_space=pl.ANY)] * len(kept),
        out_specs=[
            rows,
            rows,
            token_rows,
            token_rows,
            hidden_rows,
            hidden_rows,
            whole(parts, pairs, 16, wide),
            pl.BlockSpec((1, FCHUNK), lambda f: (0, f)),
            whole(8, wide),
        ],
        out_shape=[
            jax.ShapeDtypeStruct(tokens.shape, BF16),
            jax.ShapeDtypeStruct(tokens.shape, F32),
            jax.ShapeDtypeStruct((groups * count, wide), BF16),
            jax.ShapeDtypeStruct((groups * count, wide), BF16),
            jax.ShapeDtypeStruct((groups * count, hidden), BF16),
            jax.ShapeDtypeStruct((groups * count, hidden), BF16),
            jax.ShapeDtypeStruct((parts, pairs, 16, wide), BF16),
            jax.ShapeDtypeStruct((1, hidden), F32),
            jax.ShapeDtypeStruct((8, wide), F32),
        ],
        scratch_shapes=[pltpu.VMEM((count, wide), F32)] * 3,
        input_output_aliases={10 + i: i for i in range(len(kept))},
        compiler_params=SCHED,
        cost_estimate=cost(25, 30 * 1024 * 1024),
    )(tokens, cotangent, low, high, inverse, table, params, in_bias, in_work, out_work, *kept)


def gather_grad_body(
    tokens_ref, mixed_grad_ref, low_ref, high_ref, inverse_ref, params_ref, grad_ref
):
    count = GROUP * LON
    wide = 2 * HALF
    mixed_grad = mixed_grad_ref[...].reshape(count, wide)
    low = dot(inverse_ref[...], low_ref[...].reshape(count, HALF), 1, 0)
    high = dot(inverse_ref[...], high_ref[...].reshape(count, HALF), 1, 0)
    upstream = mixed_grad + jnp.concatenate([low, high], axis=1)
    normed, inv_std = normalise(tokens_ref[...].astype(F32).reshape(count, wide))
    scaled = upstream * params_ref[0:1, :]
    first_mean = jnp.mean(scaled, axis=-1, keepdims=True)
    second_mean = jnp.mean(scaled * normed, axis=-1, keepdims=True)
    out = mixed_grad + inv_std * (scaled - first_mean - normed * second_mean)
    grad_ref[...] = out.reshape(grad_ref.shape)


def gather_grad(tokens, mixed_grad, low, high, inverse, params):
    parts, groups, pairs = low.shape[:3]
    wide = 2 * HALF

    def whole(*shape):
        return pl.BlockSpec(shape, lambda r: (0,) * len(shape))

    rows = pl.BlockSpec((1, GROUP, LON, wide), lambda r: (0, r, 0, 0))
    arrived = pl.BlockSpec((parts, 1, pairs, 16, HALF), lambda r: (0, r, 0, 0, 0))
    return pl.pallas_call(
        gather_grad_body,
        name="longitude_and_norm_grad",
        grid=(groups,),
        in_specs=[rows, rows, arrived, arrived, whole(*inverse.shape), whole(16, wide)],
        out_specs=rows,
        out_shape=jax.ShapeDtypeStruct((1, groups * GROUP, LON, wide), F32),
        compiler_params=SCHED,
        cost_estimate=cost(12, 16 * 1024 * 1024),
    )(tokens, mixed_grad, low, high, inverse, params)


def block_matrices(weight):
    size = weight.shape[1] // 4
    places = np.arange(HALF)
    pick = (np.arange(4 * size)[:, None, None] == np.arange(4)[:, None] * size + places % size)
    own = places[:, None] // size == places[None, :] // size
    halves = weight.reshape(2, HALF, 4 * size)

    def spread_columns(form, first):
        full = jnp.einsum(
            form, halves, jnp.asarray(pick[:, first : first + 2], BF16), preferred_element_type=F32
        )
        return full

    one = spread_columns("qrc,cpn->qrpn", 0) * own[:, None, :]
    two = spread_columns("qrc,cpn->qprn", 2) * own
    return (
        one.astype(BF16).reshape(2, HALF, 2 * HALF),
        two.astype(BF16).reshape(2, 2 * HALF, HALF),
    )


def own_blocks(matrix, size):
    count = HALF // size
    return jnp.concatenate(
        [matrix[i * size : (i + 1) * size, i * size : (i + 1) * size] for i in range(count)], axis=0
    )


def in_turn(values, last):
    return lax.optimization_barrier((values, last))[0]


def exchange(values, last=None):
    if last is not None:
        values = in_turn(values, last)
    return lax.all_to_all(values, "sp", split_axis=0, concat_axis=0, tiled=True)


AXES = ("y", "core", "sp")
BITS = (("y", 1), ("core", 1), ("sp", 4), ("sp", 2), ("sp", 1))
SIZES = {"y": 2, "core": 2, "sp": 8}


def swap(values, axis, bit):
    return lax.ppermute(values, axis, [(i, i ^ bit) for i in range(SIZES[axis])])


def mine(axis, bit):
    return (lax.axis_index(axis) // bit) % 2


def gather_bit(values, axis, bit):
    other = swap(values, axis, bit)
    low = mine(axis, bit) == 0
    return jnp.stack([jnp.where(low, values, other), jnp.where(low, other, values)])


def scatter_bits(values, order, late, last):
    held = list(BITS)
    values = values.reshape((2,) * len(held) + values.shape[1:])
    for step, (axis, bit) in enumerate(order):
        if step == late:
            values = in_turn(values, last)
        place = held.index((axis, bit))
        keep = lax.dynamic_index_in_dim(values, mine(axis, bit), place, keepdims=False)
        give = lax.dynamic_index_in_dim(values, 1 - mine(axis, bit), place, keepdims=False)
        values = keep + swap(give, axis, bit)
        held.pop(place)
    return values


SMALL = pl.CostEstimate(flops=1 << 20, bytes_accessed=1 << 20, transcendentals=0)
IN_ORDER = (("core", 1), ("y", 1), ("sp", 1), ("sp", 2), ("sp", 4))
OUT_ORDER = (("core", 1), ("sp", 1), ("y", 1), ("sp", 2), ("sp", 4))


def device_rows(order):
    lists = []
    for core in range(2):
        indices = []
        for count in range(16):
            samp, sp = core, 0
            for place, (axis, bit) in enumerate(order[1:]):
                if count >> (3 - place) & 1:
                    samp, sp = (samp + 2 * bit, sp) if axis == "y" else (samp, sp + bit)
            indices.append(samp * 8 + sp)
        lists.append(indices)
    return lists


def in_weight_grad_body(pick_ref, second_ref, grad_pre_ref, keep_ref, give_ref):
    out = dot(second_ref[...], grad_pre_ref[...], 0, 0)
    rows = out.shape[0] // 32
    halves = [
        jnp.concatenate([out[i * rows : (i + 1) * rows] for i in indices], axis=0).astype(BF16)
        for indices in device_rows(IN_ORDER)
    ]

    @pl.when(pick_ref[0] == 0)
    def _():
        keep_ref[...] = halves[0]
        give_ref[...] = halves[1]

    @pl.when(pick_ref[0] == 1)
    def _():
        keep_ref[...] = halves[1]
        give_ref[...] = halves[0]


def in_weight_grad(core, second, grad_pre):
    tokens, wide = second.shape
    hidden = grad_pre.shape[1]
    step = 512
    half = pl.BlockSpec((wide // 2, step), lambda i, pick_ref: (0, i))
    return pl.pallas_call(
        in_weight_grad_body,
        name="in_weight_grad",
        grid_spec=pltpu.PrefetchScalarGridSpec(
            num_scalar_prefetch=1,
            grid=(hidden // step,),
            in_specs=[
                pl.BlockSpec((tokens, wide), lambda i, pick_ref: (0, 0)),
                pl.BlockSpec((tokens, step), lambda i, pick_ref: (0, i)),
            ],
            out_specs=[half, half],
        ),
        out_shape=[jax.ShapeDtypeStruct((wide // 2, hidden), BF16)] * 2,
        compiler_params=SCHED,
        cost_estimate=SMALL,
    )(core, second, grad_pre)


def out_weight_grad_body(pick_ref, act_ref, grad_low_ref, keep_ref, give_ref):
    out = dot(act_ref[...], grad_low_ref[...], 0, 0)
    rows = out.shape[0] // 8
    out = out.astype(BF16)
    pieces = [
        jnp.concatenate(
            [
                out[(z1 * 4 + z0 * 2 + x) * rows : (z1 * 4 + z0 * 2 + x + 1) * rows]
                for z0 in range(2)
                for z1 in range(2)
            ],
            axis=0,
        )
        for x in range(2)
    ]

    @pl.when(pl.program_id(0) == 0)
    def _():
        for x in range(2):
            keep_ref[x, 0] = pieces[x]

    @pl.when(pl.program_id(0) == 1)
    def _():
        for x in range(2):
            give_ref[x, 0] = pieces[x]


def out_weight_grad(core, act, grad_low):
    tokens, hidden = act.shape
    wide = grad_low.shape[1]
    part = hidden // 4
    shape = (2, 2, part // 2, wide)

    def columns(give, y, pick_ref):
        return (0, y * 2 + (pick_ref[0] + give) % 2)

    keep, give = pl.pallas_call(
        out_weight_grad_body,
        name="out_weight_grad",
        grid_spec=pltpu.PrefetchScalarGridSpec(
            num_scalar_prefetch=1,
            grid=(2, 2),
            in_specs=[
                pl.BlockSpec((tokens, part), columns),
                pl.BlockSpec((tokens, wide), lambda give, y, pick_ref: (0, 0)),
            ],
            out_specs=[
                pl.BlockSpec(
                    (2, 1) + shape[2:], lambda give, y, pick_ref: (0, jnp.maximum(y, give), 0, 0)
                ),
                pl.BlockSpec((2, 1) + shape[2:], lambda give, y, pick_ref: (0, y * give, 0, 0)),
            ],
        ),
        out_shape=[jax.ShapeDtypeStruct(shape, BF16)] * 2,
        compiler_params=SCHED,
        cost_estimate=SMALL,
    )(core, act, grad_low)
    return keep.reshape(-1, wide), give.reshape(-1, wide)


def add_split_body(pick_ref, keep_one, got_one, keep_two, got_two, keep_ref, give_ref):
    keep_ref[...] = (keep_one[...].astype(F32) + got_one[...].astype(F32)).astype(BF16)
    give_ref[...] = (keep_two[...].astype(F32) + got_two[...].astype(F32)).astype(BF16)


def add_split(pick, keep, got):
    rows, columns = keep.shape
    steps = 2 if rows % 64 == 0 else 1
    block = (rows // 2 // steps, columns)
    stays = pl.BlockSpec(block, lambda i, pick_ref: (pick_ref[0] * steps + i, 0))
    goes = pl.BlockSpec(block, lambda i, pick_ref: ((1 - pick_ref[0]) * steps + i, 0))
    out = pl.BlockSpec(block, lambda i, pick_ref: (i, 0))
    return pl.pallas_call(
        add_split_body,
        name="add_split",
        grid_spec=pltpu.PrefetchScalarGridSpec(
            num_scalar_prefetch=1,
            grid=(steps,),
            in_specs=[stays, stays, goes, goes],
            out_specs=[out, out],
        ),
        out_shape=[jax.ShapeDtypeStruct((rows // 2, columns), BF16)] * 2,
        compiler_params=SCHED,
        cost_estimate=SMALL,
    )(pick, keep, got, keep, got)


def picks(order):
    return [mine(axis, bit).astype(jnp.int32).reshape(1) for axis, bit in order]


def scatter_steps(keep, give, order, chosen, first, last):
    for place in range(first, last):
        keep, give = add_split(chosen[place + 1], keep, swap(give, *order[place]))
    return keep, give


def scatter_last(keep, give, order):
    return keep.astype(F32) + swap(give, *order[-1]).astype(F32)


def fast_shards(
    sizes,
    tokens,
    cotangent,
    storm_weight,
    filter_master,
    in_master,
    out_master,
    small_master,
    filter_m,
    filter_v,
    in_m,
    in_v,
    out_m,
    out_v,
    small_m,
    small_v,
    filter_ema,
    in_ema,
    out_ema,
    small_ema,
):
    parts = sizes[1]
    devices = sizes[0] * sizes[1]
    groups = tokens.shape[1] // GROUP
    pairs = LON // 4 // parts
    width = tokens.shape[-1]
    block = width // NB
    small_share = small_master.shape[0]
    sp_index = lax.axis_index("sp")

    lon = lon_matrix()
    lon_table = jnp.asarray(lon, BF16)
    lon_back = jnp.asarray(lon.T, BF16)
    tables = lat_tables(parts)
    pick = jnp.where((sp_index == 0) & (jnp.arange(pairs) == 0), 0, 1).astype(jnp.int32)

    filter_rows = filter_master.shape[0]
    small_row = jnp.pad(small_master, (0, 4 * block - small_share)).reshape(1, -1)
    sent = spread(tokens, lon_table, filter_master, small_row, parts)
    arrived_low = exchange(sent[0])
    arrived_high = exchange(sent[1], arrived_low)

    units = groups * pairs
    near = arrived_low[:, units:].reshape(parts, -1, 4 * block)
    packed_all = gather_bit(gather_bit(near, "core", 1), "y", 1)
    packed_all = packed_all.reshape((devices,) + near.shape[1:])
    filter_work = packed_all[:, :filter_rows].reshape(width, 4 * block)
    small_work = packed_all[:, filter_rows, :small_share].reshape(-1)

    in_rows, hidden = in_master.shape
    chunks = hidden // width
    in_line, out_line = in_turn((in_master, out_master), sent[0])
    in_block = in_line.astype(BF16).reshape(in_rows, chunks, width).transpose(1, 0, 2)
    dense_block = jnp.concatenate(
        [in_block.reshape(in_rows * chunks, width), out_line.astype(BF16)], axis=0
    )
    dense_all = lax.all_gather(dense_block, AXES, axis=0, tiled=False)
    in_work = dense_all[:, : in_rows * chunks].reshape(devices, chunks, in_rows, width)
    in_work = in_work.transpose(0, 2, 1, 3).reshape(width, hidden)
    out_work = dense_all[:, in_rows * chunks :].reshape(hidden, width)

    params = small_work.astype(F32).reshape(13, width)
    scale = storm_weight.astype(F32)[0] / 64.0
    in_bias = params[9:13].reshape(1, -1)
    params = jnp.concatenate(
        [params, jnp.full((1, width), scale, F32), jnp.zeros((2, width), F32)], axis=0
    )
    one, two = block_matrices(filter_work)

    forward_low = filter_forward(pick, arrived_low, tables, params, one, two, 0, (groups,))
    returned_low = exchange(forward_low[0], arrived_high)
    high_pieces = (1, groups - 1) if groups > 1 else (1,)
    forward_high = filter_forward(pick, arrived_high, tables, params, one, two, 1, high_pieces)
    last = (returned_low, in_work, out_work)
    returned_high = []
    for piece in range(len(high_pieces)):
        last = exchange(forward_high[piece], last)
        returned_high.append(last)
    kept = []
    grad_arrived = []
    dense_rows = 0.0
    in_bias_grad = 0.0
    for group in range(groups):
        piece = min(group, 1)
        *kept, sent_piece, bias_piece, rows_piece = dense(
            kept,
            tokens,
            cotangent,
            returned_low,
            returned_high[piece],
            (group, group - piece),
            lon_back,
            lon_table,
            params,
            in_bias,
            in_work,
            out_work,
            group,
        )
        in_bias_grad = in_bias_grad + bias_piece
        dense_rows = dense_rows + rows_piece
        before_last = last
        last = exchange(sent_piece, last)
        grad_arrived.append(last)
    result, mixed_grad, second, grad_low, act, grad_pre = kept
    act, grad_pre = in_turn((act, grad_pre), before_last)
    in_picks, out_picks = picks(IN_ORDER), picks(OUT_ORDER)
    out_part, in_part = in_turn(
        (
            out_weight_grad(out_picks[0], act, grad_low),
            in_weight_grad(in_picks[0], second, grad_pre),
        ),
        last,
    )
    out_part = scatter_steps(*out_part, OUT_ORDER, out_picks, 0, 1)
    in_part = scatter_steps(*in_part, IN_ORDER, in_picks, 0, 1)

    backward = []
    grad_returned = []
    for q, (normed, forward) in enumerate(
        ((arrived_low, forward_low), (arrived_high, forward_high))
    ):
        if q == 1:
            grad_arrived = in_turn(grad_arrived, (in_part, out_part))
        backward.append(
            filter_backward(pick, grad_arrived, tables, one, two, normed, *forward[-3:], q)
        )
        if q == 1:
            out_part = scatter_steps(*out_part, OUT_ORDER, out_picks, 1, 2)
            in_part = scatter_steps(*in_part, IN_ORDER, in_picks, 1, 2)
            last = (last, out_part, in_part)
        last = exchange(backward[q][0], last)
        grad_returned.append(last)

    out_part = scatter_steps(*out_part, OUT_ORDER, out_picks, 2, 4)
    in_part = scatter_steps(*in_part, IN_ORDER, in_picks, 2, 4)
    out_part, in_part = in_turn((out_part, in_part), last)
    out_grad = scatter_last(*out_part, OUT_ORDER)
    in_grad = scatter_last(*in_part, IN_ORDER)

    pieces = []
    for q in range(2):
        one_grad, two_grad = in_turn((backward[q][1], backward[q][2]), grad_returned[0])
        pieces.append(
            jnp.concatenate(
                [
                    own_blocks(one_grad[:, :HALF], block),
                    own_blocks(one_grad[:, HALF:], block),
                    own_blocks(two_grad[:HALF], block),
                    own_blocks(two_grad[HALF:], block),
                ],
                axis=1,
            )
        )
    filter_local = jnp.concatenate(pieces, axis=0).reshape(devices, filter_rows, 4 * block)
    bias_rows = jnp.concatenate([backward[0][3], backward[1][3]], axis=1)
    small_rows = jnp.concatenate(
        [
            dense_rows[3:5] + bias_rows[4:6],
            dense_rows[0:2],
            bias_rows[0:2],
            bias_rows[2:3] + bias_rows[2:3],
            bias_rows[3:4] - bias_rows[3:4],
            dense_rows[2:3],
            in_bias_grad.reshape(4, width),
        ],
        axis=0,
    )

    def shares(rows):
        flat = rows.reshape(-1)
        flat = jnp.pad(flat, (0, devices * small_share - flat.shape[0]))
        return jnp.pad(flat.reshape(devices, small_share), ((0, 0), (0, 4 * block - small_share)))

    early = scatter_bits(
        jnp.concatenate([filter_local, shares(small_rows)[:, None]], axis=1), IN_ORDER, 3, last
    )
    filter_grad = early[:filter_rows]
    small_grad = early[filter_rows, :small_share]

    input_grad = gather_grad(
        tokens,
        mixed_grad,
        grad_returned[0],
        grad_returned[1],
        lon_back,
        params,
    )

    filter_new, filter_m_new, filter_v_new, filter_ema_new = adam_update(
        filter_master, filter_grad, filter_m, filter_v, filter_ema, 0.2
    )
    in_new, in_m_new, in_v_new, in_ema_new = adam_update(
        in_master, in_grad, in_m, in_v, in_ema, 0.1
    )
    out_new, out_m_new, out_v_new, out_ema_new = adam_update(
        out_master, out_grad, out_m, out_v, out_ema, 0.05
    )
    small_new, small_m_new, small_v_new, small_ema_new = adam_update(
        small_master, small_grad, small_m, small_v, small_ema, 0.5
    )
    return (
        result,
        input_grad,
        filter_grad,
        in_grad,
        out_grad,
        small_grad,
        filter_new,
        in_new,
        out_new,
        small_new,
        filter_m_new,
        filter_v_new,
        in_m_new,
        in_v_new,
        out_m_new,
        out_v_new,
        small_m_new,
        small_v_new,
        filter_ema_new,
        in_ema_new,
        out_ema_new,
        small_ema_new,
    )


def solution(mesh):
    sizes = (mesh.shape["samp"], mesh.shape["sp"])
    samp = "samp"
    body = plain_shards
    if fits(sizes):
        samp = ("y", "core")
        mesh = Mesh(mesh.devices.reshape(2, 2, sizes[1]), AXES)
        body = functools.partial(fast_shards, sizes)
    every = (*samp, "sp") if isinstance(samp, tuple) else (samp, "sp")
    return jax.shard_map(
        body,
        mesh=mesh,
        in_specs=(
            P(samp, "sp", None, None),
            P(samp, "sp", None, None),
            P(samp),
            P(every, None),
            P(every, None),
            P(every, None),
            P(every),
            P(every, None),
            P(every, None),
            P(every, None),
            P(every, None),
            P(every, None),
            P(every, None),
            P(every),
            P(every),
            P(every, None),
            P(every, None),
            P(every, None),
            P(every),
        ),
        out_specs=(
            P(samp, "sp", None, None),
            P(samp, "sp", None, None),
            P(every, None),
            P(every, None),
            P(every, None),
            P(every),
            P(every, None),
            P(every, None),
            P(every, None),
            P(every),
            P(every, None),
            P(every, None),
            P(every, None),
            P(every, None),
            P(every, None),
            P(every, None),
            P(every),
            P(every),
            P(every, None),
            P(every, None),
            P(every, None),
            P(every),
        ),
        check_vma=False,
    )
```

```python
import functools
import math

import jax
import jax.numpy as jnp
import numpy as np
from jax import lax
from jax.experimental import pallas as pl
from jax.experimental.pallas import tpu as pltpu
from jax.sharding import Mesh
from jax.sharding import PartitionSpec as P

NB = 8
STEP = 10


HIGHEST = lax.Precision.HIGHEST
NORM_EPS = 1e-05
BETA_ONE = 0.9
BETA_TWO = 0.95
ADAM_EPS = 1e-08
DECAY = 0.05
EMA_KEEP = 0.75


def gelu_exact(values):
    return jax.nn.gelu(values, approximate=False)


def norm_forward(values):
    center = values - jnp.mean(values, axis=-1, keepdims=True)
    inv_std = lax.rsqrt(jnp.mean(center * center, axis=-1, keepdims=True) + NORM_EPS)
    return (center * inv_std, inv_std)


def norm_back(upstream, normed, inv_std, gain):
    scaled = upstream * gain
    first_mean = jnp.mean(scaled, axis=-1, keepdims=True)
    second_mean = jnp.mean(scaled * normed, axis=-1, keepdims=True)
    leading = tuple(range(upstream.ndim - 1))
    input_part = inv_std * (scaled - first_mean - normed * second_mean)
    return (input_part, jnp.sum(upstream * normed, axis=leading), jnp.sum(upstream, axis=leading))


def dft_table(points):
    positions = jnp.arange(points, dtype=jnp.int32)
    phases = positions[:, None] * positions[None, :] % points
    angles = phases.astype(jnp.float32) * (2.0 * math.pi / points)
    factor = 1.0 / math.sqrt(points)
    return (jnp.cos(angles) * factor, jnp.sin(angles) * factor)


def lat_table(cosine, sine_part, sign_value):
    upper_rows = jnp.stack([cosine, -sign_value * sine_part], axis=-1)
    lower_rows = jnp.stack([sign_value * sine_part, cosine], axis=-1)
    return jnp.stack([upper_rows, lower_rows], axis=1)


def split_table(table):
    upper_part = table.astype(jnp.bfloat16)
    lower_part = (table - upper_part.astype(jnp.float32)).astype(jnp.bfloat16)
    return (upper_part, lower_part)


def table_first(form, table, values):
    upper_part, lower_part = split_table(table)
    return jnp.einsum(form, upper_part, values, preferred_element_type=jnp.float32) + jnp.einsum(
        form, lower_part, values, preferred_element_type=jnp.float32
    )


def table_second(form, values, table):
    upper_part, lower_part = split_table(table)
    return jnp.einsum(form, values, upper_part, preferred_element_type=jnp.float32) + jnp.einsum(
        form, values, lower_part, preferred_element_type=jnp.float32
    )


def complex_mix(inputs, weight):
    shape_in = inputs.shape
    size_block = weight.shape[1] // 2
    grouped = inputs.reshape(shape_in[:4] + (NB, size_block))
    matrices = weight.reshape(NB, size_block, 2, size_block)
    product = jnp.einsum(
        "sgckbi,bieo->sgcekbo", grouped, matrices, preferred_element_type=jnp.float32
    )
    real_part = product[:, :, 0, 0] - product[:, :, 1, 1]
    imag_part = product[:, :, 1, 0] + product[:, :, 0, 1]
    return jnp.stack([real_part, imag_part], axis=2).reshape(shape_in)


def mix_back(upstream, inputs, weight):
    shape_in = inputs.shape
    size_block = weight.shape[1] // 2
    grouped = inputs.reshape(shape_in[:4] + (NB, size_block))
    upstream_grouped = upstream.reshape(shape_in[:4] + (NB, size_block))
    matrices = weight.reshape(NB, size_block, 2, size_block)
    toward = jnp.einsum(
        "sgekbo,bico->sgeckbi", upstream_grouped, matrices, preferred_element_type=jnp.float32
    )
    grad_real = toward[:, :, 0, 0] + toward[:, :, 1, 1]
    grad_imag = toward[:, :, 1, 0] - toward[:, :, 0, 1]
    grad_inputs = jnp.stack([grad_real, grad_imag], axis=2).reshape(shape_in)
    outer_sums = jnp.einsum(
        "sgckbi,sgekbo->cebio", grouped, upstream_grouped, preferred_element_type=jnp.float32
    )
    weight_real = outer_sums[0, 0] + outer_sums[1, 1]
    weight_imag = outer_sums[0, 1] - outer_sums[1, 0]
    weight_grad = jnp.stack([weight_real, weight_imag], axis=2).reshape(weight.shape)
    bias_grad = jnp.sum(upstream, axis=(0, 1, 3), dtype=jnp.float32)
    return (grad_inputs, weight_grad, bias_grad)


def adam_update(master, gradient, moment, second, average, step_rate):
    moment_new = BETA_ONE * moment + (1.0 - BETA_ONE) * gradient
    second_new = BETA_TWO * second + (1.0 - BETA_TWO) * gradient * gradient
    scaled_moment = moment_new / (1.0 - BETA_ONE**STEP)
    scaled_second = second_new / (1.0 - BETA_TWO**STEP)
    master_new = master - step_rate * (
        scaled_moment / (jnp.sqrt(scaled_second) + ADAM_EPS) + DECAY * master
    )
    average_new = EMA_KEEP * average + (1.0 - EMA_KEEP) * master_new
    return (master_new, moment_new, second_new, average_new)


def plain_shards(
    tokens,
    cotangent,
    storm_weight,
    filter_master,
    in_master,
    out_master,
    small_master,
    filter_m,
    filter_v,
    in_m,
    in_v,
    out_m,
    out_v,
    small_m,
    small_v,
    filter_ema,
    in_ema,
    out_ema,
    small_ema,
):
    filter_work, small_work = (
        lax.all_gather(filter_master.astype(jnp.bfloat16), ("samp", "sp"), axis=0, tiled=True),
        lax.all_gather(small_master.astype(jnp.bfloat16), ("samp", "sp"), axis=0, tiled=True),
    )
    width = filter_work.shape[0]
    size_block = width // NB
    params = small_work.astype(jnp.float32).reshape(13, width)
    inputs = tokens.astype(jnp.float32)
    normed_one, inv_one = norm_forward(inputs)
    first = normed_one * params[0] + params[1]
    lon_cos, lon_sin = dft_table(tokens.shape[2])
    lon_forward = jnp.stack([lon_cos, -lon_sin], axis=1)
    lon_inverse = jnp.stack([lon_cos, -lon_sin], axis=0)
    spectrum = jnp.einsum("shwd,wck->shckd", first, lon_forward, precision=HIGHEST).astype(
        jnp.bfloat16
    )
    arrived = lax.all_to_all(spectrum, "sp", split_axis=3, concat_axis=1, tiled=True)
    lat_cos, lat_sin = dft_table(arrived.shape[1])
    lat_forward = lat_table(lat_cos, lat_sin, -1.0)
    lat_inverse = lat_table(lat_cos, lat_sin, 1.0)
    modes = table_first("gohc,shckd->sgokd", lat_forward, arrived).astype(jnp.bfloat16)
    bias_one = params[4:6][:, None, :]
    bias_two = params[6:8][:, None, :]
    pre_one = complex_mix(modes, filter_work[:, : 2 * size_block]) + bias_one
    hidden_one = gelu_exact(pre_one).astype(jnp.bfloat16)
    pre_two = complex_mix(hidden_one, filter_work[:, 2 * size_block :]) + bias_two
    leaving = jnp.einsum("gohc,shckd->sgokd", lat_inverse, pre_two, precision=HIGHEST).astype(
        jnp.bfloat16
    )
    returned = lax.all_to_all(leaving, "sp", split_axis=1, concat_axis=3, tiled=True)
    spatial = table_second("shckd,ckw->shwd", returned, lon_inverse)
    mixed = spatial + first + inputs
    in_work, out_work = (
        lax.all_gather(in_master.astype(jnp.bfloat16), ("samp", "sp"), axis=0, tiled=True),
        lax.all_gather(out_master.astype(jnp.bfloat16), ("samp", "sp"), axis=0, tiled=True),
    )
    normed_two, inv_two = norm_forward(mixed)
    second = (normed_two * params[2] + params[3]).astype(jnp.bfloat16).reshape(-1, width)
    pre_dense = jnp.dot(second, in_work, preferred_element_type=jnp.float32) + params[9:13].reshape(
        -1
    )
    act_dense = gelu_exact(pre_dense).astype(jnp.bfloat16)
    branch = jnp.dot(act_dense, out_work, preferred_element_type=jnp.float32) + params[8]
    result = (mixed + branch.reshape(mixed.shape)).astype(jnp.bfloat16)
    filter_back = lax.all_gather(
        filter_master.astype(jnp.bfloat16), ("samp", "sp"), axis=0, tiled=True
    )
    in_back, out_back = (
        lax.all_gather(in_master.astype(jnp.bfloat16), ("samp", "sp"), axis=0, tiled=True),
        lax.all_gather(out_master.astype(jnp.bfloat16), ("samp", "sp"), axis=0, tiled=True),
    )
    sample_scale = storm_weight.astype(jnp.float32)[:, None, None, None] / 64.0
    grad_out = cotangent.astype(jnp.float32) * sample_scale
    grad_low = grad_out.astype(jnp.bfloat16).reshape(-1, width)
    out_local = jnp.einsum("tf,td->fd", act_dense, grad_low, preferred_element_type=jnp.float32)
    out_bias_grad = jnp.sum(grad_low, axis=0, dtype=jnp.float32)
    grad_act = jnp.einsum("td,fd->tf", grad_low, out_back, preferred_element_type=jnp.float32)
    dense_values, dense_pull = jax.vjp(gelu_exact, pre_dense)
    grad_pre = dense_pull(grad_act)[0].astype(jnp.bfloat16)
    in_local = jnp.einsum("td,tf->df", second, grad_pre, preferred_element_type=jnp.float32)
    in_bias_grad = jnp.sum(grad_pre, axis=0, dtype=jnp.float32)
    grad_second = jnp.einsum(
        "tf,df->td", grad_pre, in_back, preferred_element_type=jnp.float32
    ).reshape(mixed.shape)
    grad_norm_two, gain_two_grad, shift_two_grad = norm_back(
        grad_second, normed_two, inv_two, params[2]
    )
    grad_mixed = grad_out + grad_norm_two
    grad_leaving = jnp.einsum("shwd,ckw->shckd", grad_mixed, lon_inverse, precision=HIGHEST).astype(
        jnp.bfloat16
    )
    grad_arrived = lax.all_to_all(grad_leaving, "sp", split_axis=3, concat_axis=1, tiled=True)
    grad_pre_two = table_first("gohc,sgokd->shckd", lat_inverse, grad_arrived).astype(jnp.bfloat16)
    grad_hidden, weight_two_grad, bias_two_grad = mix_back(
        grad_pre_two, hidden_one, filter_back[:, 2 * size_block :]
    )
    gelu_values, gelu_pull = jax.vjp(gelu_exact, pre_one)
    grad_pre_one = gelu_pull(grad_hidden)[0].astype(jnp.bfloat16)
    grad_modes, weight_one_grad, bias_one_grad = mix_back(
        grad_pre_one, modes, filter_back[:, : 2 * size_block]
    )
    grad_spectrum = jnp.einsum(
        "gohc,sgokd->shckd", lat_forward, grad_modes, precision=HIGHEST
    ).astype(jnp.bfloat16)
    grad_sent = lax.all_to_all(grad_spectrum, "sp", split_axis=1, concat_axis=3, tiled=True)
    grad_first = grad_mixed + table_second("shckd,wck->shwd", grad_sent, lon_forward)
    grad_norm_one, gain_one_grad, shift_one_grad = norm_back(
        grad_first, normed_one, inv_one, params[0]
    )
    input_grad = grad_mixed + grad_norm_one
    norm_rows = jnp.stack([gain_one_grad, shift_one_grad, gain_two_grad, shift_two_grad])
    small_local = jnp.concatenate(
        [
            norm_rows,
            bias_one_grad,
            bias_two_grad,
            out_bias_grad[None, :],
            in_bias_grad.reshape(-1, width),
        ],
        axis=0,
    ).reshape(-1)
    filter_local = jnp.concatenate([weight_one_grad, weight_two_grad], axis=1)
    filter_grad, in_grad, out_grad, small_grad = (
        lax.psum_scatter(filter_local, ("samp", "sp"), scatter_dimension=0, tiled=True),
        lax.psum_scatter(in_local, ("samp", "sp"), scatter_dimension=0, tiled=True),
        lax.psum_scatter(out_local, ("samp", "sp"), scatter_dimension=0, tiled=True),
        lax.psum_scatter(small_local, ("samp", "sp"), scatter_dimension=0, tiled=True),
    )
    filter_new, filter_m_new, filter_v_new, filter_ema_new = adam_update(
        filter_master, filter_grad, filter_m, filter_v, filter_ema, 0.2
    )
    in_new, in_m_new, in_v_new, in_ema_new = adam_update(
        in_master, in_grad, in_m, in_v, in_ema, 0.1
    )
    out_new, out_m_new, out_v_new, out_ema_new = adam_update(
        out_master, out_grad, out_m, out_v, out_ema, 0.05
    )
    small_new, small_m_new, small_v_new, small_ema_new = adam_update(
        small_master, small_grad, small_m, small_v, small_ema, 0.5
    )
    return (
        result,
        input_grad,
        filter_grad,
        in_grad,
        out_grad,
        small_grad,
        filter_new,
        in_new,
        out_new,
        small_new,
        filter_m_new,
        filter_v_new,
        in_m_new,
        in_v_new,
        out_m_new,
        out_v_new,
        small_m_new,
        small_v_new,
        filter_ema_new,
        in_ema_new,
        out_ema_new,
        small_ema_new,
    )


F32 = jnp.float32
BF16 = jnp.bfloat16
LAT = 96
LON = 160
GROUP = 4
HALF = 384
ROWS = 208
FCHUNK = 512
VMEM_BYTES = 56 * 1024 * 1024
SCHED = pltpu.CompilerParams(vmem_limit_bytes=VMEM_BYTES)


def fits(sizes):
    parts = sizes[1]
    return sizes == (4, 8) and LAT % (parts * GROUP) == 0 and LON // 2 % (2 * parts) == 0


def cost(time_us, bytes_moved):
    return pl.CostEstimate(
        flops=int(time_us * 1.15e9), bytes_accessed=bytes_moved, transcendentals=0
    )


def dot(left, right, left_dim, right_dim):
    return lax.dot_general(
        left, right, (((left_dim,), (right_dim,)), ((), ())), preferred_element_type=F32
    )


def gelu_pair(values):
    cdf = 0.5 + 0.5 * lax.erf(values * math.sqrt(0.5))
    pdf = jnp.exp2(values * values * (-0.5 * math.log2(math.e))) * (1.0 / math.sqrt(2.0 * math.pi))
    return (values * cdf, cdf + values * pdf)


@functools.lru_cache(maxsize=None)
def lon_matrix():
    slots = LON // 2
    points = np.arange(LON)
    table = np.zeros((slots, 2, LON))
    for slot in range(slots):
        angles = 2.0 * np.pi * (slot * points % LON) / LON
        table[slot, 0] = np.cos(angles)
        table[slot, 1] = -np.sin(angles)
    table[0, 1] = np.where(points % 2 == 0, 1.0, -1.0)
    table /= np.sqrt(LON)
    full = np.zeros((slots, 2, GROUP, GROUP, LON))
    for row in range(GROUP):
        full[:, :, row, row, :] = table
    return full.reshape(slots * 2 * GROUP, GROUP * LON)


@functools.lru_cache(maxsize=None)
def lat_matrices(parts):
    per_part = LAT // parts
    groups = per_part // GROUP
    forward = np.zeros((2, 2, ROWS, LAT, 2, 2))
    share = np.zeros((2, ROWS))
    lat = np.arange(LAT)

    def put_plain(variant, start, slot):
        for mode in range(LAT):
            angles = 2.0 * np.pi * (mode * lat % LAT) / LAT
            forward[variant, 0, start + mode, :, slot, 0] = np.cos(angles)
            forward[variant, 0, start + mode, :, slot, 1] = np.sin(angles)
            forward[variant, 1, start + mode, :, slot, 0] = -np.sin(angles)
            forward[variant, 1, start + mode, :, slot, 1] = np.cos(angles)
            share[variant, start + mode] = 1.0

    half = LAT // 2 + 1
    for column in range(2):
        for mode in range(half):
            angles = 2.0 * np.pi * (mode * lat % LAT) / LAT
            row = column * half + mode
            own = mode in (0, LAT // 2)
            forward[0, 0, row, :, 0, column] = np.cos(angles)
            forward[0, 1, row, :, 0, column] = 0.0 if own else -np.sin(angles)
            share[0, row] = 0.5 if own else 1.0
    put_plain(0, 2 * half, 1)
    put_plain(1, 0, 0)
    put_plain(1, LAT, 1)
    forward /= np.sqrt(LAT)
    forward = forward.reshape(2, 2, ROWS, parts, groups, GROUP, 2, 2)
    forward = forward.transpose(0, 1, 2, 3, 4, 6, 7, 5)
    shift_row = np.zeros((2, ROWS, 128))
    shift_row[0, 0] = np.sqrt(LAT * LON)
    return (forward, share, shift_row)


def lat_tables(parts):
    forward, share, shift_row = lat_matrices(parts)
    tall = 2 * ROWS
    wide = forward[0].size // tall
    by_part = forward.reshape(2, tall, wide)
    by_group = forward.transpose(0, 1, 2, 4, 3, 5, 6, 7).reshape(2, tall, wide)
    weights = np.concatenate([share, share], axis=1)[:, :, None]
    tables = (
        by_part,
        (weights * by_group).transpose(0, 2, 1),
        weights * by_group,
        by_part.transpose(0, 2, 1),
    )
    return tuple(jnp.asarray(table, BF16) for table in tables) + (jnp.asarray(shift_row, F32),)


def normalise(values):
    center = values - jnp.mean(values, axis=-1, keepdims=True)
    inv_std = lax.rsqrt(jnp.mean(center * center, axis=-1, keepdims=True) + NORM_EPS)
    return (center * inv_std, inv_std)


def spread_body(tokens_ref, table_ref, filter_ref, small_ref, low_ref, high_ref):
    step = pl.program_id(0)
    values = tokens_ref[...].astype(F32).reshape(GROUP * LON, 2 * HALF)
    normed, _ = normalise(values)
    out = dot(table_ref[...], normed.astype(BF16), 1, 0).astype(BF16)
    pairs = high_ref.shape[1]
    parts = high_ref.shape[0]
    units = low_ref.shape[1]
    low_ref[:, pl.ds(step * pairs, pairs)] = out[:, :HALF].reshape(parts, pairs, 16, HALF)
    high_ref[...] = out[:, HALF:].reshape(parts, pairs, 16, HALF)

    @pl.when(step == 0)
    def _():
        rows = filter_ref.shape[0]
        extra = units - pl.num_programs(0) * pairs
        spare = jnp.zeros((16 * extra - rows - 1, HALF), F32)
        own = jnp.concatenate([filter_ref[...], small_ref[...], spare], axis=0).astype(BF16)
        own = own.reshape(1, extra, 16, HALF)
        low_ref[:, units - extra :] = jnp.broadcast_to(own, (parts, extra, 16, HALF))


def spread(tokens, table, filter_rows, small_row, parts):
    groups = tokens.shape[1] // GROUP
    pairs = LON // 4 // parts
    extra = filter_rows.shape[0] // 16 + 1
    low = (parts, groups * pairs + extra, 16, HALF)
    high = (parts, groups * pairs, 16, HALF)

    def whole(*shape):
        return pl.BlockSpec(shape, lambda r: (0,) * len(shape))

    return pl.pallas_call(
        spread_body,
        name="norm_and_longitude",
        grid=(groups,),
        in_specs=[
            pl.BlockSpec((1, GROUP, LON, 2 * HALF), lambda r: (0, r, 0, 0)),
            whole(*table.shape),
            whole(*filter_rows.shape),
            whole(*small_row.shape),
        ],
        out_specs=[
            whole(*low),
            pl.BlockSpec((parts, pairs, 16, HALF), lambda r: (0, r, 0, 0)),
        ],
        out_shape=[jax.ShapeDtypeStruct(low, BF16), jax.ShapeDtypeStruct(high, BF16)],
        compiler_params=SCHED,
        cost_estimate=cost(7, 2 * tokens.size),
    )(tokens, table, filter_rows, small_row)


def unit_specs(parts, groups, pairs):
    return [
        pl.BlockSpec((parts, 1, 16, HALF), lambda b, pick_ref, r=r: (0, r * pairs + b, 0, 0))
        for r in range(groups)
    ]


def stacked(refs):
    return jnp.concatenate([ref[...] for ref in refs], axis=1).reshape(-1, HALF)


def filter_body(
    pieces,
    pick_ref,
    *refs,
):
    arrived_refs = refs[: sum(pieces)]
    forward_ref, inverse_ref, shift_row_ref, params_ref, one_ref, two_ref, *outs = refs[
        sum(pieces) :
    ]
    back_refs = outs[:-3]
    modes_ref, sums_ref, slopes_ref = outs[-3:]
    columns = forward_ref.shape[-1]
    raw = dot(forward_ref[0], stacked(arrived_refs), 1, 0)
    gain = params_ref[0:1, :]
    shift = params_ref[1:2, :]
    modes_re = (raw[:ROWS] * gain + shift_row_ref[0, :, 0:1] * shift).astype(BF16)
    modes_im = (raw[ROWS:] * gain).astype(BF16)
    modes_ref[0, :ROWS] = modes_re
    modes_ref[0, ROWS:] = modes_im
    from_re = dot(modes_re, one_ref[0], 1, 0)
    from_im = dot(modes_im, one_ref[0], 1, 0)
    bias_re = params_ref[4:5, :]
    bias_im = params_ref[5:6, :]
    re_a = from_re[:, :HALF] + bias_re
    re_b = from_re[:, HALF:] + bias_im
    im_a = from_im[:, :HALF]
    im_b = from_im[:, HALF:]
    plus_re, slope = gelu_pair(re_a - im_b)
    slopes_ref[0, 0] = slope.astype(BF16)
    minus_re, slope = gelu_pair(re_a + im_b)
    slopes_ref[0, 1] = slope.astype(BF16)
    sums_ref[0, 0, :, :HALF] = (plus_re + minus_re).astype(BF16)
    sums_ref[0, 1, :, HALF:] = (plus_re - minus_re).astype(BF16)
    plus_im, slope = gelu_pair(re_b + im_a)
    slopes_ref[0, 2] = slope.astype(BF16)
    minus_im, slope = gelu_pair(re_b - im_a)
    slopes_ref[0, 3] = slope.astype(BF16)
    sums_ref[0, 0, :, HALF:] = (-plus_im - minus_im).astype(BF16)
    sums_ref[0, 1, :, :HALF] = (plus_im - minus_im).astype(BF16)
    two_bias_re = params_ref[6:7, :]
    two_bias_im = params_ref[7:8, :]
    two_re = dot(sums_ref[0, 0], two_ref[0], 1, 0) + (two_bias_re + two_bias_re)
    two_im = dot(sums_ref[0, 1], two_ref[0], 1, 0) + (two_bias_im - two_bias_im)
    both = jnp.concatenate([two_re.astype(BF16), two_im.astype(BF16)], axis=0)
    back = dot(inverse_ref[0], both, 1, 0).astype(BF16)
    step = columns // sum(pieces)
    group = 0
    for ref, count in zip(back_refs, pieces):
        for place in range(count):
            rows = back[group * step : (group + 1) * step]
            ref[:, place] = rows.reshape(-1, 1, 16, HALF)
            group += 1


def filter_forward(pick, arrived, tables, params, one, two, part_of_channels, pieces):
    parts = arrived.shape[0]
    groups = sum(pieces)
    pairs = LON // 4 // parts
    forward, inverse, _, _, shift_row = tables
    q = part_of_channels
    tall = 2 * ROWS

    def chosen(*shape):
        return pl.BlockSpec((1,) + shape, lambda b, pick_ref: (pick_ref[b], 0, 0))

    def fixed(*shape):
        return pl.BlockSpec((1,) + shape, lambda b, pick_ref: (q, 0, 0))

    def stepped(*shape):
        zeros = (0,) * len(shape)
        return pl.BlockSpec((1,) + shape, lambda b, pick_ref: (b,) + zeros)

    back_blocks = [
        pl.BlockSpec((parts, count, 1, 16, HALF), lambda b, pick_ref: (0, 0, b, 0, 0))
        for count in pieces
    ]
    back_shapes = [jax.ShapeDtypeStruct((parts, count, pairs, 16, HALF), BF16) for count in pieces]
    columns = forward.shape[-1]
    return pl.pallas_call(
        functools.partial(filter_body, pieces),
        name="filter_forward",
        grid_spec=pltpu.PrefetchScalarGridSpec(
            num_scalar_prefetch=1,
            grid=(pairs,),
            in_specs=unit_specs(parts, groups, pairs)
            + [
                chosen(tall, columns),
                chosen(columns, tall),
                chosen(ROWS, 128),
                pl.BlockSpec((16, HALF), lambda b, pick_ref: (0, q)),
                fixed(HALF, 2 * HALF),
                fixed(2 * HALF, HALF),
            ],
            out_specs=back_blocks
            + [stepped(tall, HALF), stepped(2, ROWS, 2 * HALF), stepped(4, ROWS, HALF)],
        ),
        out_shape=back_shapes
        + [
            jax.ShapeDtypeStruct((pairs, tall, HALF), BF16),
            jax.ShapeDtypeStruct((pairs, 2, ROWS, 2 * HALF), BF16),
            jax.ShapeDtypeStruct((pairs, 4, ROWS, HALF), BF16),
        ],
        compiler_params=SCHED,
        cost_estimate=cost(14, 12 * 1024 * 1024),
    )(pick, *[arrived] * groups, forward, inverse, shift_row, params, one, two)


def filter_back_body(
    groups,
    pick_ref,
    *refs,
):
    arrived_refs = refs[:groups]
    adjoint_ref, inverse_ref, shift_row_ref, one_ref, two_ref = refs[groups : groups + 5]
    normed_refs = refs[groups + 5 : 2 * groups + 5]
    modes_ref, sums_ref, slopes_ref = refs[2 * groups + 5 : 2 * groups + 8]
    sent_ref, one_grad_ref, two_grad_ref, bias_ref = refs[2 * groups + 8 :]
    columns = adjoint_ref.shape[-1]
    step = columns // groups
    arrived = jnp.concatenate([ref[...].reshape(step, HALF) for ref in arrived_refs], axis=0)
    grad = dot(adjoint_ref[0], arrived, 1, 0)
    grad_re = grad[:ROWS].astype(BF16)
    grad_im = grad[ROWS:].astype(BF16)
    from_re = dot(grad_re, two_ref[0], 1, 1)
    from_im = dot(grad_im, two_ref[0], 1, 1)
    du = from_re[:, :HALF]
    dv = -from_re[:, HALF:]
    dw = from_im[:, :HALF]
    dx = from_im[:, HALF:]
    plus_re = (du + dx) * slopes_ref[0, 0].astype(F32)
    minus_re = (du - dx) * slopes_ref[0, 1].astype(F32)
    plus_im = (dv + dw) * slopes_ref[0, 2].astype(F32)
    minus_im = (dv - dw) * slopes_ref[0, 3].astype(F32)
    re_a = plus_re + minus_re
    im_b = minus_re - plus_re
    im_a = plus_im - minus_im
    re_b = plus_im + minus_im
    out_re = jnp.concatenate([re_a.astype(BF16), re_b.astype(BF16)], axis=1)
    out_im = jnp.concatenate([im_a.astype(BF16), im_b.astype(BF16)], axis=1)
    modes_re = dot(out_re, one_ref[0], 1, 1)
    modes_im = dot(out_im, one_ref[0], 1, 1)
    both = jnp.concatenate([modes_re.astype(BF16), modes_im.astype(BF16)], axis=0)
    sent = dot(inverse_ref[0], both, 1, 0).astype(BF16)
    sent_ref[...] = sent.reshape(sent_ref.shape)
    one_part = dot(modes_ref[0, :ROWS], out_re, 0, 0) + dot(modes_ref[0, ROWS:], out_im, 0, 0)
    two_part = dot(sums_ref[0, 0], grad_re, 0, 0) + dot(sums_ref[0, 1], grad_im, 0, 0)
    gain_part = sent.astype(F32) * stacked(normed_refs).astype(F32)
    shift_part = modes_re * shift_row_ref[0, :, 0:1]
    rows = [
        jnp.sum(part, axis=0, keepdims=True)
        for part in (re_a, re_b, grad[:ROWS], grad[ROWS:], gain_part, shift_part)
    ]
    bias_part = jnp.concatenate(rows + [jnp.zeros((2, HALF), F32)], axis=0)
    first = pl.program_id(0) == 0

    @pl.when(first)
    def _():
        one_grad_ref[...] = one_part
        two_grad_ref[...] = two_part
        bias_ref[...] = bias_part

    @pl.when(jnp.logical_not(first))
    def _():
        one_grad_ref[...] += one_part
        two_grad_ref[...] += two_part
        bias_ref[...] += bias_part


def filter_backward(pick, arrived, tables, one, two, normed, modes, sums, slopes, part_of_channels):
    groups = len(arrived)
    parts, pairs = arrived[0].shape[:2]
    _, _, adjoint, inverse, shift_row = tables
    q = part_of_channels
    tall = 2 * ROWS
    columns = adjoint.shape[-1]

    def chosen(*shape):
        return pl.BlockSpec((1,) + shape, lambda b, pick_ref: (pick_ref[b], 0, 0))

    def fixed(*shape):
        return pl.BlockSpec((1,) + shape, lambda b, pick_ref: (q, 0, 0))

    def stepped(*shape):
        zeros = (0,) * len(shape)
        return pl.BlockSpec((1,) + shape, lambda b, pick_ref: (b,) + zeros)

    def whole(*shape):
        return pl.BlockSpec(shape, lambda b, pick_ref: (0,) * len(shape))

    arrived_block = pl.BlockSpec((parts, 1, 16, HALF), lambda b, pick_ref: (0, b, 0, q))
    return pl.pallas_call(
        functools.partial(filter_back_body, groups),
        name="filter_backward",
        grid_spec=pltpu.PrefetchScalarGridSpec(
            num_scalar_prefetch=1,
            grid=(pairs,),
            in_specs=[arrived_block] * groups
            + [
                chosen(tall, columns),
                chosen(columns, tall),
                chosen(ROWS, 128),
                fixed(HALF, 2 * HALF),
                fixed(2 * HALF, HALF),
            ]
            + unit_specs(parts, groups, pairs)
            + [
                stepped(tall, HALF),
                stepped(2, ROWS, 2 * HALF),
                stepped(4, ROWS, HALF),
            ],
            out_specs=[
                pl.BlockSpec((parts, groups, 1, 16, HALF), lambda b, pick_ref: (0, 0, b, 0, 0)),
                whole(HALF, 2 * HALF),
                whole(2 * HALF, HALF),
                whole(8, HALF),
            ],
        ),
        out_shape=[
            jax.ShapeDtypeStruct((parts, groups, pairs, 16, HALF), BF16),
            jax.ShapeDtypeStruct((HALF, 2 * HALF), F32),
            jax.ShapeDtypeStruct((2 * HALF, HALF), F32),
            jax.ShapeDtypeStruct((8, HALF), F32),
        ],
        compiler_params=SCHED,
        cost_estimate=cost(18, 12 * 1024 * 1024),
    )(pick, *arrived, adjoint, inverse, shift_row, one, two, *[normed] * groups, modes, sums, slopes)


def dense_body(
    tokens_ref,
    cotangent_ref,
    low_ref,
    high_ref,
    inverse_ref,
    table_ref,
    params_ref,
    in_bias_ref,
    in_ref,
    out_ref,
    *refs,
):
    (
        result_ref,
        mixed_grad_ref,
        second_ref,
        grad_low_ref,
        act_ref,
        grad_pre_ref,
        sent_ref,
        in_bias_grad_ref,
        rows_ref,
        branch_ref,
        grad_second_ref,
        normed_two_ref,
        inv_two_ref,
        normed_one_ref,
    ) = refs[-14:]
    chunk = pl.program_id(0)
    count = GROUP * LON
    wide = 2 * HALF

    @pl.when(chunk == 0)
    def _():
        inputs = tokens_ref[...].astype(F32).reshape(count, wide)
        normed, _ = normalise(inputs)
        normed_one_ref[...] = normed.astype(BF16)
        base = normed * params_ref[0:1, :] + params_ref[1:2, :] + inputs
        arrived = jnp.concatenate(
            [low_ref[...].reshape(count, HALF), high_ref[...].reshape(count, HALF)], axis=1
        )
        mixed = dot(inverse_ref[...], arrived, 1, 0) + base
        branch_ref[...] = mixed + params_ref[8:9, :]
        normed_two, inv_two = normalise(mixed)
        normed_two_ref[...] = normed_two
        inv_two_ref[...] = jnp.broadcast_to(inv_two, inv_two_ref.shape)
        second_ref[...] = (normed_two * params_ref[2:3, :] + params_ref[3:4, :]).astype(BF16)
        grad_low_ref[...] = (
            cotangent_ref[...].astype(F32).reshape(count, wide) * params_ref[13:14, :]
        ).astype(BF16)
        grad_second_ref[...] = jnp.zeros_like(grad_second_ref)

    pre = dot(second_ref[...], in_ref[...], 1, 0) + in_bias_ref[...]
    grad_act = dot(grad_low_ref[...], out_ref[...], 1, 1)
    act, slope = gelu_pair(pre)
    act = act.astype(BF16)
    grad_pre = grad_act * slope
    in_bias_grad_ref[...] = jnp.sum(grad_pre, axis=0, keepdims=True)
    grad_pre = grad_pre.astype(BF16)
    act_ref[...] = act
    grad_pre_ref[...] = grad_pre
    branch_ref[...] += dot(act, out_ref[...], 1, 0)
    grad_second_ref[...] += dot(grad_pre, in_ref[...], 1, 1)

    @pl.when(chunk == pl.num_programs(0) - 1)
    def _():
        result_ref[...] = branch_ref[...].astype(BF16).reshape(result_ref.shape)
        normed_two = normed_two_ref[...]
        inv_two = inv_two_ref[:, 0:1]
        upstream = grad_second_ref[...]
        scaled = upstream * params_ref[2:3, :]
        first_mean = jnp.mean(scaled, axis=-1, keepdims=True)
        second_mean = jnp.mean(scaled * normed_two, axis=-1, keepdims=True)
        grad_out = cotangent_ref[...].astype(F32).reshape(count, wide) * params_ref[13:14, :]
        mixed_grad = grad_out + inv_two * (scaled - first_mean - normed_two * second_mean)
        mixed_grad_ref[...] = mixed_grad.reshape(mixed_grad_ref.shape)
        rows = [
            jnp.sum(part, axis=0, keepdims=True)
            for part in (upstream * normed_two, upstream, grad_low_ref[...].astype(F32))
        ]
        normed_one = normed_one_ref[...].astype(F32)
        rows += [
            jnp.sum(part, axis=0, keepdims=True) for part in (mixed_grad * normed_one, mixed_grad)
        ]
        rows_ref[...] = jnp.concatenate(rows + [jnp.zeros((3, wide), F32)], axis=0)
        sent = dot(table_ref[...], mixed_grad.astype(BF16), 1, 0).astype(BF16)
        sent_ref[...] = sent.reshape(sent_ref.shape)


def dense(
    kept, tokens, cotangent, low, high, places, inverse, table, params, in_bias, in_work, out_work, group
):
    parts, _, pairs = high.shape[:3]
    groups = tokens.shape[1] // GROUP
    count = GROUP * LON
    wide = 2 * HALF
    hidden = in_work.shape[1]

    def whole(*shape):
        return pl.BlockSpec(shape, lambda f: (0,) * len(shape))

    rows = pl.BlockSpec((1, GROUP, LON, wide), lambda f: (0, group, 0, 0))
    low_spec, high_spec = (
        pl.BlockSpec((parts, 1, pairs, 16, HALF), lambda f, place=place: (0, place, 0, 0, 0))
        for place in places
    )
    token_rows = pl.BlockSpec((count, wide), lambda f: (group, 0))
    hidden_rows = pl.BlockSpec((count, FCHUNK), lambda f: (group, f))
    return pl.pallas_call(
        dense_body,
        name="dense_group",
        grid=(hidden // FCHUNK,),
        in_specs=[
            rows,
            rows,
            low_spec,
            high_spec,
            whole(*inverse.shape),
            whole(*table.shape),
            whole(16, wide),
            pl.BlockSpec((1, FCHUNK), lambda f: (0, f)),
            pl.BlockSpec((wide, FCHUNK), lambda f: (0, f)),
            pl.BlockSpec((FCHUNK, wide), lambda f: (f, 0)),
        ]
        + [pl.BlockSpec(memory_space=pl.ANY)] * len(kept),
        out_specs=[
            rows,
            rows,
            token_rows,
            token_rows,
            hidden_rows,
            hidden_rows,
            whole(parts, pairs, 16, wide),
            pl.BlockSpec((1, FCHUNK), lambda f: (0, f)),
            whole(8, wide),
        ],
        out_shape=[
            jax.ShapeDtypeStruct(tokens.shape, BF16),
            jax.ShapeDtypeStruct(tokens.shape, F32),
            jax.ShapeDtypeStruct((groups * count, wide), BF16),
            jax.ShapeDtypeStruct((groups * count, wide), BF16),
            jax.ShapeDtypeStruct((groups * count, hidden), BF16),
            jax.ShapeDtypeStruct((groups * count, hidden), BF16),
            jax.ShapeDtypeStruct((parts, pairs, 16, wide), BF16),
            jax.ShapeDtypeStruct((1, hidden), F32),
            jax.ShapeDtypeStruct((8, wide), F32),
        ],
        scratch_shapes=[pltpu.VMEM((count, wide), F32)] * 3
        + [pltpu.VMEM((count, 128), F32), pltpu.VMEM((count, wide), BF16)],
        input_output_aliases={10 + i: i for i in range(len(kept))},
        compiler_params=SCHED,
        cost_estimate=cost(25, 30 * 1024 * 1024),
    )(tokens, cotangent, low, high, inverse, table, params, in_bias, in_work, out_work, *kept)


def gather_grad_body(
    tokens_ref, mixed_grad_ref, low_ref, high_ref, inverse_ref, params_ref, grad_ref
):
    count = GROUP * LON
    wide = 2 * HALF
    mixed_grad = mixed_grad_ref[...].reshape(count, wide)
    low = dot(inverse_ref[...], low_ref[...].reshape(count, HALF), 1, 0)
    high = dot(inverse_ref[...], high_ref[...].reshape(count, HALF), 1, 0)
    upstream = mixed_grad + jnp.concatenate([low, high], axis=1)
    normed, inv_std = normalise(tokens_ref[...].astype(F32).reshape(count, wide))
    scaled = upstream * params_ref[0:1, :]
    first_mean = jnp.mean(scaled, axis=-1, keepdims=True)
    second_mean = jnp.mean(scaled * normed, axis=-1, keepdims=True)
    out = mixed_grad + inv_std * (scaled - first_mean - normed * second_mean)
    grad_ref[...] = out.reshape(grad_ref.shape)


def gather_grad(tokens, mixed_grad, low, high, inverse, params):
    parts, groups, pairs = low.shape[:3]
    wide = 2 * HALF

    def whole(*shape):
        return pl.BlockSpec(shape, lambda r: (0,) * len(shape))

    rows = pl.BlockSpec((1, GROUP, LON, wide), lambda r: (0, r, 0, 0))
    arrived = pl.BlockSpec((parts, 1, pairs, 16, HALF), lambda r: (0, r, 0, 0, 0))
    return pl.pallas_call(
        gather_grad_body,
        name="longitude_and_norm_grad",
        grid=(groups,),
        in_specs=[rows, rows, arrived, arrived, whole(*inverse.shape), whole(16, wide)],
        out_specs=rows,
        out_shape=jax.ShapeDtypeStruct((1, groups * GROUP, LON, wide), F32),
        compiler_params=SCHED,
        cost_estimate=cost(12, 16 * 1024 * 1024),
    )(tokens, mixed_grad, low, high, inverse, params)


def block_matrices(weight):
    size = weight.shape[1] // 4
    places = np.arange(HALF)
    pick = (np.arange(4 * size)[:, None, None] == np.arange(4)[:, None] * size + places % size)
    own = places[:, None] // size == places[None, :] // size
    halves = weight.reshape(2, HALF, 4 * size)

    def spread_columns(form, first):
        full = jnp.einsum(
            form, halves, jnp.asarray(pick[:, first : first + 2], BF16), preferred_element_type=F32
        )
        return full

    one = spread_columns("qrc,cpn->qrpn", 0) * own[:, None, :]
    two = spread_columns("qrc,cpn->qprn", 2) * own
    return (
        one.astype(BF16).reshape(2, HALF, 2 * HALF),
        two.astype(BF16).reshape(2, 2 * HALF, HALF),
    )


def own_blocks(matrix, size):
    count = HALF // size
    return jnp.concatenate(
        [matrix[i * size : (i + 1) * size, i * size : (i + 1) * size] for i in range(count)], axis=0
    )


def in_turn(values, last):
    return lax.optimization_barrier((values, last))[0]


def exchange(values, last=None):
    if last is not None:
        values = in_turn(values, last)
    return lax.all_to_all(values, "sp", split_axis=0, concat_axis=0, tiled=True)


AXES = ("y", "core", "sp")
BITS = (("y", 1), ("core", 1), ("sp", 4), ("sp", 2), ("sp", 1))
SIZES = {"y": 2, "core": 2, "sp": 8}


def swap(values, axis, bit):
    return lax.ppermute(values, axis, [(i, i ^ bit) for i in range(SIZES[axis])])


def mine(axis, bit):
    return (lax.axis_index(axis) // bit) % 2


def gather_bit(values, axis, bit, place=0, last=None):
    other = swap(values, axis, bit)
    if last is not None:
        other = in_turn(other, last)
    low = mine(axis, bit) == 0
    return jnp.stack([jnp.where(low, values, other), jnp.where(low, other, values)], axis=place)


def gather_steps(values, held, order, last=None):
    for axis, bit in order:
        held = sorted([*held, (axis, bit)], key=BITS.index)
        values = gather_bit(values, axis, bit, held.index((axis, bit)), last)
    return values, held


def scatter_small(values, last):
    held = list(BITS)
    values = values.reshape((2,) * len(held) + values.shape[1:])
    for step, (axis, bit) in enumerate(IN_ORDER):
        if step == 3:
            values = in_turn(values, last)
        place = held.index((axis, bit))
        keep = lax.dynamic_index_in_dim(values, mine(axis, bit), place, keepdims=False)
        give = lax.dynamic_index_in_dim(values, 1 - mine(axis, bit), place, keepdims=False)
        values = keep + swap(give, axis, bit)
        held.pop(place)
    return values


SMALL = pl.CostEstimate(flops=1 << 20, bytes_accessed=1 << 20, transcendentals=0)
IN_ORDER = (("core", 1), ("y", 1), ("sp", 1), ("sp", 2), ("sp", 4))
OUT_ORDER = (("core", 1), ("sp", 1), ("y", 1), ("sp", 2), ("sp", 4))


def device_rows(order):
    lists = []
    for core in range(2):
        indices = []
        for count in range(16):
            samp, sp = core, 0
            for place, (axis, bit) in enumerate(order[1:]):
                if count >> (3 - place) & 1:
                    samp, sp = (samp + 2 * bit, sp) if axis == "y" else (samp, sp + bit)
            indices.append(samp * 8 + sp)
        lists.append(indices)
    return lists


def in_weight_grad_body(pick_ref, second_ref, grad_pre_ref, keep_ref, give_ref):
    out = dot(second_ref[...], grad_pre_ref[...], 0, 0)
    rows = out.shape[0] // 32
    halves = [
        jnp.concatenate([out[i * rows : (i + 1) * rows] for i in indices], axis=0).astype(BF16)
        for indices in device_rows(IN_ORDER)
    ]

    @pl.when(pick_ref[0] == 0)
    def _():
        keep_ref[...] = halves[0]
        give_ref[...] = halves[1]

    @pl.when(pick_ref[0] == 1)
    def _():
        keep_ref[...] = halves[1]
        give_ref[...] = halves[0]


def in_weight_grad(core, second, grad_pre):
    tokens, wide = second.shape
    hidden = grad_pre.shape[1]
    step = 512
    half = pl.BlockSpec((wide // 2, step), lambda i, pick_ref: (0, i))
    return pl.pallas_call(
        in_weight_grad_body,
        name="in_weight_grad",
        grid_spec=pltpu.PrefetchScalarGridSpec(
            num_scalar_prefetch=1,
            grid=(hidden // step,),
            in_specs=[
                pl.BlockSpec((tokens, wide), lambda i, pick_ref: (0, 0)),
                pl.BlockSpec((tokens, step), lambda i, pick_ref: (0, i)),
            ],
            out_specs=[half, half],
        ),
        out_shape=[jax.ShapeDtypeStruct((wide // 2, hidden), BF16)] * 2,
        compiler_params=SCHED,
        cost_estimate=SMALL,
    )(core, second, grad_pre)


def out_weight_grad_body(pick_ref, act_ref, grad_low_ref, keep_ref, give_ref):
    out = dot(act_ref[...], grad_low_ref[...], 0, 0)
    rows = out.shape[0] // 8
    out = out.astype(BF16)
    pieces = [
        jnp.concatenate(
            [
                out[(z1 * 4 + z0 * 2 + x) * rows : (z1 * 4 + z0 * 2 + x + 1) * rows]
                for z0 in range(2)
                for z1 in range(2)
            ],
            axis=0,
        )
        for x in range(2)
    ]

    @pl.when(pl.program_id(0) == 0)
    def _():
        for x in range(2):
            keep_ref[x, 0] = pieces[x]

    @pl.when(pl.program_id(0) == 1)
    def _():
        for x in range(2):
            give_ref[x, 0] = pieces[x]


def out_weight_grad(core, act, grad_low):
    tokens, hidden = act.shape
    wide = grad_low.shape[1]
    part = hidden // 4
    shape = (2, 2, part // 2, wide)

    def columns(give, y, pick_ref):
        return (0, y * 2 + (pick_ref[0] + give) % 2)

    keep, give = pl.pallas_call(
        out_weight_grad_body,
        name="out_weight_grad",
        grid_spec=pltpu.PrefetchScalarGridSpec(
            num_scalar_prefetch=1,
            grid=(2, 2),
            in_specs=[
                pl.BlockSpec((tokens, part), columns),
                pl.BlockSpec((tokens, wide), lambda give, y, pick_ref: (0, 0)),
            ],
            out_specs=[
                pl.BlockSpec(
                    (2, 1) + shape[2:], lambda give, y, pick_ref: (0, jnp.maximum(y, give), 0, 0)
                ),
                pl.BlockSpec((2, 1) + shape[2:], lambda give, y, pick_ref: (0, y * give, 0, 0)),
            ],
        ),
        out_shape=[jax.ShapeDtypeStruct(shape, BF16)] * 2,
        compiler_params=SCHED,
        cost_estimate=SMALL,
    )(core, act, grad_low)
    return keep.reshape(-1, wide), give.reshape(-1, wide)


def add_split_body(pick_ref, keep_one, got_one, keep_two, got_two, keep_ref, give_ref):
    keep_ref[...] = (keep_one[...].astype(F32) + got_one[...].astype(F32)).astype(BF16)
    give_ref[...] = (keep_two[...].astype(F32) + got_two[...].astype(F32)).astype(BF16)


def add_split(pick, keep, got):
    rows, columns = keep.shape
    steps = 2 if rows % 64 == 0 else 1
    block = (rows // 2 // steps, columns)
    stays = pl.BlockSpec(block, lambda i, pick_ref: (pick_ref[0] * steps + i, 0))
    goes = pl.BlockSpec(block, lambda i, pick_ref: ((1 - pick_ref[0]) * steps + i, 0))
    out = pl.BlockSpec(block, lambda i, pick_ref: (i, 0))
    return pl.pallas_call(
        add_split_body,
        name="add_split",
        grid_spec=pltpu.PrefetchScalarGridSpec(
            num_scalar_prefetch=1,
            grid=(steps,),
            in_specs=[stays, stays, goes, goes],
            out_specs=[out, out],
        ),
        out_shape=[jax.ShapeDtypeStruct((rows // 2, columns), BF16)] * 2,
        compiler_params=SCHED,
        cost_estimate=SMALL,
    )(pick, keep, got, keep, got)


def picks(order):
    return [mine(axis, bit).astype(jnp.int32).reshape(1) for axis, bit in order]


def scatter_steps(keep, give, order, chosen, first, last):
    for place in range(first, last):
        keep, give = add_split(chosen[place + 1], keep, swap(give, *order[place]))
    return keep, give


def scatter_last(keep, give, order):
    return keep.astype(F32) + swap(give, *order[-1]).astype(F32)


def fast_shards(
    sizes,
    tokens,
    cotangent,
    storm_weight,
    filter_master,
    in_master,
    out_master,
    small_master,
    filter_m,
    filter_v,
    in_m,
    in_v,
    out_m,
    out_v,
    small_m,
    small_v,
    filter_ema,
    in_ema,
    out_ema,
    small_ema,
):
    parts = sizes[1]
    devices = sizes[0] * sizes[1]
    groups = tokens.shape[1] // GROUP
    pairs = LON // 4 // parts
    width = tokens.shape[-1]
    block = width // NB
    small_share = small_master.shape[0]
    sp_index = lax.axis_index("sp")

    lon = lon_matrix()
    lon_table = jnp.asarray(lon, BF16)
    lon_back = jnp.asarray(lon.T, BF16)
    tables = lat_tables(parts)
    pick = jnp.where((sp_index == 0) & (jnp.arange(pairs) == 0), 0, 1).astype(jnp.int32)

    filter_rows = filter_master.shape[0]
    small_row = jnp.pad(small_master, (0, 4 * block - small_share)).reshape(1, -1)
    in_gather, out_gather = IN_ORDER[::-1], OUT_ORDER[::-1]
    in_part, in_held = gather_steps(in_master.astype(BF16), [], in_gather[:1])
    out_part, out_held = gather_steps(out_master.astype(BF16), [], out_gather[:1])
    sent = spread(tokens, lon_table, filter_master, small_row, parts)
    arrived_low = exchange(sent[0], (in_part, out_part))
    arrived_high = exchange(sent[1], arrived_low)

    units = groups * pairs
    near = arrived_low[:, units:].reshape(parts, -1, 4 * block)
    packed_all = gather_bit(gather_bit(near, "core", 1), "y", 1)
    packed_all = packed_all.reshape((devices,) + near.shape[1:])
    filter_work = packed_all[:, :filter_rows].reshape(width, 4 * block)
    small_work = packed_all[:, filter_rows, :small_share].reshape(-1)

    in_rows, hidden = in_master.shape
    params = small_work.astype(F32).reshape(13, width)
    scale = storm_weight.astype(F32)[0] / 64.0
    in_bias = params[9:13].reshape(1, -1)
    params = jnp.concatenate(
        [params, jnp.full((1, width), scale, F32), jnp.zeros((2, width), F32)], axis=0
    )
    one, two = block_matrices(filter_work)

    in_part, in_held = gather_steps(in_part, in_held, in_gather[1:2])
    out_part, out_held = gather_steps(out_part, out_held, out_gather[1:2])
    in_part, out_part = in_turn((in_part, out_part), arrived_low)
    in_part, in_held = gather_steps(in_part, in_held, in_gather[2:3])
    out_part, out_held = gather_steps(out_part, out_held, out_gather[2:3])
    forward_low = filter_forward(pick, arrived_low, tables, params, one, two, 0, (groups,))
    returned_low = exchange(forward_low[0], arrived_high)
    high_pieces = (1, groups - 1) if groups > 1 else (1,)
    forward_high = filter_forward(pick, arrived_high, tables, params, one, two, 1, high_pieces)
    in_part, in_held = gather_steps(in_part, in_held, in_gather[3:4], forward_low[0])
    in_work = gather_steps(in_part, in_held, in_gather[4:])[0].reshape(width, hidden)
    out_part, out_held = gather_steps(
        out_part, out_held, out_gather[3:4], forward_high[0]
    )
    out_work = gather_steps(out_part, out_held, out_gather[4:])[0].reshape(hidden, width)
    last = returned_low
    returned_high = []
    for piece in range(len(high_pieces)):
        last = exchange(forward_high[piece], last)
        returned_high.append(last)
    kept = []
    grad_arrived = []
    dense_rows = 0.0
    in_bias_grad = 0.0
    for group in range(groups):
        piece = min(group, 1)
        *kept, sent_piece, bias_piece, rows_piece = dense(
            kept,
            tokens,
            cotangent,
            returned_low,
            returned_high[piece],
            (group, group - piece),
            lon_back,
            lon_table,
            params,
            in_bias,
            in_work,
            out_work,
            group,
        )
        in_bias_grad = in_bias_grad + bias_piece
        dense_rows = dense_rows + rows_piece
        before_last = last
        last = exchange(sent_piece, last)
        grad_arrived.append(last)
    result, mixed_grad, second, grad_low, act, grad_pre = kept
    act, grad_pre = in_turn((act, grad_pre), before_last)
    in_picks, out_picks = picks(IN_ORDER), picks(OUT_ORDER)
    out_part, in_part = in_turn(
        (
            out_weight_grad(out_picks[0], act, grad_low),
            in_weight_grad(in_picks[0], second, grad_pre),
        ),
        last,
    )
    out_part = scatter_steps(*out_part, OUT_ORDER, out_picks, 0, 1)
    in_part = scatter_steps(*in_part, IN_ORDER, in_picks, 0, 1)

    backward = []
    grad_returned = []
    for q, (normed, forward) in enumerate(
        ((arrived_low, forward_low), (arrived_high, forward_high))
    ):
        if q == 1:
            grad_arrived = in_turn(grad_arrived, (in_part, out_part))
        backward.append(
            filter_backward(pick, grad_arrived, tables, one, two, normed, *forward[-3:], q)
        )
        if q == 1:
            out_part = scatter_steps(*out_part, OUT_ORDER, out_picks, 1, 2)
            in_part = scatter_steps(*in_part, IN_ORDER, in_picks, 1, 2)
            last = (last, out_part, in_part)
            second_half = last
        last = exchange(backward[q][0], last)
        grad_returned.append(last)

    out_part = scatter_steps(*out_part, OUT_ORDER, out_picks, 2, 3)
    in_part = scatter_steps(*in_part, IN_ORDER, in_picks, 2, 3)
    out_part = scatter_steps(*out_part, OUT_ORDER, out_picks, 3, 4)
    in_part = scatter_steps(*in_part, IN_ORDER, in_picks, 3, 4)
    out_part, in_part = in_turn((out_part, in_part), last)
    out_grad = scatter_last(*out_part, OUT_ORDER)
    in_grad = scatter_last(*in_part, IN_ORDER)

    pieces = []
    for q in range(2):
        one_grad, two_grad = in_turn((backward[q][1], backward[q][2]), second_half)
        pieces.append(
            jnp.concatenate(
                [
                    own_blocks(one_grad[:, :HALF], block),
                    own_blocks(one_grad[:, HALF:], block),
                    own_blocks(two_grad[:HALF], block),
                    own_blocks(two_grad[HALF:], block),
                ],
                axis=1,
            )
        )
    filter_local = jnp.concatenate(pieces, axis=0).reshape(devices, filter_rows, 4 * block)
    bias_rows = jnp.concatenate([backward[0][3], backward[1][3]], axis=1)
    small_rows = jnp.concatenate(
        [
            dense_rows[3:5] + bias_rows[4:6],
            dense_rows[0:2],
            bias_rows[0:2],
            bias_rows[2:3] + bias_rows[2:3],
            bias_rows[3:4] - bias_rows[3:4],
            dense_rows[2:3],
            in_bias_grad.reshape(4, width),
        ],
        axis=0,
    )

    def shares(rows):
        flat = rows.reshape(-1)
        flat = jnp.pad(flat, (0, devices * small_share - flat.shape[0]))
        return jnp.pad(flat.reshape(devices, small_share), ((0, 0), (0, 4 * block - small_share)))

    early = scatter_small(
        jnp.concatenate([filter_local, shares(small_rows)[:, None]], axis=1), last
    )
    filter_grad = early[:filter_rows]
    small_grad = early[filter_rows, :small_share]

    input_grad = gather_grad(
        tokens,
        mixed_grad,
        grad_returned[0],
        grad_returned[1],
        lon_back,
        params,
    )

    filter_new, filter_m_new, filter_v_new, filter_ema_new = adam_update(
        filter_master, filter_grad, filter_m, filter_v, filter_ema, 0.2
    )
    in_new, in_m_new, in_v_new, in_ema_new = adam_update(
        in_master, in_grad, in_m, in_v, in_ema, 0.1
    )
    out_new, out_m_new, out_v_new, out_ema_new = adam_update(
        out_master, out_grad, out_m, out_v, out_ema, 0.05
    )
    small_new, small_m_new, small_v_new, small_ema_new = adam_update(
        small_master, small_grad, small_m, small_v, small_ema, 0.5
    )
    return (
        result,
        input_grad,
        filter_grad,
        in_grad,
        out_grad,
        small_grad,
        filter_new,
        in_new,
        out_new,
        small_new,
        filter_m_new,
        filter_v_new,
        in_m_new,
        in_v_new,
        out_m_new,
        out_v_new,
        small_m_new,
        small_v_new,
        filter_ema_new,
        in_ema_new,
        out_ema_new,
        small_ema_new,
    )


def solution(mesh):
    sizes = (mesh.shape["samp"], mesh.shape["sp"])
    samp = "samp"
    body = plain_shards
    if fits(sizes):
        samp = ("y", "core")
        mesh = Mesh(mesh.devices.reshape(2, 2, sizes[1]), AXES)
        body = functools.partial(fast_shards, sizes)
    every = (*samp, "sp") if isinstance(samp, tuple) else (samp, "sp")
    return jax.shard_map(
        body,
        mesh=mesh,
        in_specs=(
            P(samp, "sp", None, None),
            P(samp, "sp", None, None),
            P(samp),
            P(every, None),
            P(every, None),
            P(every, None),
            P(every),
            P(every, None),
            P(every, None),
            P(every, None),
            P(every, None),
            P(every, None),
            P(every, None),
            P(every),
            P(every),
            P(every, None),
            P(every, None),
            P(every, None),
            P(every),
        ),
        out_specs=(
            P(samp, "sp", None, None),
            P(samp, "sp", None, None),
            P(every, None),
            P(every, None),
            P(every, None),
            P(every),
            P(every, None),
            P(every, None),
            P(every, None),
            P(every),
            P(every, None),
            P(every, None),
            P(every, None),
            P(every, None),
            P(every, None),
            P(every, None),
            P(every),
            P(every),
            P(every, None),
            P(every, None),
            P(every, None),
            P(every),
        ),
        check_vma=False,
    )
```

```python
import functools
import math

import jax
import jax.numpy as jnp
import numpy as np
from jax import lax
from jax.experimental import pallas as pl
from jax.experimental.pallas import tpu as pltpu
from jax.sharding import Mesh
from jax.sharding import PartitionSpec as P

NB = 8
STEP = 10


HIGHEST = lax.Precision.HIGHEST
NORM_EPS = 1e-05
BETA_ONE = 0.9
BETA_TWO = 0.95
ADAM_EPS = 1e-08
DECAY = 0.05
EMA_KEEP = 0.75


def gelu_exact(values):
    return jax.nn.gelu(values, approximate=False)


def norm_forward(values):
    center = values - jnp.mean(values, axis=-1, keepdims=True)
    inv_std = lax.rsqrt(jnp.mean(center * center, axis=-1, keepdims=True) + NORM_EPS)
    return (center * inv_std, inv_std)


def norm_back(upstream, normed, inv_std, gain):
    scaled = upstream * gain
    first_mean = jnp.mean(scaled, axis=-1, keepdims=True)
    second_mean = jnp.mean(scaled * normed, axis=-1, keepdims=True)
    leading = tuple(range(upstream.ndim - 1))
    input_part = inv_std * (scaled - first_mean - normed * second_mean)
    return (input_part, jnp.sum(upstream * normed, axis=leading), jnp.sum(upstream, axis=leading))


def dft_table(points):
    positions = jnp.arange(points, dtype=jnp.int32)
    phases = positions[:, None] * positions[None, :] % points
    angles = phases.astype(jnp.float32) * (2.0 * math.pi / points)
    factor = 1.0 / math.sqrt(points)
    return (jnp.cos(angles) * factor, jnp.sin(angles) * factor)


def lat_table(cosine, sine_part, sign_value):
    upper_rows = jnp.stack([cosine, -sign_value * sine_part], axis=-1)
    lower_rows = jnp.stack([sign_value * sine_part, cosine], axis=-1)
    return jnp.stack([upper_rows, lower_rows], axis=1)


def split_table(table):
    upper_part = table.astype(jnp.bfloat16)
    lower_part = (table - upper_part.astype(jnp.float32)).astype(jnp.bfloat16)
    return (upper_part, lower_part)


def table_first(form, table, values):
    upper_part, lower_part = split_table(table)
    return jnp.einsum(form, upper_part, values, preferred_element_type=jnp.float32) + jnp.einsum(
        form, lower_part, values, preferred_element_type=jnp.float32
    )


def table_second(form, values, table):
    upper_part, lower_part = split_table(table)
    return jnp.einsum(form, values, upper_part, preferred_element_type=jnp.float32) + jnp.einsum(
        form, values, lower_part, preferred_element_type=jnp.float32
    )


def complex_mix(inputs, weight):
    shape_in = inputs.shape
    size_block = weight.shape[1] // 2
    grouped = inputs.reshape(shape_in[:4] + (NB, size_block))
    matrices = weight.reshape(NB, size_block, 2, size_block)
    product = jnp.einsum(
        "sgckbi,bieo->sgcekbo", grouped, matrices, preferred_element_type=jnp.float32
    )
    real_part = product[:, :, 0, 0] - product[:, :, 1, 1]
    imag_part = product[:, :, 1, 0] + product[:, :, 0, 1]
    return jnp.stack([real_part, imag_part], axis=2).reshape(shape_in)


def mix_back(upstream, inputs, weight):
    shape_in = inputs.shape
    size_block = weight.shape[1] // 2
    grouped = inputs.reshape(shape_in[:4] + (NB, size_block))
    upstream_grouped = upstream.reshape(shape_in[:4] + (NB, size_block))
    matrices = weight.reshape(NB, size_block, 2, size_block)
    toward = jnp.einsum(
        "sgekbo,bico->sgeckbi", upstream_grouped, matrices, preferred_element_type=jnp.float32
    )
    grad_real = toward[:, :, 0, 0] + toward[:, :, 1, 1]
    grad_imag = toward[:, :, 1, 0] - toward[:, :, 0, 1]
    grad_inputs = jnp.stack([grad_real, grad_imag], axis=2).reshape(shape_in)
    outer_sums = jnp.einsum(
        "sgckbi,sgekbo->cebio", grouped, upstream_grouped, preferred_element_type=jnp.float32
    )
    weight_real = outer_sums[0, 0] + outer_sums[1, 1]
    weight_imag = outer_sums[0, 1] - outer_sums[1, 0]
    weight_grad = jnp.stack([weight_real, weight_imag], axis=2).reshape(weight.shape)
    bias_grad = jnp.sum(upstream, axis=(0, 1, 3), dtype=jnp.float32)
    return (grad_inputs, weight_grad, bias_grad)


def adam_update(master, gradient, moment, second, average, step_rate):
    moment_new = BETA_ONE * moment + (1.0 - BETA_ONE) * gradient
    second_new = BETA_TWO * second + (1.0 - BETA_TWO) * gradient * gradient
    scaled_moment = moment_new / (1.0 - BETA_ONE**STEP)
    scaled_second = second_new / (1.0 - BETA_TWO**STEP)
    master_new = master - step_rate * (
        scaled_moment / (jnp.sqrt(scaled_second) + ADAM_EPS) + DECAY * master
    )
    average_new = EMA_KEEP * average + (1.0 - EMA_KEEP) * master_new
    return (master_new, moment_new, second_new, average_new)


def plain_shards(
    tokens,
    cotangent,
    storm_weight,
    filter_master,
    in_master,
    out_master,
    small_master,
    filter_m,
    filter_v,
    in_m,
    in_v,
    out_m,
    out_v,
    small_m,
    small_v,
    filter_ema,
    in_ema,
    out_ema,
    small_ema,
):
    filter_work, small_work = (
        lax.all_gather(filter_master.astype(jnp.bfloat16), ("samp", "sp"), axis=0, tiled=True),
        lax.all_gather(small_master.astype(jnp.bfloat16), ("samp", "sp"), axis=0, tiled=True),
    )
    width = filter_work.shape[0]
    size_block = width // NB
    params = small_work.astype(jnp.float32).reshape(13, width)
    inputs = tokens.astype(jnp.float32)
    normed_one, inv_one = norm_forward(inputs)
    first = normed_one * params[0] + params[1]
    lon_cos, lon_sin = dft_table(tokens.shape[2])
    lon_forward = jnp.stack([lon_cos, -lon_sin], axis=1)
    lon_inverse = jnp.stack([lon_cos, -lon_sin], axis=0)
    spectrum = jnp.einsum("shwd,wck->shckd", first, lon_forward, precision=HIGHEST).astype(
        jnp.bfloat16
    )
    arrived = lax.all_to_all(spectrum, "sp", split_axis=3, concat_axis=1, tiled=True)
    lat_cos, lat_sin = dft_table(arrived.shape[1])
    lat_forward = lat_table(lat_cos, lat_sin, -1.0)
    lat_inverse = lat_table(lat_cos, lat_sin, 1.0)
    modes = table_first("gohc,shckd->sgokd", lat_forward, arrived).astype(jnp.bfloat16)
    bias_one = params[4:6][:, None, :]
    bias_two = params[6:8][:, None, :]
    pre_one = complex_mix(modes, filter_work[:, : 2 * size_block]) + bias_one
    hidden_one = gelu_exact(pre_one).astype(jnp.bfloat16)
    pre_two = complex_mix(hidden_one, filter_work[:, 2 * size_block :]) + bias_two
    leaving = jnp.einsum("gohc,shckd->sgokd", lat_inverse, pre_two, precision=HIGHEST).astype(
        jnp.bfloat16
    )
    returned = lax.all_to_all(leaving, "sp", split_axis=1, concat_axis=3, tiled=True)
    spatial = table_second("shckd,ckw->shwd", returned, lon_inverse)
    mixed = spatial + first + inputs
    in_work, out_work = (
        lax.all_gather(in_master.astype(jnp.bfloat16), ("samp", "sp"), axis=0, tiled=True),
        lax.all_gather(out_master.astype(jnp.bfloat16), ("samp", "sp"), axis=0, tiled=True),
    )
    normed_two, inv_two = norm_forward(mixed)
    second = (normed_two * params[2] + params[3]).astype(jnp.bfloat16).reshape(-1, width)
    pre_dense = jnp.dot(second, in_work, preferred_element_type=jnp.float32) + params[9:13].reshape(
        -1
    )
    act_dense = gelu_exact(pre_dense).astype(jnp.bfloat16)
    branch = jnp.dot(act_dense, out_work, preferred_element_type=jnp.float32) + params[8]
    result = (mixed + branch.reshape(mixed.shape)).astype(jnp.bfloat16)
    filter_back = lax.all_gather(
        filter_master.astype(jnp.bfloat16), ("samp", "sp"), axis=0, tiled=True
    )
    in_back, out_back = (
        lax.all_gather(in_master.astype(jnp.bfloat16), ("samp", "sp"), axis=0, tiled=True),
        lax.all_gather(out_master.astype(jnp.bfloat16), ("samp", "sp"), axis=0, tiled=True),
    )
    sample_scale = storm_weight.astype(jnp.float32)[:, None, None, None] / 64.0
    grad_out = cotangent.astype(jnp.float32) * sample_scale
    grad_low = grad_out.astype(jnp.bfloat16).reshape(-1, width)
    out_local = jnp.einsum("tf,td->fd", act_dense, grad_low, preferred_element_type=jnp.float32)
    out_bias_grad = jnp.sum(grad_low, axis=0, dtype=jnp.float32)
    grad_act = jnp.einsum("td,fd->tf", grad_low, out_back, preferred_element_type=jnp.float32)
    dense_values, dense_pull = jax.vjp(gelu_exact, pre_dense)
    grad_pre = dense_pull(grad_act)[0].astype(jnp.bfloat16)
    in_local = jnp.einsum("td,tf->df", second, grad_pre, preferred_element_type=jnp.float32)
    in_bias_grad = jnp.sum(grad_pre, axis=0, dtype=jnp.float32)
    grad_second = jnp.einsum(
        "tf,df->td", grad_pre, in_back, preferred_element_type=jnp.float32
    ).reshape(mixed.shape)
    grad_norm_two, gain_two_grad, shift_two_grad = norm_back(
        grad_second, normed_two, inv_two, params[2]
    )
    grad_mixed = grad_out + grad_norm_two
    grad_leaving = jnp.einsum("shwd,ckw->shckd", grad_mixed, lon_inverse, precision=HIGHEST).astype(
        jnp.bfloat16
    )
    grad_arrived = lax.all_to_all(grad_leaving, "sp", split_axis=3, concat_axis=1, tiled=True)
    grad_pre_two = table_first("gohc,sgokd->shckd", lat_inverse, grad_arrived).astype(jnp.bfloat16)
    grad_hidden, weight_two_grad, bias_two_grad = mix_back(
        grad_pre_two, hidden_one, filter_back[:, 2 * size_block :]
    )
    gelu_values, gelu_pull = jax.vjp(gelu_exact, pre_one)
    grad_pre_one = gelu_pull(grad_hidden)[0].astype(jnp.bfloat16)
    grad_modes, weight_one_grad, bias_one_grad = mix_back(
        grad_pre_one, modes, filter_back[:, : 2 * size_block]
    )
    grad_spectrum = jnp.einsum(
        "gohc,sgokd->shckd", lat_forward, grad_modes, precision=HIGHEST
    ).astype(jnp.bfloat16)
    grad_sent = lax.all_to_all(grad_spectrum, "sp", split_axis=1, concat_axis=3, tiled=True)
    grad_first = grad_mixed + table_second("shckd,wck->shwd", grad_sent, lon_forward)
    grad_norm_one, gain_one_grad, shift_one_grad = norm_back(
        grad_first, normed_one, inv_one, params[0]
    )
    input_grad = grad_mixed + grad_norm_one
    norm_rows = jnp.stack([gain_one_grad, shift_one_grad, gain_two_grad, shift_two_grad])
    small_local = jnp.concatenate(
        [
            norm_rows,
            bias_one_grad,
            bias_two_grad,
            out_bias_grad[None, :],
            in_bias_grad.reshape(-1, width),
        ],
        axis=0,
    ).reshape(-1)
    filter_local = jnp.concatenate([weight_one_grad, weight_two_grad], axis=1)
    filter_grad, in_grad, out_grad, small_grad = (
        lax.psum_scatter(filter_local, ("samp", "sp"), scatter_dimension=0, tiled=True),
        lax.psum_scatter(in_local, ("samp", "sp"), scatter_dimension=0, tiled=True),
        lax.psum_scatter(out_local, ("samp", "sp"), scatter_dimension=0, tiled=True),
        lax.psum_scatter(small_local, ("samp", "sp"), scatter_dimension=0, tiled=True),
    )
    filter_new, filter_m_new, filter_v_new, filter_ema_new = adam_update(
        filter_master, filter_grad, filter_m, filter_v, filter_ema, 0.2
    )
    in_new, in_m_new, in_v_new, in_ema_new = adam_update(
        in_master, in_grad, in_m, in_v, in_ema, 0.1
    )
    out_new, out_m_new, out_v_new, out_ema_new = adam_update(
        out_master, out_grad, out_m, out_v, out_ema, 0.05
    )
    small_new, small_m_new, small_v_new, small_ema_new = adam_update(
        small_master, small_grad, small_m, small_v, small_ema, 0.5
    )
    return (
        result,
        input_grad,
        filter_grad,
        in_grad,
        out_grad,
        small_grad,
        filter_new,
        in_new,
        out_new,
        small_new,
        filter_m_new,
        filter_v_new,
        in_m_new,
        in_v_new,
        out_m_new,
        out_v_new,
        small_m_new,
        small_v_new,
        filter_ema_new,
        in_ema_new,
        out_ema_new,
        small_ema_new,
    )


F32 = jnp.float32
BF16 = jnp.bfloat16
LAT = 96
LON = 160
GROUP = 4
HALF = 384
ROWS = 208
FCHUNK = 512
VMEM_BYTES = 56 * 1024 * 1024
SCHED = pltpu.CompilerParams(vmem_limit_bytes=VMEM_BYTES)


def fits(sizes):
    parts = sizes[1]
    return sizes == (4, 8) and LAT % (parts * GROUP) == 0 and LON // 2 % (2 * parts) == 0


def cost(time_us, bytes_moved):
    return pl.CostEstimate(
        flops=int(time_us * 1.15e9), bytes_accessed=bytes_moved, transcendentals=0
    )


def dot(left, right, left_dim, right_dim):
    return lax.dot_general(
        left, right, (((left_dim,), (right_dim,)), ((), ())), preferred_element_type=F32
    )


def gelu_pair(values):
    cdf = 0.5 + 0.5 * lax.erf(values * math.sqrt(0.5))
    pdf = jnp.exp2(values * values * (-0.5 * math.log2(math.e))) * (1.0 / math.sqrt(2.0 * math.pi))
    return (values * cdf, cdf + values * pdf)


@functools.lru_cache(maxsize=None)
def lon_matrix():
    slots = LON // 2
    points = np.arange(LON)
    table = np.zeros((slots, 2, LON))
    for slot in range(slots):
        angles = 2.0 * np.pi * (slot * points % LON) / LON
        table[slot, 0] = np.cos(angles)
        table[slot, 1] = -np.sin(angles)
    table[0, 1] = np.where(points % 2 == 0, 1.0, -1.0)
    table /= np.sqrt(LON)
    full = np.zeros((slots, 2, GROUP, GROUP, LON))
    for row in range(GROUP):
        full[:, :, row, row, :] = table
    return full.reshape(slots * 2 * GROUP, GROUP * LON)


@functools.lru_cache(maxsize=None)
def lat_matrices(parts):
    per_part = LAT // parts
    groups = per_part // GROUP
    forward = np.zeros((2, 2, ROWS, LAT, 2, 2))
    share = np.zeros((2, ROWS))
    lat = np.arange(LAT)

    def put_plain(variant, start, slot):
        for mode in range(LAT):
            angles = 2.0 * np.pi * (mode * lat % LAT) / LAT
            forward[variant, 0, start + mode, :, slot, 0] = np.cos(angles)
            forward[variant, 0, start + mode, :, slot, 1] = np.sin(angles)
            forward[variant, 1, start + mode, :, slot, 0] = -np.sin(angles)
            forward[variant, 1, start + mode, :, slot, 1] = np.cos(angles)
            share[variant, start + mode] = 1.0

    half = LAT // 2 + 1
    for column in range(2):
        for mode in range(half):
            angles = 2.0 * np.pi * (mode * lat % LAT) / LAT
            row = column * half + mode
            own = mode in (0, LAT // 2)
            forward[0, 0, row, :, 0, column] = np.cos(angles)
            forward[0, 1, row, :, 0, column] = 0.0 if own else -np.sin(angles)
            share[0, row] = 0.5 if own else 1.0
    put_plain(0, 2 * half, 1)
    put_plain(1, 0, 0)
    put_plain(1, LAT, 1)
    forward /= np.sqrt(LAT)
    forward = forward.reshape(2, 2, ROWS, parts, groups, GROUP, 2, 2)
    forward = forward.transpose(0, 1, 2, 3, 4, 6, 7, 5)
    shift_row = np.zeros((2, ROWS, 128))
    shift_row[0, 0] = np.sqrt(LAT * LON)
    return (forward, share, shift_row)


def lat_tables(parts):
    forward, share, shift_row = lat_matrices(parts)
    tall = 2 * ROWS
    wide = forward[0].size // tall
    by_part = forward.reshape(2, tall, wide)
    by_group = forward.transpose(0, 1, 2, 4, 3, 5, 6, 7).reshape(2, tall, wide)
    weights = np.concatenate([share, share], axis=1)[:, :, None]
    tables = (
        by_part,
        (weights * by_group).transpose(0, 2, 1),
        weights * by_group,
        by_part.transpose(0, 2, 1),
    )
    return tuple(jnp.asarray(table, BF16) for table in tables) + (jnp.asarray(shift_row, F32),)


def normalise(values):
    center = values - jnp.mean(values, axis=-1, keepdims=True)
    inv_std = lax.rsqrt(jnp.mean(center * center, axis=-1, keepdims=True) + NORM_EPS)
    return (center * inv_std, inv_std)


def spread_body(tokens_ref, table_ref, filter_ref, small_ref, low_ref, high_ref):
    step = pl.program_id(0)
    values = tokens_ref[...].astype(F32).reshape(GROUP * LON, 2 * HALF)
    normed, _ = normalise(values)
    out = dot(table_ref[...], normed.astype(BF16), 1, 0).astype(BF16)
    pairs = high_ref.shape[1]
    parts = high_ref.shape[0]
    units = low_ref.shape[1]
    low_ref[:, pl.ds(step * pairs, pairs)] = out[:, :HALF].reshape(parts, pairs, 16, HALF)
    high_ref[...] = out[:, HALF:].reshape(parts, pairs, 16, HALF)

    @pl.when(step == 0)
    def _():
        rows = filter_ref.shape[0]
        extra = units - pl.num_programs(0) * pairs
        spare = jnp.zeros((16 * extra - rows - 1, HALF), F32)
        own = jnp.concatenate([filter_ref[...], small_ref[...], spare], axis=0).astype(BF16)
        own = own.reshape(1, extra, 16, HALF)
        low_ref[:, units - extra :] = jnp.broadcast_to(own, (parts, extra, 16, HALF))


def spread(tokens, table, filter_rows, small_row, parts):
    groups = tokens.shape[1] // GROUP
    pairs = LON // 4 // parts
    extra = filter_rows.shape[0] // 16 + 1
    low = (parts, groups * pairs + extra, 16, HALF)
    high = (parts, groups * pairs, 16, HALF)

    def whole(*shape):
        return pl.BlockSpec(shape, lambda r: (0,) * len(shape))

    return pl.pallas_call(
        spread_body,
        name="norm_and_longitude",
        grid=(groups,),
        in_specs=[
            pl.BlockSpec((1, GROUP, LON, 2 * HALF), lambda r: (0, r, 0, 0)),
            whole(*table.shape),
            whole(*filter_rows.shape),
            whole(*small_row.shape),
        ],
        out_specs=[
            whole(*low),
            pl.BlockSpec((parts, pairs, 16, HALF), lambda r: (0, r, 0, 0)),
        ],
        out_shape=[jax.ShapeDtypeStruct(low, BF16), jax.ShapeDtypeStruct(high, BF16)],
        compiler_params=SCHED,
        cost_estimate=cost(7, 2 * tokens.size),
    )(tokens, table, filter_rows, small_row)


def unit_specs(parts, groups, pairs):
    return [
        pl.BlockSpec((parts, 1, 16, HALF), lambda b, pick_ref, r=r: (0, r * pairs + b, 0, 0))
        for r in range(groups)
    ]


def stacked(refs):
    return jnp.concatenate([ref[...] for ref in refs], axis=1).reshape(-1, HALF)


def filter_body(
    pieces,
    pick_ref,
    *refs,
):
    arrived_refs = refs[: sum(pieces)]
    forward_ref, inverse_ref, shift_row_ref, params_ref, one_ref, two_ref, *outs = refs[
        sum(pieces) :
    ]
    back_refs = outs[:-3]
    modes_ref, sums_ref, slopes_ref = outs[-3:]
    columns = forward_ref.shape[-1]
    raw = dot(forward_ref[0], stacked(arrived_refs), 1, 0)
    gain = params_ref[0:1, :]
    shift = params_ref[1:2, :]
    modes_re = (raw[:ROWS] * gain + shift_row_ref[0, :, 0:1] * shift).astype(BF16)
    modes_im = (raw[ROWS:] * gain).astype(BF16)
    modes_ref[0, :ROWS] = modes_re
    modes_ref[0, ROWS:] = modes_im
    from_re = dot(modes_re, one_ref[0], 1, 0)
    from_im = dot(modes_im, one_ref[0], 1, 0)
    bias_re = params_ref[4:5, :]
    bias_im = params_ref[5:6, :]
    re_a = from_re[:, :HALF] + bias_re
    re_b = from_re[:, HALF:] + bias_im
    im_a = from_im[:, :HALF]
    im_b = from_im[:, HALF:]
    plus_re, slope = gelu_pair(re_a - im_b)
    slopes_ref[0, 0] = slope.astype(BF16)
    minus_re, slope = gelu_pair(re_a + im_b)
    slopes_ref[0, 1] = slope.astype(BF16)
    sums_ref[0, 0, :, :HALF] = (plus_re + minus_re).astype(BF16)
    sums_ref[0, 1, :, HALF:] = (plus_re - minus_re).astype(BF16)
    plus_im, slope = gelu_pair(re_b + im_a)
    slopes_ref[0, 2] = slope.astype(BF16)
    minus_im, slope = gelu_pair(re_b - im_a)
    slopes_ref[0, 3] = slope.astype(BF16)
    sums_ref[0, 0, :, HALF:] = (-plus_im - minus_im).astype(BF16)
    sums_ref[0, 1, :, :HALF] = (plus_im - minus_im).astype(BF16)
    two_bias_re = params_ref[6:7, :]
    two_bias_im = params_ref[7:8, :]
    two_re = dot(sums_ref[0, 0], two_ref[0], 1, 0) + (two_bias_re + two_bias_re)
    two_im = dot(sums_ref[0, 1], two_ref[0], 1, 0) + (two_bias_im - two_bias_im)
    both = jnp.concatenate([two_re.astype(BF16), two_im.astype(BF16)], axis=0)
    back = dot(inverse_ref[0], both, 1, 0).astype(BF16)
    step = columns // sum(pieces)
    group = 0
    for ref, count in zip(back_refs, pieces):
        for place in range(count):
            rows = back[group * step : (group + 1) * step]
            ref[:, place] = rows.reshape(-1, 1, 16, HALF)
            group += 1


def filter_forward(pick, arrived, tables, params, one, two, part_of_channels, pieces):
    parts = arrived.shape[0]
    groups = sum(pieces)
    pairs = LON // 4 // parts
    forward, inverse, _, _, shift_row = tables
    q = part_of_channels
    tall = 2 * ROWS

    def chosen(*shape):
        return pl.BlockSpec((1,) + shape, lambda b, pick_ref: (pick_ref[b], 0, 0))

    def fixed(*shape):
        return pl.BlockSpec((1,) + shape, lambda b, pick_ref: (q, 0, 0))

    def stepped(*shape):
        zeros = (0,) * len(shape)
        return pl.BlockSpec((1,) + shape, lambda b, pick_ref: (b,) + zeros)

    back_blocks = [
        pl.BlockSpec((parts, count, 1, 16, HALF), lambda b, pick_ref: (0, 0, b, 0, 0))
        for count in pieces
    ]
    back_shapes = [jax.ShapeDtypeStruct((parts, count, pairs, 16, HALF), BF16) for count in pieces]
    columns = forward.shape[-1]
    return pl.pallas_call(
        functools.partial(filter_body, pieces),
        name="filter_forward",
        grid_spec=pltpu.PrefetchScalarGridSpec(
            num_scalar_prefetch=1,
            grid=(pairs,),
            in_specs=unit_specs(parts, groups, pairs)
            + [
                chosen(tall, columns),
                chosen(columns, tall),
                chosen(ROWS, 128),
                pl.BlockSpec((16, HALF), lambda b, pick_ref: (0, q)),
                fixed(HALF, 2 * HALF),
                fixed(2 * HALF, HALF),
            ],
            out_specs=back_blocks
            + [stepped(tall, HALF), stepped(2, ROWS, 2 * HALF), stepped(4, ROWS, HALF)],
        ),
        out_shape=back_shapes
        + [
            jax.ShapeDtypeStruct((pairs, tall, HALF), BF16),
            jax.ShapeDtypeStruct((pairs, 2, ROWS, 2 * HALF), BF16),
            jax.ShapeDtypeStruct((pairs, 4, ROWS, HALF), BF16),
        ],
        compiler_params=SCHED,
        cost_estimate=cost(14, 12 * 1024 * 1024),
    )(pick, *[arrived] * groups, forward, inverse, shift_row, params, one, two)


def filter_back_body(
    groups,
    pick_ref,
    *refs,
):
    arrived_refs = refs[:groups]
    adjoint_ref, inverse_ref, shift_row_ref, one_ref, two_ref = refs[groups : groups + 5]
    normed_refs = refs[groups + 5 : 2 * groups + 5]
    modes_ref, sums_ref, slopes_ref = refs[2 * groups + 5 : 2 * groups + 8]
    sent_ref, one_grad_ref, two_grad_ref, bias_ref = refs[2 * groups + 8 :]
    columns = adjoint_ref.shape[-1]
    step = columns // groups
    arrived = jnp.concatenate([ref[...].reshape(step, HALF) for ref in arrived_refs], axis=0)
    grad = dot(adjoint_ref[0], arrived, 1, 0)
    grad_re = grad[:ROWS].astype(BF16)
    grad_im = grad[ROWS:].astype(BF16)
    from_re = dot(grad_re, two_ref[0], 1, 1)
    from_im = dot(grad_im, two_ref[0], 1, 1)
    du = from_re[:, :HALF]
    dv = -from_re[:, HALF:]
    dw = from_im[:, :HALF]
    dx = from_im[:, HALF:]
    plus_re = (du + dx) * slopes_ref[0, 0].astype(F32)
    minus_re = (du - dx) * slopes_ref[0, 1].astype(F32)
    plus_im = (dv + dw) * slopes_ref[0, 2].astype(F32)
    minus_im = (dv - dw) * slopes_ref[0, 3].astype(F32)
    re_a = plus_re + minus_re
    im_b = minus_re - plus_re
    im_a = plus_im - minus_im
    re_b = plus_im + minus_im
    out_re = jnp.concatenate([re_a.astype(BF16), re_b.astype(BF16)], axis=1)
    out_im = jnp.concatenate([im_a.astype(BF16), im_b.astype(BF16)], axis=1)
    modes_re = dot(out_re, one_ref[0], 1, 1)
    modes_im = dot(out_im, one_ref[0], 1, 1)
    both = jnp.concatenate([modes_re.astype(BF16), modes_im.astype(BF16)], axis=0)
    sent = dot(inverse_ref[0], both, 1, 0).astype(BF16)
    sent_ref[...] = sent.reshape(sent_ref.shape)
    one_part = dot(modes_ref[0, :ROWS], out_re, 0, 0) + dot(modes_ref[0, ROWS:], out_im, 0, 0)
    two_part = dot(sums_ref[0, 0], grad_re, 0, 0) + dot(sums_ref[0, 1], grad_im, 0, 0)
    gain_part = sent.astype(F32) * stacked(normed_refs).astype(F32)
    shift_part = modes_re * shift_row_ref[0, :, 0:1]
    rows = [
        jnp.sum(part, axis=0, keepdims=True)
        for part in (re_a, re_b, grad[:ROWS], grad[ROWS:], gain_part, shift_part)
    ]
    bias_part = jnp.concatenate(rows + [jnp.zeros((2, HALF), F32)], axis=0)
    first = pl.program_id(0) == 0

    @pl.when(first)
    def _():
        one_grad_ref[...] = one_part
        two_grad_ref[...] = two_part
        bias_ref[...] = bias_part

    @pl.when(jnp.logical_not(first))
    def _():
        one_grad_ref[...] += one_part
        two_grad_ref[...] += two_part
        bias_ref[...] += bias_part


def filter_backward(pick, arrived, tables, one, two, normed, modes, sums, slopes, part_of_channels):
    groups = len(arrived)
    parts, pairs = arrived[0].shape[:2]
    _, _, adjoint, inverse, shift_row = tables
    q = part_of_channels
    tall = 2 * ROWS
    columns = adjoint.shape[-1]

    def chosen(*shape):
        return pl.BlockSpec((1,) + shape, lambda b, pick_ref: (pick_ref[b], 0, 0))

    def fixed(*shape):
        return pl.BlockSpec((1,) + shape, lambda b, pick_ref: (q, 0, 0))

    def stepped(*shape):
        zeros = (0,) * len(shape)
        return pl.BlockSpec((1,) + shape, lambda b, pick_ref: (b,) + zeros)

    def whole(*shape):
        return pl.BlockSpec(shape, lambda b, pick_ref: (0,) * len(shape))

    arrived_block = pl.BlockSpec((parts, 1, 16, HALF), lambda b, pick_ref: (0, b, 0, q))
    return pl.pallas_call(
        functools.partial(filter_back_body, groups),
        name="filter_backward",
        grid_spec=pltpu.PrefetchScalarGridSpec(
            num_scalar_prefetch=1,
            grid=(pairs,),
            in_specs=[arrived_block] * groups
            + [
                chosen(tall, columns),
                chosen(columns, tall),
                chosen(ROWS, 128),
                fixed(HALF, 2 * HALF),
                fixed(2 * HALF, HALF),
            ]
            + unit_specs(parts, groups, pairs)
            + [
                stepped(tall, HALF),
                stepped(2, ROWS, 2 * HALF),
                stepped(4, ROWS, HALF),
            ],
            out_specs=[
                pl.BlockSpec((parts, groups, 1, 16, HALF), lambda b, pick_ref: (0, 0, b, 0, 0)),
                whole(HALF, 2 * HALF),
                whole(2 * HALF, HALF),
                whole(8, HALF),
            ],
        ),
        out_shape=[
            jax.ShapeDtypeStruct((parts, groups, pairs, 16, HALF), BF16),
            jax.ShapeDtypeStruct((HALF, 2 * HALF), F32),
            jax.ShapeDtypeStruct((2 * HALF, HALF), F32),
            jax.ShapeDtypeStruct((8, HALF), F32),
        ],
        compiler_params=SCHED,
        cost_estimate=cost(18, 12 * 1024 * 1024),
    )(pick, *arrived, adjoint, inverse, shift_row, one, two, *[normed] * groups, modes, sums, slopes)


def dense_body(
    tokens_ref,
    cotangent_ref,
    low_ref,
    high_ref,
    inverse_ref,
    table_ref,
    params_ref,
    in_bias_ref,
    in_ref,
    out_ref,
    *refs,
):
    (
        result_ref,
        mixed_grad_ref,
        second_ref,
        grad_low_ref,
        act_ref,
        grad_pre_ref,
        sent_ref,
        in_bias_grad_ref,
        rows_ref,
        branch_ref,
        grad_second_ref,
        normed_two_ref,
        inv_two_ref,
        normed_one_ref,
    ) = refs[-14:]
    chunk = pl.program_id(0)
    count = GROUP * LON
    wide = 2 * HALF

    @pl.when(chunk == 0)
    def _():
        inputs = tokens_ref[...].astype(F32).reshape(count, wide)
        normed, _ = normalise(inputs)
        normed_one_ref[...] = normed.astype(BF16)
        base = normed * params_ref[0:1, :] + params_ref[1:2, :] + inputs
        arrived = jnp.concatenate(
            [low_ref[...].reshape(count, HALF), high_ref[...].reshape(count, HALF)], axis=1
        )
        mixed = dot(inverse_ref[...], arrived, 1, 0) + base
        branch_ref[...] = mixed + params_ref[8:9, :]
        normed_two, inv_two = normalise(mixed)
        normed_two_ref[...] = normed_two
        inv_two_ref[...] = jnp.broadcast_to(inv_two, inv_two_ref.shape)
        second_ref[...] = (normed_two * params_ref[2:3, :] + params_ref[3:4, :]).astype(BF16)
        grad_low_ref[...] = (
            cotangent_ref[...].astype(F32).reshape(count, wide) * params_ref[13:14, :]
        ).astype(BF16)
        grad_second_ref[...] = jnp.zeros_like(grad_second_ref)

    pre = dot(second_ref[...], in_ref[...], 1, 0) + in_bias_ref[...]
    grad_act = dot(grad_low_ref[...], out_ref[...], 1, 1)
    act, slope = gelu_pair(pre)
    act = act.astype(BF16)
    grad_pre = grad_act * slope
    in_bias_grad_ref[...] = jnp.sum(grad_pre, axis=0, keepdims=True)
    grad_pre = grad_pre.astype(BF16)
    act_ref[...] = act
    grad_pre_ref[...] = grad_pre
    branch_ref[...] += dot(act, out_ref[...], 1, 0)
    grad_second_ref[...] += dot(grad_pre, in_ref[...], 1, 1)

    @pl.when(chunk == pl.num_programs(0) - 1)
    def _():
        result_ref[...] = branch_ref[...].astype(BF16).reshape(result_ref.shape)
        normed_two = normed_two_ref[...]
        inv_two = inv_two_ref[:, 0:1]
        upstream = grad_second_ref[...]
        scaled = upstream * params_ref[2:3, :]
        first_mean = jnp.mean(scaled, axis=-1, keepdims=True)
        second_mean = jnp.mean(scaled * normed_two, axis=-1, keepdims=True)
        grad_out = cotangent_ref[...].astype(F32).reshape(count, wide) * params_ref[13:14, :]
        mixed_grad = grad_out + inv_two * (scaled - first_mean - normed_two * second_mean)
        mixed_grad_ref[...] = mixed_grad.astype(BF16).reshape(mixed_grad_ref.shape)
        rows = [
            jnp.sum(part, axis=0, keepdims=True)
            for part in (upstream * normed_two, upstream, grad_low_ref[...].astype(F32))
        ]
        normed_one = normed_one_ref[...].astype(F32)
        rows += [
            jnp.sum(part, axis=0, keepdims=True) for part in (mixed_grad * normed_one, mixed_grad)
        ]
        rows_ref[...] = jnp.concatenate(rows + [jnp.zeros((3, wide), F32)], axis=0)
        sent = dot(table_ref[...], mixed_grad.astype(BF16), 1, 0).astype(BF16)
        sent_ref[...] = sent.reshape(sent_ref.shape)


def dense(
    kept, tokens, cotangent, low, high, places, inverse, table, params, in_bias, in_work, out_work, group
):
    parts, _, pairs = high.shape[:3]
    groups = tokens.shape[1] // GROUP
    count = GROUP * LON
    wide = 2 * HALF
    hidden = in_work.shape[1]

    def whole(*shape):
        return pl.BlockSpec(shape, lambda f: (0,) * len(shape))

    rows = pl.BlockSpec((1, GROUP, LON, wide), lambda f: (0, group, 0, 0))
    low_spec, high_spec = (
        pl.BlockSpec((parts, 1, pairs, 16, HALF), lambda f, place=place: (0, place, 0, 0, 0))
        for place in places
    )
    token_rows = pl.BlockSpec((count, wide), lambda f: (group, 0))
    hidden_rows = pl.BlockSpec((count, FCHUNK), lambda f: (group, f))
    return pl.pallas_call(
        dense_body,
        name="dense_group",
        grid=(hidden // FCHUNK,),
        in_specs=[
            rows,
            rows,
            low_spec,
            high_spec,
            whole(*inverse.shape),
            whole(*table.shape),
            whole(16, wide),
            pl.BlockSpec((1, FCHUNK), lambda f: (0, f)),
            pl.BlockSpec((wide, FCHUNK), lambda f: (0, f)),
            pl.BlockSpec((FCHUNK, wide), lambda f: (f, 0)),
        ]
        + [pl.BlockSpec(memory_space=pl.ANY)] * len(kept),
        out_specs=[
            rows,
            rows,
            token_rows,
            token_rows,
            hidden_rows,
            hidden_rows,
            whole(parts, pairs, 16, wide),
            pl.BlockSpec((1, FCHUNK), lambda f: (0, f)),
            whole(8, wide),
        ],
        out_shape=[
            jax.ShapeDtypeStruct(tokens.shape, BF16),
            jax.ShapeDtypeStruct(tokens.shape, BF16),
            jax.ShapeDtypeStruct((groups * count, wide), BF16),
            jax.ShapeDtypeStruct((groups * count, wide), BF16),
            jax.ShapeDtypeStruct((groups * count, hidden), BF16),
            jax.ShapeDtypeStruct((groups * count, hidden), BF16),
            jax.ShapeDtypeStruct((parts, pairs, 16, wide), BF16),
            jax.ShapeDtypeStruct((1, hidden), F32),
            jax.ShapeDtypeStruct((8, wide), F32),
        ],
        scratch_shapes=[pltpu.VMEM((count, wide), F32)] * 3
        + [pltpu.VMEM((count, 128), F32), pltpu.VMEM((count, wide), BF16)],
        input_output_aliases={10 + i: i for i in range(len(kept))},
        compiler_params=SCHED,
        cost_estimate=cost(25, 30 * 1024 * 1024),
    )(tokens, cotangent, low, high, inverse, table, params, in_bias, in_work, out_work, *kept)


def gather_grad_body(
    tokens_ref, mixed_grad_ref, low_ref, high_ref, inverse_ref, params_ref, grad_ref
):
    count = GROUP * LON
    wide = 2 * HALF
    mixed_grad = mixed_grad_ref[...].astype(F32).reshape(count, wide)
    low = dot(inverse_ref[...], low_ref[...].reshape(count, HALF), 1, 0)
    high = dot(inverse_ref[...], high_ref[...].reshape(count, HALF), 1, 0)
    upstream = mixed_grad + jnp.concatenate([low, high], axis=1)
    normed, inv_std = normalise(tokens_ref[...].astype(F32).reshape(count, wide))
    scaled = upstream * params_ref[0:1, :]
    first_mean = jnp.mean(scaled, axis=-1, keepdims=True)
    second_mean = jnp.mean(scaled * normed, axis=-1, keepdims=True)
    out = mixed_grad + inv_std * (scaled - first_mean - normed * second_mean)
    grad_ref[...] = out.reshape(grad_ref.shape)


def gather_grad(tokens, mixed_grad, low, high, inverse, params):
    parts, groups, pairs = low.shape[:3]
    wide = 2 * HALF

    def whole(*shape):
        return pl.BlockSpec(shape, lambda r: (0,) * len(shape))

    rows = pl.BlockSpec((1, GROUP, LON, wide), lambda r: (0, r, 0, 0))
    arrived = pl.BlockSpec((parts, 1, pairs, 16, HALF), lambda r: (0, r, 0, 0, 0))
    return pl.pallas_call(
        gather_grad_body,
        name="longitude_and_norm_grad",
        grid=(groups,),
        in_specs=[rows, rows, arrived, arrived, whole(*inverse.shape), whole(16, wide)],
        out_specs=rows,
        out_shape=jax.ShapeDtypeStruct((1, groups * GROUP, LON, wide), F32),
        compiler_params=SCHED,
        cost_estimate=cost(12, 16 * 1024 * 1024),
    )(tokens, mixed_grad, low, high, inverse, params)


def block_matrices(weight):
    size = weight.shape[1] // 4
    places = np.arange(HALF)
    pick = (np.arange(4 * size)[:, None, None] == np.arange(4)[:, None] * size + places % size)
    own = places[:, None] // size == places[None, :] // size
    halves = weight.reshape(2, HALF, 4 * size)

    def spread_columns(form, first):
        full = jnp.einsum(
            form, halves, jnp.asarray(pick[:, first : first + 2], BF16), preferred_element_type=F32
        )
        return full

    one = spread_columns("qrc,cpn->qrpn", 0) * own[:, None, :]
    two = spread_columns("qrc,cpn->qprn", 2) * own
    return (
        one.astype(BF16).reshape(2, HALF, 2 * HALF),
        two.astype(BF16).reshape(2, 2 * HALF, HALF),
    )


def own_blocks(matrix, size):
    count = HALF // size
    return jnp.concatenate(
        [matrix[i * size : (i + 1) * size, i * size : (i + 1) * size] for i in range(count)], axis=0
    )


def in_turn(values, last):
    return lax.optimization_barrier((values, last))[0]


def exchange(values, last=None):
    if last is not None:
        values = in_turn(values, last)
    return lax.all_to_all(values, "sp", split_axis=0, concat_axis=0, tiled=True)


AXES = ("y", "core", "sp")
BITS = (("y", 1), ("core", 1), ("sp", 4), ("sp", 2), ("sp", 1))
SIZES = {"y": 2, "core": 2, "sp": 8}


def swap(values, axis, bit):
    return lax.ppermute(values, axis, [(i, i ^ bit) for i in range(SIZES[axis])])


def mine(axis, bit):
    return (lax.axis_index(axis) // bit) % 2


def gather_bit(values, axis, bit, place=0, last=None):
    other = swap(values, axis, bit)
    if last is not None:
        other = in_turn(other, last)
    low = mine(axis, bit) == 0
    return jnp.stack([jnp.where(low, values, other), jnp.where(low, other, values)], axis=place)


def gather_steps(values, held, order, last=None):
    for axis, bit in order:
        held = sorted([*held, (axis, bit)], key=BITS.index)
        values = gather_bit(values, axis, bit, held.index((axis, bit)), last)
    return values, held


def scatter_small(values, last):
    held = list(BITS)
    values = values.reshape((2,) * len(held) + values.shape[1:])
    for step, (axis, bit) in enumerate(IN_ORDER):
        if step == 3:
            values = in_turn(values, last)
        place = held.index((axis, bit))
        keep = lax.dynamic_index_in_dim(values, mine(axis, bit), place, keepdims=False)
        give = lax.dynamic_index_in_dim(values, 1 - mine(axis, bit), place, keepdims=False)
        values = keep + swap(give, axis, bit)
        held.pop(place)
    return values


SMALL = pl.CostEstimate(flops=1 << 20, bytes_accessed=1 << 20, transcendentals=0)
IN_ORDER = (("core", 1), ("y", 1), ("sp", 1), ("sp", 2), ("sp", 4))
OUT_ORDER = (("core", 1), ("sp", 1), ("y", 1), ("sp", 2), ("sp", 4))


def device_rows(order):
    lists = []
    for core in range(2):
        indices = []
        for count in range(16):
            samp, sp = core, 0
            for place, (axis, bit) in enumerate(order[1:]):
                if count >> (3 - place) & 1:
                    samp, sp = (samp + 2 * bit, sp) if axis == "y" else (samp, sp + bit)
            indices.append(samp * 8 + sp)
        lists.append(indices)
    return lists


def in_weight_grad_body(pick_ref, second_ref, grad_pre_ref, keep_ref, give_ref):
    out = dot(second_ref[...], grad_pre_ref[...], 0, 0)
    rows = out.shape[0] // 32
    halves = [
        jnp.concatenate([out[i * rows : (i + 1) * rows] for i in indices], axis=0).astype(BF16)
        for indices in device_rows(IN_ORDER)
    ]

    @pl.when(pick_ref[0] == 0)
    def _():
        keep_ref[...] = halves[0]
        give_ref[...] = halves[1]

    @pl.when(pick_ref[0] == 1)
    def _():
        keep_ref[...] = halves[1]
        give_ref[...] = halves[0]


def in_weight_grad(core, second, grad_pre):
    tokens, wide = second.shape
    hidden = grad_pre.shape[1]
    step = 512
    half = pl.BlockSpec((wide // 2, step), lambda i, pick_ref: (0, i))
    return pl.pallas_call(
        in_weight_grad_body,
        name="in_weight_grad",
        grid_spec=pltpu.PrefetchScalarGridSpec(
            num_scalar_prefetch=1,
            grid=(hidden // step,),
            in_specs=[
                pl.BlockSpec((tokens, wide), lambda i, pick_ref: (0, 0)),
                pl.BlockSpec((tokens, step), lambda i, pick_ref: (0, i)),
            ],
            out_specs=[half, half],
        ),
        out_shape=[jax.ShapeDtypeStruct((wide // 2, hidden), BF16)] * 2,
        compiler_params=SCHED,
        cost_estimate=SMALL,
    )(core, second, grad_pre)


def out_weight_grad_body(pick_ref, act_ref, grad_low_ref, keep_ref, give_ref):
    out = dot(act_ref[...], grad_low_ref[...], 0, 0)
    rows = out.shape[0] // 8
    out = out.astype(BF16)
    pieces = [
        jnp.concatenate(
            [
                out[(z1 * 4 + z0 * 2 + x) * rows : (z1 * 4 + z0 * 2 + x + 1) * rows]
                for z0 in range(2)
                for z1 in range(2)
            ],
            axis=0,
        )
        for x in range(2)
    ]

    @pl.when(pl.program_id(0) == 0)
    def _():
        for x in range(2):
            keep_ref[x, 0] = pieces[x]

    @pl.when(pl.program_id(0) == 1)
    def _():
        for x in range(2):
            give_ref[x, 0] = pieces[x]


def out_weight_grad(core, act, grad_low):
    tokens, hidden = act.shape
    wide = grad_low.shape[1]
    part = hidden // 4
    shape = (2, 2, part // 2, wide)

    def columns(give, y, pick_ref):
        return (0, y * 2 + (pick_ref[0] + give) % 2)

    keep, give = pl.pallas_call(
        out_weight_grad_body,
        name="out_weight_grad",
        grid_spec=pltpu.PrefetchScalarGridSpec(
            num_scalar_prefetch=1,
            grid=(2, 2),
            in_specs=[
                pl.BlockSpec((tokens, part), columns),
                pl.BlockSpec((tokens, wide), lambda give, y, pick_ref: (0, 0)),
            ],
            out_specs=[
                pl.BlockSpec(
                    (2, 1) + shape[2:], lambda give, y, pick_ref: (0, jnp.maximum(y, give), 0, 0)
                ),
                pl.BlockSpec((2, 1) + shape[2:], lambda give, y, pick_ref: (0, y * give, 0, 0)),
            ],
        ),
        out_shape=[jax.ShapeDtypeStruct(shape, BF16)] * 2,
        compiler_params=SCHED,
        cost_estimate=SMALL,
    )(core, act, grad_low)
    return keep.reshape(-1, wide), give.reshape(-1, wide)


def add_split_body(pick_ref, keep_one, got_one, keep_two, got_two, keep_ref, give_ref):
    keep_ref[...] = (keep_one[...].astype(F32) + got_one[...].astype(F32)).astype(BF16)
    give_ref[...] = (keep_two[...].astype(F32) + got_two[...].astype(F32)).astype(BF16)


def add_split(pick, keep, got):
    rows, columns = keep.shape
    steps = 2 if rows % 64 == 0 else 1
    block = (rows // 2 // steps, columns)
    stays = pl.BlockSpec(block, lambda i, pick_ref: (pick_ref[0] * steps + i, 0))
    goes = pl.BlockSpec(block, lambda i, pick_ref: ((1 - pick_ref[0]) * steps + i, 0))
    out = pl.BlockSpec(block, lambda i, pick_ref: (i, 0))
    return pl.pallas_call(
        add_split_body,
        name="add_split",
        grid_spec=pltpu.PrefetchScalarGridSpec(
            num_scalar_prefetch=1,
            grid=(steps,),
            in_specs=[stays, stays, goes, goes],
            out_specs=[out, out],
        ),
        out_shape=[jax.ShapeDtypeStruct((rows // 2, columns), BF16)] * 2,
        compiler_params=SCHED,
        cost_estimate=SMALL,
    )(pick, keep, got, keep, got)


def picks(order):
    return [mine(axis, bit).astype(jnp.int32).reshape(1) for axis, bit in order]


def scatter_steps(keep, give, order, chosen, first, last):
    for place in range(first, last):
        keep, give = add_split(chosen[place + 1], keep, swap(give, *order[place]))
    return keep, give


def scatter_last(keep, give, order):
    return keep.astype(F32) + swap(give, *order[-1]).astype(F32)


def fast_shards(
    sizes,
    tokens,
    cotangent,
    storm_weight,
    filter_master,
    in_master,
    out_master,
    small_master,
    filter_m,
    filter_v,
    in_m,
    in_v,
    out_m,
    out_v,
    small_m,
    small_v,
    filter_ema,
    in_ema,
    out_ema,
    small_ema,
):
    parts = sizes[1]
    devices = sizes[0] * sizes[1]
    groups = tokens.shape[1] // GROUP
    pairs = LON // 4 // parts
    width = tokens.shape[-1]
    block = width // NB
    small_share = small_master.shape[0]
    sp_index = lax.axis_index("sp")

    lon = lon_matrix()
    lon_table = jnp.asarray(lon, BF16)
    lon_back = jnp.asarray(lon.T, BF16)
    tables = lat_tables(parts)
    pick = jnp.where((sp_index == 0) & (jnp.arange(pairs) == 0), 0, 1).astype(jnp.int32)

    filter_rows = filter_master.shape[0]
    small_row = jnp.pad(small_master, (0, 4 * block - small_share)).reshape(1, -1)
    in_gather, out_gather = IN_ORDER[::-1], IN_ORDER[::-1]
    in_part, in_held = gather_steps(in_master.astype(BF16), [], in_gather[:1])
    out_part, out_held = gather_steps(out_master.astype(BF16), [], out_gather[:1])
    sent = spread(tokens, lon_table, filter_master, small_row, parts)
    arrived_low = exchange(sent[0], (in_part, out_part))
    arrived_high = exchange(sent[1], arrived_low)

    units = groups * pairs
    near = arrived_low[:, units:].reshape(parts, -1, 4 * block)
    packed_all = gather_bit(gather_bit(near, "core", 1), "y", 1)
    packed_all = packed_all.reshape((devices,) + near.shape[1:])
    filter_work = packed_all[:, :filter_rows].reshape(width, 4 * block)
    small_work = packed_all[:, filter_rows, :small_share].reshape(-1)

    in_rows, hidden = in_master.shape
    params = small_work.astype(F32).reshape(13, width)
    scale = storm_weight.astype(F32)[0] / 64.0
    in_bias = params[9:13].reshape(1, -1)
    params = jnp.concatenate(
        [params, jnp.full((1, width), scale, F32), jnp.zeros((2, width), F32)], axis=0
    )
    one, two = block_matrices(filter_work)
    params, in_bias = lax.optimization_barrier((params, in_bias))

    in_part, in_held = gather_steps(in_part, in_held, in_gather[1:2])
    out_part, out_held = gather_steps(out_part, out_held, out_gather[1:2])
    in_part, out_part = in_turn((in_part, out_part), arrived_low)
    forward_low = filter_forward(pick, arrived_low, tables, params, one, two, 0, (groups,))
    in_part, in_held = gather_steps(in_part, in_held, in_gather[2:3], forward_low[0])
    out_part, out_held = gather_steps(out_part, out_held, out_gather[2:3], forward_low[0])
    returned_low = exchange(forward_low[0], arrived_high)
    high_pieces = (1, groups - 1) if groups > 1 else (1,)
    forward_high = filter_forward(pick, arrived_high, tables, params, one, two, 1, high_pieces)
    last = returned_low
    returned_high = []
    for piece in range(len(high_pieces)):
        last = exchange(forward_high[piece], last)
        returned_high.append(last)
    in_part, in_held = gather_steps(in_part, in_held, in_gather[3:4], returned_high[0])
    in_work = gather_steps(in_part, in_held, in_gather[4:])[0].reshape(width, hidden)
    out_part, out_held = gather_steps(out_part, out_held, out_gather[3:4], forward_high[0])
    out_work = gather_steps(out_part, out_held, out_gather[4:])[0].reshape(hidden, width)
    kept = []
    grad_arrived = []
    dense_rows = 0.0
    in_bias_grad = 0.0
    for group in range(groups):
        piece = min(group, 1)
        *kept, sent_piece, bias_piece, rows_piece = dense(
            kept,
            tokens,
            cotangent,
            returned_low,
            returned_high[piece],
            (group, group - piece),
            lon_back,
            lon_table,
            params,
            in_bias,
            in_work,
            out_work,
            group,
        )
        in_bias_grad = in_bias_grad + bias_piece
        dense_rows = dense_rows + rows_piece
        before_last = last
        last = exchange(sent_piece, last)
        grad_arrived.append(last)
    result, mixed_grad, second, grad_low, act, grad_pre = kept
    act, grad_pre = in_turn((act, grad_pre), before_last)
    in_picks, out_picks = picks(IN_ORDER), picks(OUT_ORDER)
    out_part, in_part = in_turn(
        (
            out_weight_grad(out_picks[0], act, grad_low),
            in_weight_grad(in_picks[0], second, grad_pre),
        ),
        last,
    )
    out_part = scatter_steps(*out_part, OUT_ORDER, out_picks, 0, 1)
    in_part = scatter_steps(*in_part, IN_ORDER, in_picks, 0, 1)

    backward = []
    grad_returned = []
    for q, (normed, forward) in enumerate(
        ((arrived_low, forward_low), (arrived_high, forward_high))
    ):
        if q == 1:
            grad_arrived = in_turn(grad_arrived, (in_part, out_part))
        backward.append(
            filter_backward(pick, grad_arrived, tables, one, two, normed, *forward[-3:], q)
        )
        if q == 1:
            out_part = scatter_steps(*out_part, OUT_ORDER, out_picks, 1, 2)
            in_part = scatter_steps(*in_part, IN_ORDER, in_picks, 1, 2)
            last = (last, out_part, in_part)
            second_half = last
        last = exchange(backward[q][0], last)
        grad_returned.append(last)

    out_part = scatter_steps(*out_part, OUT_ORDER, out_picks, 2, 3)
    in_part = scatter_steps(*in_part, IN_ORDER, in_picks, 2, 3)
    out_part = scatter_steps(*out_part, OUT_ORDER, out_picks, 3, 4)
    in_part = scatter_steps(*in_part, IN_ORDER, in_picks, 3, 4)
    out_part, in_part = in_turn((out_part, in_part), last)
    out_grad = scatter_last(*out_part, OUT_ORDER)
    in_grad = scatter_last(*in_part, IN_ORDER)

    pieces = []
    for q in range(2):
        one_grad, two_grad = in_turn((backward[q][1], backward[q][2]), second_half)
        pieces.append(
            jnp.concatenate(
                [
                    own_blocks(one_grad[:, :HALF], block),
                    own_blocks(one_grad[:, HALF:], block),
                    own_blocks(two_grad[:HALF], block),
                    own_blocks(two_grad[HALF:], block),
                ],
                axis=1,
            )
        )
    filter_local = jnp.concatenate(pieces, axis=0).reshape(devices, filter_rows, 4 * block)
    bias_rows = jnp.concatenate([backward[0][3], backward[1][3]], axis=1)
    small_rows = jnp.concatenate(
        [
            dense_rows[3:5] + bias_rows[4:6],
            dense_rows[0:2],
            bias_rows[0:2],
            bias_rows[2:3] + bias_rows[2:3],
            bias_rows[3:4] - bias_rows[3:4],
            dense_rows[2:3],
            in_bias_grad.reshape(4, width),
        ],
        axis=0,
    )

    def shares(rows):
        flat = rows.reshape(-1)
        flat = jnp.pad(flat, (0, devices * small_share - flat.shape[0]))
        return jnp.pad(flat.reshape(devices, small_share), ((0, 0), (0, 4 * block - small_share)))

    early = scatter_small(
        jnp.concatenate([filter_local, shares(small_rows)[:, None]], axis=1), last
    )
    filter_grad = early[:filter_rows]
    small_grad = early[filter_rows, :small_share]

    input_grad = gather_grad(
        tokens,
        mixed_grad,
        grad_returned[0],
        grad_returned[1],
        lon_back,
        params,
    )

    filter_new, filter_m_new, filter_v_new, filter_ema_new = adam_update(
        filter_master, filter_grad, filter_m, filter_v, filter_ema, 0.2
    )
    in_new, in_m_new, in_v_new, in_ema_new = adam_update(
        in_master, in_grad, in_m, in_v, in_ema, 0.1
    )
    out_new, out_m_new, out_v_new, out_ema_new = adam_update(
        out_master, out_grad, out_m, out_v, out_ema, 0.05
    )
    small_new, small_m_new, small_v_new, small_ema_new = adam_update(
        small_master, small_grad, small_m, small_v, small_ema, 0.5
    )
    return (
        result,
        input_grad,
        filter_grad,
        in_grad,
        out_grad,
        small_grad,
        filter_new,
        in_new,
        out_new,
        small_new,
        filter_m_new,
        filter_v_new,
        in_m_new,
        in_v_new,
        out_m_new,
        out_v_new,
        small_m_new,
        small_v_new,
        filter_ema_new,
        in_ema_new,
        out_ema_new,
        small_ema_new,
    )


def solution(mesh):
    sizes = (mesh.shape["samp"], mesh.shape["sp"])
    samp = "samp"
    body = plain_shards
    if fits(sizes):
        samp = ("y", "core")
        mesh = Mesh(mesh.devices.reshape(2, 2, sizes[1]), AXES)
        body = functools.partial(fast_shards, sizes)
    every = (*samp, "sp") if isinstance(samp, tuple) else (samp, "sp")
    return jax.shard_map(
        body,
        mesh=mesh,
        in_specs=(
            P(samp, "sp", None, None),
            P(samp, "sp", None, None),
            P(samp),
            P(every, None),
            P(every, None),
            P(every, None),
            P(every),
            P(every, None),
            P(every, None),
            P(every, None),
            P(every, None),
            P(every, None),
            P(every, None),
            P(every),
            P(every),
            P(every, None),
            P(every, None),
            P(every, None),
            P(every),
        ),
        out_specs=(
            P(samp, "sp", None, None),
            P(samp, "sp", None, None),
            P(every, None),
            P(every, None),
            P(every, None),
            P(every),
            P(every, None),
            P(every, None),
            P(every, None),
            P(every),
            P(every, None),
            P(every, None),
            P(every, None),
            P(every, None),
            P(every, None),
            P(every, None),
            P(every),
            P(every),
            P(every, None),
            P(every, None),
            P(every, None),
            P(every),
        ),
        check_vma=False,
    )
```

```python
import functools
import math

import jax
import jax.numpy as jnp
import numpy as np
from jax import lax
from jax.experimental import pallas as pl
from jax.experimental.pallas import tpu as pltpu
from jax.sharding import Mesh
from jax.sharding import PartitionSpec as P

NB = 8
STEP = 10


HIGHEST = lax.Precision.HIGHEST
NORM_EPS = 1e-05
BETA_ONE = 0.9
BETA_TWO = 0.95
ADAM_EPS = 1e-08
DECAY = 0.05
EMA_KEEP = 0.75


def gelu_exact(values):
    return jax.nn.gelu(values, approximate=False)


def norm_forward(values):
    center = values - jnp.mean(values, axis=-1, keepdims=True)
    inv_std = lax.rsqrt(jnp.mean(center * center, axis=-1, keepdims=True) + NORM_EPS)
    return (center * inv_std, inv_std)


def norm_back(upstream, normed, inv_std, gain):
    scaled = upstream * gain
    first_mean = jnp.mean(scaled, axis=-1, keepdims=True)
    second_mean = jnp.mean(scaled * normed, axis=-1, keepdims=True)
    leading = tuple(range(upstream.ndim - 1))
    input_part = inv_std * (scaled - first_mean - normed * second_mean)
    return (input_part, jnp.sum(upstream * normed, axis=leading), jnp.sum(upstream, axis=leading))


def dft_table(points):
    positions = jnp.arange(points, dtype=jnp.int32)
    phases = positions[:, None] * positions[None, :] % points
    angles = phases.astype(jnp.float32) * (2.0 * math.pi / points)
    factor = 1.0 / math.sqrt(points)
    return (jnp.cos(angles) * factor, jnp.sin(angles) * factor)


def lat_table(cosine, sine_part, sign_value):
    upper_rows = jnp.stack([cosine, -sign_value * sine_part], axis=-1)
    lower_rows = jnp.stack([sign_value * sine_part, cosine], axis=-1)
    return jnp.stack([upper_rows, lower_rows], axis=1)


def split_table(table):
    upper_part = table.astype(jnp.bfloat16)
    lower_part = (table - upper_part.astype(jnp.float32)).astype(jnp.bfloat16)
    return (upper_part, lower_part)


def table_first(form, table, values):
    upper_part, lower_part = split_table(table)
    return jnp.einsum(form, upper_part, values, preferred_element_type=jnp.float32) + jnp.einsum(
        form, lower_part, values, preferred_element_type=jnp.float32
    )


def table_second(form, values, table):
    upper_part, lower_part = split_table(table)
    return jnp.einsum(form, values, upper_part, preferred_element_type=jnp.float32) + jnp.einsum(
        form, values, lower_part, preferred_element_type=jnp.float32
    )


def complex_mix(inputs, weight):
    shape_in = inputs.shape
    size_block = weight.shape[1] // 2
    grouped = inputs.reshape(shape_in[:4] + (NB, size_block))
    matrices = weight.reshape(NB, size_block, 2, size_block)
    product = jnp.einsum(
        "sgckbi,bieo->sgcekbo", grouped, matrices, preferred_element_type=jnp.float32
    )
    real_part = product[:, :, 0, 0] - product[:, :, 1, 1]
    imag_part = product[:, :, 1, 0] + product[:, :, 0, 1]
    return jnp.stack([real_part, imag_part], axis=2).reshape(shape_in)


def mix_back(upstream, inputs, weight):
    shape_in = inputs.shape
    size_block = weight.shape[1] // 2
    grouped = inputs.reshape(shape_in[:4] + (NB, size_block))
    upstream_grouped = upstream.reshape(shape_in[:4] + (NB, size_block))
    matrices = weight.reshape(NB, size_block, 2, size_block)
    toward = jnp.einsum(
        "sgekbo,bico->sgeckbi", upstream_grouped, matrices, preferred_element_type=jnp.float32
    )
    grad_real = toward[:, :, 0, 0] + toward[:, :, 1, 1]
    grad_imag = toward[:, :, 1, 0] - toward[:, :, 0, 1]
    grad_inputs = jnp.stack([grad_real, grad_imag], axis=2).reshape(shape_in)
    outer_sums = jnp.einsum(
        "sgckbi,sgekbo->cebio", grouped, upstream_grouped, preferred_element_type=jnp.float32
    )
    weight_real = outer_sums[0, 0] + outer_sums[1, 1]
    weight_imag = outer_sums[0, 1] - outer_sums[1, 0]
    weight_grad = jnp.stack([weight_real, weight_imag], axis=2).reshape(weight.shape)
    bias_grad = jnp.sum(upstream, axis=(0, 1, 3), dtype=jnp.float32)
    return (grad_inputs, weight_grad, bias_grad)


def adam_update(master, gradient, moment, second, average, step_rate):
    moment_new = BETA_ONE * moment + (1.0 - BETA_ONE) * gradient
    second_new = BETA_TWO * second + (1.0 - BETA_TWO) * gradient * gradient
    scaled_moment = moment_new / (1.0 - BETA_ONE**STEP)
    scaled_second = second_new / (1.0 - BETA_TWO**STEP)
    master_new = master - step_rate * (
        scaled_moment / (jnp.sqrt(scaled_second) + ADAM_EPS) + DECAY * master
    )
    average_new = EMA_KEEP * average + (1.0 - EMA_KEEP) * master_new
    return (master_new, moment_new, second_new, average_new)


def plain_shards(
    tokens,
    cotangent,
    storm_weight,
    filter_master,
    in_master,
    out_master,
    small_master,
    filter_m,
    filter_v,
    in_m,
    in_v,
    out_m,
    out_v,
    small_m,
    small_v,
    filter_ema,
    in_ema,
    out_ema,
    small_ema,
):
    filter_work, small_work = (
        lax.all_gather(filter_master.astype(jnp.bfloat16), ("samp", "sp"), axis=0, tiled=True),
        lax.all_gather(small_master.astype(jnp.bfloat16), ("samp", "sp"), axis=0, tiled=True),
    )
    width = filter_work.shape[0]
    size_block = width // NB
    params = small_work.astype(jnp.float32).reshape(13, width)
    inputs = tokens.astype(jnp.float32)
    normed_one, inv_one = norm_forward(inputs)
    first = normed_one * params[0] + params[1]
    lon_cos, lon_sin = dft_table(tokens.shape[2])
    lon_forward = jnp.stack([lon_cos, -lon_sin], axis=1)
    lon_inverse = jnp.stack([lon_cos, -lon_sin], axis=0)
    spectrum = jnp.einsum("shwd,wck->shckd", first, lon_forward, precision=HIGHEST).astype(
        jnp.bfloat16
    )
    arrived = lax.all_to_all(spectrum, "sp", split_axis=3, concat_axis=1, tiled=True)
    lat_cos, lat_sin = dft_table(arrived.shape[1])
    lat_forward = lat_table(lat_cos, lat_sin, -1.0)
    lat_inverse = lat_table(lat_cos, lat_sin, 1.0)
    modes = table_first("gohc,shckd->sgokd", lat_forward, arrived).astype(jnp.bfloat16)
    bias_one = params[4:6][:, None, :]
    bias_two = params[6:8][:, None, :]
    pre_one = complex_mix(modes, filter_work[:, : 2 * size_block]) + bias_one
    hidden_one = gelu_exact(pre_one).astype(jnp.bfloat16)
    pre_two = complex_mix(hidden_one, filter_work[:, 2 * size_block :]) + bias_two
    leaving = jnp.einsum("gohc,shckd->sgokd", lat_inverse, pre_two, precision=HIGHEST).astype(
        jnp.bfloat16
    )
    returned = lax.all_to_all(leaving, "sp", split_axis=1, concat_axis=3, tiled=True)
    spatial = table_second("shckd,ckw->shwd", returned, lon_inverse)
    mixed = spatial + first + inputs
    in_work, out_work = (
        lax.all_gather(in_master.astype(jnp.bfloat16), ("samp", "sp"), axis=0, tiled=True),
        lax.all_gather(out_master.astype(jnp.bfloat16), ("samp", "sp"), axis=0, tiled=True),
    )
    normed_two, inv_two = norm_forward(mixed)
    second = (normed_two * params[2] + params[3]).astype(jnp.bfloat16).reshape(-1, width)
    pre_dense = jnp.dot(second, in_work, preferred_element_type=jnp.float32) + params[9:13].reshape(
        -1
    )
    act_dense = gelu_exact(pre_dense).astype(jnp.bfloat16)
    branch = jnp.dot(act_dense, out_work, preferred_element_type=jnp.float32) + params[8]
    result = (mixed + branch.reshape(mixed.shape)).astype(jnp.bfloat16)
    filter_back = lax.all_gather(
        filter_master.astype(jnp.bfloat16), ("samp", "sp"), axis=0, tiled=True
    )
    in_back, out_back = (
        lax.all_gather(in_master.astype(jnp.bfloat16), ("samp", "sp"), axis=0, tiled=True),
        lax.all_gather(out_master.astype(jnp.bfloat16), ("samp", "sp"), axis=0, tiled=True),
    )
    sample_scale = storm_weight.astype(jnp.float32)[:, None, None, None] / 64.0
    grad_out = cotangent.astype(jnp.float32) * sample_scale
    grad_low = grad_out.astype(jnp.bfloat16).reshape(-1, width)
    out_local = jnp.einsum("tf,td->fd", act_dense, grad_low, preferred_element_type=jnp.float32)
    out_bias_grad = jnp.sum(grad_low, axis=0, dtype=jnp.float32)
    grad_act = jnp.einsum("td,fd->tf", grad_low, out_back, preferred_element_type=jnp.float32)
    dense_values, dense_pull = jax.vjp(gelu_exact, pre_dense)
    grad_pre = dense_pull(grad_act)[0].astype(jnp.bfloat16)
    in_local = jnp.einsum("td,tf->df", second, grad_pre, preferred_element_type=jnp.float32)
    in_bias_grad = jnp.sum(grad_pre, axis=0, dtype=jnp.float32)
    grad_second = jnp.einsum(
        "tf,df->td", grad_pre, in_back, preferred_element_type=jnp.float32
    ).reshape(mixed.shape)
    grad_norm_two, gain_two_grad, shift_two_grad = norm_back(
        grad_second, normed_two, inv_two, params[2]
    )
    grad_mixed = grad_out + grad_norm_two
    grad_leaving = jnp.einsum("shwd,ckw->shckd", grad_mixed, lon_inverse, precision=HIGHEST).astype(
        jnp.bfloat16
    )
    grad_arrived = lax.all_to_all(grad_leaving, "sp", split_axis=3, concat_axis=1, tiled=True)
    grad_pre_two = table_first("gohc,sgokd->shckd", lat_inverse, grad_arrived).astype(jnp.bfloat16)
    grad_hidden, weight_two_grad, bias_two_grad = mix_back(
        grad_pre_two, hidden_one, filter_back[:, 2 * size_block :]
    )
    gelu_values, gelu_pull = jax.vjp(gelu_exact, pre_one)
    grad_pre_one = gelu_pull(grad_hidden)[0].astype(jnp.bfloat16)
    grad_modes, weight_one_grad, bias_one_grad = mix_back(
        grad_pre_one, modes, filter_back[:, : 2 * size_block]
    )
    grad_spectrum = jnp.einsum(
        "gohc,sgokd->shckd", lat_forward, grad_modes, precision=HIGHEST
    ).astype(jnp.bfloat16)
    grad_sent = lax.all_to_all(grad_spectrum, "sp", split_axis=1, concat_axis=3, tiled=True)
    grad_first = grad_mixed + table_second("shckd,wck->shwd", grad_sent, lon_forward)
    grad_norm_one, gain_one_grad, shift_one_grad = norm_back(
        grad_first, normed_one, inv_one, params[0]
    )
    input_grad = grad_mixed + grad_norm_one
    norm_rows = jnp.stack([gain_one_grad, shift_one_grad, gain_two_grad, shift_two_grad])
    small_local = jnp.concatenate(
        [
            norm_rows,
            bias_one_grad,
            bias_two_grad,
            out_bias_grad[None, :],
            in_bias_grad.reshape(-1, width),
        ],
        axis=0,
    ).reshape(-1)
    filter_local = jnp.concatenate([weight_one_grad, weight_two_grad], axis=1)
    filter_grad, in_grad, out_grad, small_grad = (
        lax.psum_scatter(filter_local, ("samp", "sp"), scatter_dimension=0, tiled=True),
        lax.psum_scatter(in_local, ("samp", "sp"), scatter_dimension=0, tiled=True),
        lax.psum_scatter(out_local, ("samp", "sp"), scatter_dimension=0, tiled=True),
        lax.psum_scatter(small_local, ("samp", "sp"), scatter_dimension=0, tiled=True),
    )
    filter_new, filter_m_new, filter_v_new, filter_ema_new = adam_update(
        filter_master, filter_grad, filter_m, filter_v, filter_ema, 0.2
    )
    in_new, in_m_new, in_v_new, in_ema_new = adam_update(
        in_master, in_grad, in_m, in_v, in_ema, 0.1
    )
    out_new, out_m_new, out_v_new, out_ema_new = adam_update(
        out_master, out_grad, out_m, out_v, out_ema, 0.05
    )
    small_new, small_m_new, small_v_new, small_ema_new = adam_update(
        small_master, small_grad, small_m, small_v, small_ema, 0.5
    )
    return (
        result,
        input_grad,
        filter_grad,
        in_grad,
        out_grad,
        small_grad,
        filter_new,
        in_new,
        out_new,
        small_new,
        filter_m_new,
        filter_v_new,
        in_m_new,
        in_v_new,
        out_m_new,
        out_v_new,
        small_m_new,
        small_v_new,
        filter_ema_new,
        in_ema_new,
        out_ema_new,
        small_ema_new,
    )


F32 = jnp.float32
BF16 = jnp.bfloat16
LAT = 96
LON = 160
GROUP = 4
HALF = 384
ROWS = 208
FCHUNK = 512
VMEM_BYTES = 56 * 1024 * 1024
SCHED = pltpu.CompilerParams(vmem_limit_bytes=VMEM_BYTES)


def fits(sizes):
    parts = sizes[1]
    return sizes == (4, 8) and LAT % (parts * GROUP) == 0 and LON // 2 % (2 * parts) == 0


def cost(time_us, bytes_moved):
    return pl.CostEstimate(
        flops=int(time_us * 1.15e9), bytes_accessed=bytes_moved, transcendentals=0
    )


def dot(left, right, left_dim, right_dim):
    return lax.dot_general(
        left, right, (((left_dim,), (right_dim,)), ((), ())), preferred_element_type=F32
    )


def gelu_pair(values):
    cdf = 0.5 + 0.5 * lax.erf(values * math.sqrt(0.5))
    pdf = jnp.exp2(values * values * (-0.5 * math.log2(math.e))) * (1.0 / math.sqrt(2.0 * math.pi))
    return (values * cdf, cdf + values * pdf)


@functools.lru_cache(maxsize=None)
def lon_matrix():
    slots = LON // 2
    points = np.arange(LON)
    table = np.zeros((slots, 2, LON))
    for slot in range(slots):
        angles = 2.0 * np.pi * (slot * points % LON) / LON
        table[slot, 0] = np.cos(angles)
        table[slot, 1] = -np.sin(angles)
    table[0, 1] = np.where(points % 2 == 0, 1.0, -1.0)
    table /= np.sqrt(LON)
    full = np.zeros((slots, 2, GROUP, GROUP, LON))
    for row in range(GROUP):
        full[:, :, row, row, :] = table
    return full.reshape(slots * 2 * GROUP, GROUP * LON)


@functools.lru_cache(maxsize=None)
def lat_matrices(parts):
    per_part = LAT // parts
    groups = per_part // GROUP
    forward = np.zeros((2, 2, ROWS, LAT, 2, 2))
    share = np.zeros((2, ROWS))
    lat = np.arange(LAT)

    def put_plain(variant, start, slot):
        for mode in range(LAT):
            angles = 2.0 * np.pi * (mode * lat % LAT) / LAT
            forward[variant, 0, start + mode, :, slot, 0] = np.cos(angles)
            forward[variant, 0, start + mode, :, slot, 1] = np.sin(angles)
            forward[variant, 1, start + mode, :, slot, 0] = -np.sin(angles)
            forward[variant, 1, start + mode, :, slot, 1] = np.cos(angles)
            share[variant, start + mode] = 1.0

    half = LAT // 2 + 1
    for column in range(2):
        for mode in range(half):
            angles = 2.0 * np.pi * (mode * lat % LAT) / LAT
            row = column * half + mode
            own = mode in (0, LAT // 2)
            forward[0, 0, row, :, 0, column] = np.cos(angles)
            forward[0, 1, row, :, 0, column] = 0.0 if own else -np.sin(angles)
            share[0, row] = 0.5 if own else 1.0
    put_plain(0, 2 * half, 1)
    put_plain(1, 0, 0)
    put_plain(1, LAT, 1)
    forward /= np.sqrt(LAT)
    forward = forward.reshape(2, 2, ROWS, parts, groups, GROUP, 2, 2)
    forward = forward.transpose(0, 1, 2, 3, 4, 6, 7, 5)
    shift_row = np.zeros((2, ROWS, 128))
    shift_row[0, 0] = np.sqrt(LAT * LON)
    return (forward, share, shift_row)


def lat_tables(parts):
    forward, share, shift_row = lat_matrices(parts)
    tall = 2 * ROWS
    wide = forward[0].size // tall
    by_part = forward.reshape(2, tall, wide)
    by_group = forward.transpose(0, 1, 2, 4, 3, 5, 6, 7).reshape(2, tall, wide)
    weights = np.concatenate([share, share], axis=1)[:, :, None]
    tables = (
        by_part,
        (weights * by_group).transpose(0, 2, 1),
        weights * by_group,
        by_part.transpose(0, 2, 1),
    )
    return tuple(jnp.asarray(table, BF16) for table in tables) + (jnp.asarray(shift_row, F32),)


def normalise(values):
    center = values - jnp.mean(values, axis=-1, keepdims=True)
    inv_std = lax.rsqrt(jnp.mean(center * center, axis=-1, keepdims=True) + NORM_EPS)
    return (center * inv_std, inv_std)


def spread_body(tokens_ref, table_ref, filter_ref, small_ref, low_ref, high_ref):
    step = pl.program_id(0)
    values = tokens_ref[...].astype(F32).reshape(GROUP * LON, 2 * HALF)
    normed, _ = normalise(values)
    out = dot(table_ref[...], normed.astype(BF16), 1, 0).astype(BF16)
    pairs = high_ref.shape[1]
    parts = high_ref.shape[0]
    units = low_ref.shape[1]
    low_ref[:, pl.ds(step * pairs, pairs)] = out[:, :HALF].reshape(parts, pairs, 16, HALF)
    high_ref[...] = out[:, HALF:].reshape(parts, pairs, 16, HALF)

    @pl.when(step == 0)
    def _():
        rows = filter_ref.shape[0]
        extra = units - pl.num_programs(0) * pairs
        spare = jnp.zeros((16 * extra - rows - 1, HALF), F32)
        own = jnp.concatenate([filter_ref[...], small_ref[...], spare], axis=0).astype(BF16)
        own = own.reshape(1, extra, 16, HALF)
        low_ref[:, units - extra :] = jnp.broadcast_to(own, (parts, extra, 16, HALF))


def spread(tokens, table, filter_rows, small_row, parts):
    groups = tokens.shape[1] // GROUP
    pairs = LON // 4 // parts
    extra = filter_rows.shape[0] // 16 + 1
    low = (parts, groups * pairs + extra, 16, HALF)
    high = (parts, groups * pairs, 16, HALF)

    def whole(*shape):
        return pl.BlockSpec(shape, lambda r: (0,) * len(shape))

    return pl.pallas_call(
        spread_body,
        name="norm_and_longitude",
        grid=(groups,),
        in_specs=[
            pl.BlockSpec((1, GROUP, LON, 2 * HALF), lambda r: (0, r, 0, 0)),
            whole(*table.shape),
            whole(*filter_rows.shape),
            whole(*small_row.shape),
        ],
        out_specs=[
            whole(*low),
            pl.BlockSpec((parts, pairs, 16, HALF), lambda r: (0, r, 0, 0)),
        ],
        out_shape=[jax.ShapeDtypeStruct(low, BF16), jax.ShapeDtypeStruct(high, BF16)],
        compiler_params=SCHED,
        cost_estimate=cost(7, 2 * tokens.size),
    )(tokens, table, filter_rows, small_row)


def unit_specs(parts, groups, pairs):
    return [
        pl.BlockSpec((parts, 1, 16, HALF), lambda b, pick_ref, r=r: (0, r * pairs + b, 0, 0))
        for r in range(groups)
    ]


def stacked(refs):
    return jnp.concatenate([ref[...] for ref in refs], axis=1).reshape(-1, HALF)


def filter_body(
    pieces,
    pick_ref,
    *refs,
):
    arrived_refs = refs[: sum(pieces)]
    forward_ref, inverse_ref, shift_row_ref, params_ref, one_ref, two_ref, *outs = refs[
        sum(pieces) :
    ]
    back_refs = outs[:-3]
    modes_ref, sums_ref, slopes_ref = outs[-3:]
    columns = forward_ref.shape[-1]
    raw = dot(forward_ref[0], stacked(arrived_refs), 1, 0)
    gain = params_ref[0:1, :]
    shift = params_ref[1:2, :]
    modes_re = (raw[:ROWS] * gain + shift_row_ref[0, :, 0:1] * shift).astype(BF16)
    modes_im = (raw[ROWS:] * gain).astype(BF16)
    modes_ref[0, :ROWS] = modes_re
    modes_ref[0, ROWS:] = modes_im
    from_re = dot(modes_re, one_ref[0], 1, 0)
    from_im = dot(modes_im, one_ref[0], 1, 0)
    bias_re = params_ref[4:5, :]
    bias_im = params_ref[5:6, :]
    re_a = from_re[:, :HALF] + bias_re
    re_b = from_re[:, HALF:] + bias_im
    im_a = from_im[:, :HALF]
    im_b = from_im[:, HALF:]
    plus_re, slope = gelu_pair(re_a - im_b)
    slopes_ref[0, 0] = slope.astype(BF16)
    minus_re, slope = gelu_pair(re_a + im_b)
    slopes_ref[0, 1] = slope.astype(BF16)
    sums_ref[0, 0, :, :HALF] = (plus_re + minus_re).astype(BF16)
    sums_ref[0, 1, :, HALF:] = (plus_re - minus_re).astype(BF16)
    plus_im, slope = gelu_pair(re_b + im_a)
    slopes_ref[0, 2] = slope.astype(BF16)
    minus_im, slope = gelu_pair(re_b - im_a)
    slopes_ref[0, 3] = slope.astype(BF16)
    sums_ref[0, 0, :, HALF:] = (-plus_im - minus_im).astype(BF16)
    sums_ref[0, 1, :, :HALF] = (plus_im - minus_im).astype(BF16)
    two_bias_re = params_ref[6:7, :]
    two_bias_im = params_ref[7:8, :]
    two_re = dot(sums_ref[0, 0], two_ref[0], 1, 0) + (two_bias_re + two_bias_re)
    two_im = dot(sums_ref[0, 1], two_ref[0], 1, 0) + (two_bias_im - two_bias_im)
    both = jnp.concatenate([two_re.astype(BF16), two_im.astype(BF16)], axis=0)
    back = dot(inverse_ref[0], both, 1, 0).astype(BF16)
    step = columns // sum(pieces)
    group = 0
    for ref, count in zip(back_refs, pieces):
        for place in range(count):
            rows = back[group * step : (group + 1) * step]
            ref[:, place] = rows.reshape(-1, 1, 16, HALF)
            group += 1


def filter_forward(pick, arrived, tables, params, one, two, part_of_channels, pieces):
    parts = arrived.shape[0]
    groups = sum(pieces)
    pairs = LON // 4 // parts
    forward, inverse, _, _, shift_row = tables
    q = part_of_channels
    tall = 2 * ROWS

    def chosen(*shape):
        return pl.BlockSpec((1,) + shape, lambda b, pick_ref: (pick_ref[b], 0, 0))

    def fixed(*shape):
        return pl.BlockSpec((1,) + shape, lambda b, pick_ref: (q, 0, 0))

    def stepped(*shape):
        zeros = (0,) * len(shape)
        return pl.BlockSpec((1,) + shape, lambda b, pick_ref: (b,) + zeros)

    back_blocks = [
        pl.BlockSpec((parts, count, 1, 16, HALF), lambda b, pick_ref: (0, 0, b, 0, 0))
        for count in pieces
    ]
    back_shapes = [jax.ShapeDtypeStruct((parts, count, pairs, 16, HALF), BF16) for count in pieces]
    columns = forward.shape[-1]
    return pl.pallas_call(
        functools.partial(filter_body, pieces),
        name="filter_forward",
        grid_spec=pltpu.PrefetchScalarGridSpec(
            num_scalar_prefetch=1,
            grid=(pairs,),
            in_specs=unit_specs(parts, groups, pairs)
            + [
                chosen(tall, columns),
                chosen(columns, tall),
                chosen(ROWS, 128),
                pl.BlockSpec((16, HALF), lambda b, pick_ref: (0, q)),
                fixed(HALF, 2 * HALF),
                fixed(2 * HALF, HALF),
            ],
            out_specs=back_blocks
            + [stepped(tall, HALF), stepped(2, ROWS, 2 * HALF), stepped(4, ROWS, HALF)],
        ),
        out_shape=back_shapes
        + [
            jax.ShapeDtypeStruct((pairs, tall, HALF), BF16),
            jax.ShapeDtypeStruct((pairs, 2, ROWS, 2 * HALF), BF16),
            jax.ShapeDtypeStruct((pairs, 4, ROWS, HALF), BF16),
        ],
        compiler_params=SCHED,
        cost_estimate=cost(14, 12 * 1024 * 1024),
    )(pick, *[arrived] * groups, forward, inverse, shift_row, params, one, two)


def filter_back_body(
    groups,
    pick_ref,
    *refs,
):
    arrived_refs = refs[:groups]
    adjoint_ref, inverse_ref, shift_row_ref, one_ref, two_ref = refs[groups : groups + 5]
    normed_refs = refs[groups + 5 : 2 * groups + 5]
    modes_ref, sums_ref, slopes_ref = refs[2 * groups + 5 : 2 * groups + 8]
    sent_ref, one_grad_ref, two_grad_ref, bias_ref = refs[2 * groups + 8 :]
    columns = adjoint_ref.shape[-1]
    step = columns // groups
    arrived = jnp.concatenate([ref[...].reshape(step, HALF) for ref in arrived_refs], axis=0)
    grad = dot(adjoint_ref[0], arrived, 1, 0)
    grad_re = grad[:ROWS].astype(BF16)
    grad_im = grad[ROWS:].astype(BF16)
    from_re = dot(grad_re, two_ref[0], 1, 1)
    from_im = dot(grad_im, two_ref[0], 1, 1)
    du = from_re[:, :HALF]
    dv = -from_re[:, HALF:]
    dw = from_im[:, :HALF]
    dx = from_im[:, HALF:]
    plus_re = (du + dx) * slopes_ref[0, 0].astype(F32)
    minus_re = (du - dx) * slopes_ref[0, 1].astype(F32)
    plus_im = (dv + dw) * slopes_ref[0, 2].astype(F32)
    minus_im = (dv - dw) * slopes_ref[0, 3].astype(F32)
    re_a = plus_re + minus_re
    im_b = minus_re - plus_re
    im_a = plus_im - minus_im
    re_b = plus_im + minus_im
    out_re = jnp.concatenate([re_a.astype(BF16), re_b.astype(BF16)], axis=1)
    out_im = jnp.concatenate([im_a.astype(BF16), im_b.astype(BF16)], axis=1)
    modes_re = dot(out_re, one_ref[0], 1, 1)
    modes_im = dot(out_im, one_ref[0], 1, 1)
    both = jnp.concatenate([modes_re.astype(BF16), modes_im.astype(BF16)], axis=0)
    sent = dot(inverse_ref[0], both, 1, 0).astype(BF16)
    sent_ref[...] = sent.reshape(sent_ref.shape)
    one_part = dot(modes_ref[0], jnp.concatenate([out_re, out_im], axis=0), 0, 0)
    sums = sums_ref[...].reshape(2 * ROWS, 2 * HALF)
    two_part = dot(sums, grad.astype(BF16), 0, 0)
    gain_part = sent.astype(F32) * stacked(normed_refs).astype(F32)
    shift_part = modes_re * shift_row_ref[0, :, 0:1]
    rows = [
        jnp.sum(part, axis=0, keepdims=True)
        for part in (re_a, re_b, grad[:ROWS], grad[ROWS:], gain_part, shift_part)
    ]
    bias_part = jnp.concatenate(rows + [jnp.zeros((2, HALF), F32)], axis=0)
    first = pl.program_id(0) == 0

    @pl.when(first)
    def _():
        one_grad_ref[...] = one_part
        two_grad_ref[...] = two_part
        bias_ref[...] = bias_part

    @pl.when(jnp.logical_not(first))
    def _():
        one_grad_ref[...] += one_part
        two_grad_ref[...] += two_part
        bias_ref[...] += bias_part


def filter_backward(pick, arrived, tables, one, two, normed, modes, sums, slopes, part_of_channels):
    groups = len(arrived)
    parts, pairs = arrived[0].shape[:2]
    _, _, adjoint, inverse, shift_row = tables
    q = part_of_channels
    tall = 2 * ROWS
    columns = adjoint.shape[-1]

    def chosen(*shape):
        return pl.BlockSpec((1,) + shape, lambda b, pick_ref: (pick_ref[b], 0, 0))

    def fixed(*shape):
        return pl.BlockSpec((1,) + shape, lambda b, pick_ref: (q, 0, 0))

    def stepped(*shape):
        zeros = (0,) * len(shape)
        return pl.BlockSpec((1,) + shape, lambda b, pick_ref: (b,) + zeros)

    def whole(*shape):
        return pl.BlockSpec(shape, lambda b, pick_ref: (0,) * len(shape))

    arrived_block = pl.BlockSpec((parts, 1, 16, HALF), lambda b, pick_ref: (0, b, 0, q))
    return pl.pallas_call(
        functools.partial(filter_back_body, groups),
        name="filter_backward",
        grid_spec=pltpu.PrefetchScalarGridSpec(
            num_scalar_prefetch=1,
            grid=(pairs,),
            in_specs=[arrived_block] * groups
            + [
                chosen(tall, columns),
                chosen(columns, tall),
                chosen(ROWS, 128),
                fixed(HALF, 2 * HALF),
                fixed(2 * HALF, HALF),
            ]
            + unit_specs(parts, groups, pairs)
            + [
                stepped(tall, HALF),
                stepped(2, ROWS, 2 * HALF),
                stepped(4, ROWS, HALF),
            ],
            out_specs=[
                pl.BlockSpec((parts, groups, 1, 16, HALF), lambda b, pick_ref: (0, 0, b, 0, 0)),
                whole(HALF, 2 * HALF),
                whole(2 * HALF, HALF),
                whole(8, HALF),
            ],
        ),
        out_shape=[
            jax.ShapeDtypeStruct((parts, groups, pairs, 16, HALF), BF16),
            jax.ShapeDtypeStruct((HALF, 2 * HALF), F32),
            jax.ShapeDtypeStruct((2 * HALF, HALF), F32),
            jax.ShapeDtypeStruct((8, HALF), F32),
        ],
        compiler_params=SCHED,
        cost_estimate=cost(18, 12 * 1024 * 1024),
    )(pick, *arrived, adjoint, inverse, shift_row, one, two, *[normed] * groups, modes, sums, slopes)


def dense_body(
    tokens_ref,
    cotangent_ref,
    low_ref,
    high_ref,
    inverse_ref,
    table_ref,
    params_ref,
    in_bias_ref,
    in_ref,
    out_ref,
    *refs,
):
    (
        result_ref,
        mixed_grad_ref,
        second_ref,
        grad_low_ref,
        act_ref,
        grad_pre_ref,
        sent_ref,
        in_bias_grad_ref,
        rows_ref,
        branch_ref,
        grad_second_ref,
        normed_two_ref,
        inv_two_ref,
        normed_one_ref,
    ) = refs[-14:]
    chunk = pl.program_id(0)
    count = GROUP * LON
    wide = 2 * HALF

    @pl.when(chunk == 0)
    def _():
        inputs = tokens_ref[...].astype(F32).reshape(count, wide)
        normed, _ = normalise(inputs)
        normed_one_ref[...] = normed.astype(BF16)
        base = normed * params_ref[0:1, :] + params_ref[1:2, :] + inputs
        arrived = jnp.concatenate(
            [low_ref[...].reshape(count, HALF), high_ref[...].reshape(count, HALF)], axis=1
        )
        mixed = dot(inverse_ref[...], arrived, 1, 0) + base
        branch_ref[...] = mixed + params_ref[8:9, :]
        normed_two, inv_two = normalise(mixed)
        normed_two_ref[...] = normed_two
        inv_two_ref[...] = jnp.broadcast_to(inv_two, inv_two_ref.shape)
        second_ref[...] = (normed_two * params_ref[2:3, :] + params_ref[3:4, :]).astype(BF16)
        grad_low_ref[...] = (
            cotangent_ref[...].astype(F32).reshape(count, wide) * params_ref[13:14, :]
        ).astype(BF16)
        grad_second_ref[...] = jnp.zeros_like(grad_second_ref)

    pre = dot(second_ref[...], in_ref[...], 1, 0) + in_bias_ref[...]
    grad_act = dot(grad_low_ref[...], out_ref[...], 1, 1)
    act, slope = gelu_pair(pre)
    act = act.astype(BF16)
    grad_pre = grad_act * slope
    in_bias_grad_ref[...] = jnp.sum(grad_pre, axis=0, keepdims=True)
    grad_pre = grad_pre.astype(BF16)
    act_ref[...] = act
    grad_pre_ref[...] = grad_pre
    branch_ref[...] += dot(act, out_ref[...], 1, 0)
    grad_second_ref[...] += dot(grad_pre, in_ref[...], 1, 1)

    @pl.when(chunk == pl.num_programs(0) - 1)
    def _():
        result_ref[...] = branch_ref[...].astype(BF16).reshape(result_ref.shape)
        normed_two = normed_two_ref[...]
        inv_two = inv_two_ref[:, 0:1]
        upstream = grad_second_ref[...]
        scaled = upstream * params_ref[2:3, :]
        first_mean = jnp.mean(scaled, axis=-1, keepdims=True)
        second_mean = jnp.mean(scaled * normed_two, axis=-1, keepdims=True)
        grad_out = cotangent_ref[...].astype(F32).reshape(count, wide) * params_ref[13:14, :]
        mixed_grad = grad_out + inv_two * (scaled - first_mean - normed_two * second_mean)
        mixed_grad_ref[...] = mixed_grad.astype(BF16).reshape(mixed_grad_ref.shape)
        rows = [
            jnp.sum(part, axis=0, keepdims=True)
            for part in (upstream * normed_two, upstream, grad_low_ref[...].astype(F32))
        ]
        normed_one = normed_one_ref[...].astype(F32)
        rows += [
            jnp.sum(part, axis=0, keepdims=True) for part in (mixed_grad * normed_one, mixed_grad)
        ]
        rows_ref[...] = jnp.concatenate(rows + [jnp.zeros((3, wide), F32)], axis=0)
        sent = dot(table_ref[...], mixed_grad.astype(BF16), 1, 0).astype(BF16)
        sent_ref[...] = sent.reshape(sent_ref.shape)


def dense(
    kept, tokens, cotangent, low, high, places, inverse, table, params, in_bias, in_work, out_work, group
):
    parts, _, pairs = high.shape[:3]
    groups = tokens.shape[1] // GROUP
    count = GROUP * LON
    wide = 2 * HALF
    hidden = in_work.shape[1]

    def whole(*shape):
        return pl.BlockSpec(shape, lambda f: (0,) * len(shape))

    rows = pl.BlockSpec((1, GROUP, LON, wide), lambda f: (0, group, 0, 0))
    low_spec, high_spec = (
        pl.BlockSpec((parts, 1, pairs, 16, HALF), lambda f, place=place: (0, place, 0, 0, 0))
        for place in places
    )
    token_rows = pl.BlockSpec((count, wide), lambda f: (group, 0))
    hidden_rows = pl.BlockSpec((count, FCHUNK), lambda f: (group, f))
    return pl.pallas_call(
        dense_body,
        name="dense_group",
        grid=(hidden // FCHUNK,),
        in_specs=[
            rows,
            rows,
            low_spec,
            high_spec,
            whole(*inverse.shape),
            whole(*table.shape),
            whole(16, wide),
            pl.BlockSpec((1, FCHUNK), lambda f: (0, f)),
            pl.BlockSpec((wide, FCHUNK), lambda f: (0, f)),
            pl.BlockSpec((FCHUNK, wide), lambda f: (f, 0)),
        ]
        + [pl.BlockSpec(memory_space=pl.ANY)] * len(kept),
        out_specs=[
            rows,
            rows,
            token_rows,
            token_rows,
            hidden_rows,
            hidden_rows,
            whole(parts, pairs, 16, wide),
            pl.BlockSpec((1, FCHUNK), lambda f: (0, f)),
            whole(8, wide),
        ],
        out_shape=[
            jax.ShapeDtypeStruct(tokens.shape, BF16),
            jax.ShapeDtypeStruct(tokens.shape, BF16),
            jax.ShapeDtypeStruct((groups * count, wide), BF16),
            jax.ShapeDtypeStruct((groups * count, wide), BF16),
            jax.ShapeDtypeStruct((groups * count, hidden), BF16),
            jax.ShapeDtypeStruct((groups * count, hidden), BF16),
            jax.ShapeDtypeStruct((parts, pairs, 16, wide), BF16),
            jax.ShapeDtypeStruct((1, hidden), F32),
            jax.ShapeDtypeStruct((8, wide), F32),
        ],
        scratch_shapes=[pltpu.VMEM((count, wide), F32)] * 3
        + [pltpu.VMEM((count, 128), F32), pltpu.VMEM((count, wide), BF16)],
        input_output_aliases={10 + i: i for i in range(len(kept))},
        compiler_params=SCHED,
        cost_estimate=cost(25, 30 * 1024 * 1024),
    )(tokens, cotangent, low, high, inverse, table, params, in_bias, in_work, out_work, *kept)


def gather_grad_body(
    tokens_ref, mixed_grad_ref, low_ref, high_ref, inverse_ref, params_ref, grad_ref
):
    count = GROUP * LON
    wide = 2 * HALF
    mixed_grad = mixed_grad_ref[...].astype(F32).reshape(count, wide)
    low = dot(inverse_ref[...], low_ref[...].reshape(count, HALF), 1, 0)
    high = dot(inverse_ref[...], high_ref[...].reshape(count, HALF), 1, 0)
    upstream = mixed_grad + jnp.concatenate([low, high], axis=1)
    normed, inv_std = normalise(tokens_ref[...].astype(F32).reshape(count, wide))
    scaled = upstream * params_ref[0:1, :]
    first_mean = jnp.mean(scaled, axis=-1, keepdims=True)
    second_mean = jnp.mean(scaled * normed, axis=-1, keepdims=True)
    out = mixed_grad + inv_std * (scaled - first_mean - normed * second_mean)
    grad_ref[...] = out.reshape(grad_ref.shape)


def gather_grad(tokens, mixed_grad, low, high, inverse, params):
    parts, groups, pairs = low.shape[:3]
    wide = 2 * HALF

    def whole(*shape):
        return pl.BlockSpec(shape, lambda r: (0,) * len(shape))

    rows = pl.BlockSpec((1, GROUP, LON, wide), lambda r: (0, r, 0, 0))
    arrived = pl.BlockSpec((parts, 1, pairs, 16, HALF), lambda r: (0, r, 0, 0, 0))
    return pl.pallas_call(
        gather_grad_body,
        name="longitude_and_norm_grad",
        grid=(groups,),
        in_specs=[rows, rows, arrived, arrived, whole(*inverse.shape), whole(16, wide)],
        out_specs=rows,
        out_shape=jax.ShapeDtypeStruct((1, groups * GROUP, LON, wide), F32),
        compiler_params=SCHED,
        cost_estimate=cost(12, 16 * 1024 * 1024),
    )(tokens, mixed_grad, low, high, inverse, params)


def block_matrices(weight):
    size = weight.shape[1] // 4
    places = np.arange(HALF)
    pick = (np.arange(4 * size)[:, None, None] == np.arange(4)[:, None] * size + places % size)
    own = places[:, None] // size == places[None, :] // size
    halves = weight.reshape(2, HALF, 4 * size)

    def spread_columns(form, first):
        full = jnp.einsum(
            form, halves, jnp.asarray(pick[:, first : first + 2], BF16), preferred_element_type=F32
        )
        return full

    one = spread_columns("qrc,cpn->qrpn", 0) * own[:, None, :]
    two = spread_columns("qrc,cpn->qprn", 2) * own
    return (
        one.astype(BF16).reshape(2, HALF, 2 * HALF),
        two.astype(BF16).reshape(2, 2 * HALF, HALF),
    )


def own_blocks(matrix, size):
    count = HALF // size
    return jnp.concatenate(
        [matrix[i * size : (i + 1) * size, i * size : (i + 1) * size] for i in range(count)], axis=0
    )


def in_turn(values, last):
    return lax.optimization_barrier((values, last))[0]


def exchange(values, last=None):
    if last is not None:
        values = in_turn(values, last)
    return lax.all_to_all(values, "sp", split_axis=0, concat_axis=0, tiled=True)


AXES = ("y", "core", "sp")
BITS = (("y", 1), ("core", 1), ("sp", 4), ("sp", 2), ("sp", 1))
SIZES = {"y": 2, "core": 2, "sp": 8}


def swap(values, axis, bit):
    return lax.ppermute(values, axis, [(i, i ^ bit) for i in range(SIZES[axis])])


def mine(axis, bit):
    return (lax.axis_index(axis) // bit) % 2


def gather_bit(values, axis, bit, place=0, last=None):
    other = swap(values, axis, bit)
    if last is not None:
        other = in_turn(other, last)
    low = mine(axis, bit) == 0
    return jnp.stack([jnp.where(low, values, other), jnp.where(low, other, values)], axis=place)


def gather_steps(values, held, order, last=None):
    for axis, bit in order:
        held = sorted([*held, (axis, bit)], key=BITS.index)
        values = gather_bit(values, axis, bit, held.index((axis, bit)), last)
    return values, held


def scatter_small(values, last):
    held = list(BITS)
    values = values.reshape((2,) * len(held) + values.shape[1:])
    for step, (axis, bit) in enumerate(IN_ORDER):
        if step == 3:
            values = in_turn(values, last)
        place = held.index((axis, bit))
        keep = lax.dynamic_index_in_dim(values, mine(axis, bit), place, keepdims=False)
        give = lax.dynamic_index_in_dim(values, 1 - mine(axis, bit), place, keepdims=False)
        values = keep + swap(give, axis, bit)
        held.pop(place)
    return values


SMALL = pl.CostEstimate(flops=1 << 20, bytes_accessed=1 << 20, transcendentals=0)
IN_ORDER = (("core", 1), ("y", 1), ("sp", 1), ("sp", 2), ("sp", 4))
OUT_ORDER = (("core", 1), ("sp", 1), ("y", 1), ("sp", 2), ("sp", 4))


def device_rows(order):
    lists = []
    for core in range(2):
        indices = []
        for count in range(16):
            samp, sp = core, 0
            for place, (axis, bit) in enumerate(order[1:]):
                if count >> (3 - place) & 1:
                    samp, sp = (samp + 2 * bit, sp) if axis == "y" else (samp, sp + bit)
            indices.append(samp * 8 + sp)
        lists.append(indices)
    return lists


def in_weight_grad_body(pick_ref, second_ref, grad_pre_ref, keep_ref, give_ref):
    out = dot(second_ref[...], grad_pre_ref[...], 0, 0)
    rows = out.shape[0] // 32
    halves = [
        jnp.concatenate([out[i * rows : (i + 1) * rows] for i in indices], axis=0).astype(BF16)
        for indices in device_rows(IN_ORDER)
    ]

    @pl.when(pick_ref[0] == 0)
    def _():
        keep_ref[...] = halves[0]
        give_ref[...] = halves[1]

    @pl.when(pick_ref[0] == 1)
    def _():
        keep_ref[...] = halves[1]
        give_ref[...] = halves[0]


def in_weight_grad(core, second, grad_pre):
    tokens, wide = second.shape
    hidden = grad_pre.shape[1]
    step = 512
    half = pl.BlockSpec((wide // 2, step), lambda i, pick_ref: (0, i))
    return pl.pallas_call(
        in_weight_grad_body,
        name="in_weight_grad",
        grid_spec=pltpu.PrefetchScalarGridSpec(
            num_scalar_prefetch=1,
            grid=(hidden // step,),
            in_specs=[
                pl.BlockSpec((tokens, wide), lambda i, pick_ref: (0, 0)),
                pl.BlockSpec((tokens, step), lambda i, pick_ref: (0, i)),
            ],
            out_specs=[half, half],
        ),
        out_shape=[jax.ShapeDtypeStruct((wide // 2, hidden), BF16)] * 2,
        compiler_params=SCHED,
        cost_estimate=SMALL,
    )(core, second, grad_pre)


def out_weight_grad_body(pick_ref, act_ref, grad_low_ref, keep_ref, give_ref):
    out = dot(act_ref[...], grad_low_ref[...], 0, 0)
    rows = out.shape[0] // 8
    out = out.astype(BF16)
    pieces = [
        jnp.concatenate(
            [
                out[(z1 * 4 + z0 * 2 + x) * rows : (z1 * 4 + z0 * 2 + x + 1) * rows]
                for z0 in range(2)
                for z1 in range(2)
            ],
            axis=0,
        )
        for x in range(2)
    ]

    @pl.when(pl.program_id(0) == 0)
    def _():
        for x in range(2):
            keep_ref[x, 0] = pieces[x]

    @pl.when(pl.program_id(0) == 1)
    def _():
        for x in range(2):
            give_ref[x, 0] = pieces[x]


def out_weight_grad(core, act, grad_low):
    tokens, hidden = act.shape
    wide = grad_low.shape[1]
    part = hidden // 4
    shape = (2, 2, part // 2, wide)

    def columns(give, y, pick_ref):
        return (0, y * 2 + (pick_ref[0] + give) % 2)

    keep, give = pl.pallas_call(
        out_weight_grad_body,
        name="out_weight_grad",
        grid_spec=pltpu.PrefetchScalarGridSpec(
            num_scalar_prefetch=1,
            grid=(2, 2),
            in_specs=[
                pl.BlockSpec((tokens, part), columns),
                pl.BlockSpec((tokens, wide), lambda give, y, pick_ref: (0, 0)),
            ],
            out_specs=[
                pl.BlockSpec(
                    (2, 1) + shape[2:], lambda give, y, pick_ref: (0, jnp.maximum(y, give), 0, 0)
                ),
                pl.BlockSpec((2, 1) + shape[2:], lambda give, y, pick_ref: (0, y * give, 0, 0)),
            ],
        ),
        out_shape=[jax.ShapeDtypeStruct(shape, BF16)] * 2,
        compiler_params=SCHED,
        cost_estimate=SMALL,
    )(core, act, grad_low)
    return keep.reshape(-1, wide), give.reshape(-1, wide)


def add_split_body(pick_ref, keep_one, got_one, keep_two, got_two, keep_ref, give_ref):
    keep_ref[...] = (keep_one[...].astype(F32) + got_one[...].astype(F32)).astype(BF16)
    give_ref[...] = (keep_two[...].astype(F32) + got_two[...].astype(F32)).astype(BF16)


def add_split(pick, keep, got):
    rows, columns = keep.shape
    steps = 2 if rows % 64 == 0 else 1
    block = (rows // 2 // steps, columns)
    stays = pl.BlockSpec(block, lambda i, pick_ref: (pick_ref[0] * steps + i, 0))
    goes = pl.BlockSpec(block, lambda i, pick_ref: ((1 - pick_ref[0]) * steps + i, 0))
    out = pl.BlockSpec(block, lambda i, pick_ref: (i, 0))
    return pl.pallas_call(
        add_split_body,
        name="add_split",
        grid_spec=pltpu.PrefetchScalarGridSpec(
            num_scalar_prefetch=1,
            grid=(steps,),
            in_specs=[stays, stays, goes, goes],
            out_specs=[out, out],
        ),
        out_shape=[jax.ShapeDtypeStruct((rows // 2, columns), BF16)] * 2,
        compiler_params=SCHED,
        cost_estimate=SMALL,
    )(pick, keep, got, keep, got)


def picks(order):
    return [mine(axis, bit).astype(jnp.int32).reshape(1) for axis, bit in order]


def scatter_steps(keep, give, order, chosen, first, last):
    for place in range(first, last):
        keep, give = add_split(chosen[place + 1], keep, swap(give, *order[place]))
    return keep, give


def scatter_last(keep, give, order):
    return keep.astype(F32) + swap(give, *order[-1]).astype(F32)


def fast_shards(
    sizes,
    tokens,
    cotangent,
    storm_weight,
    filter_master,
    in_master,
    out_master,
    small_master,
    filter_m,
    filter_v,
    in_m,
    in_v,
    out_m,
    out_v,
    small_m,
    small_v,
    filter_ema,
    in_ema,
    out_ema,
    small_ema,
):
    parts = sizes[1]
    devices = sizes[0] * sizes[1]
    groups = tokens.shape[1] // GROUP
    pairs = LON // 4 // parts
    width = tokens.shape[-1]
    block = width // NB
    small_share = small_master.shape[0]
    sp_index = lax.axis_index("sp")

    lon = lon_matrix()
    lon_table = jnp.asarray(lon, BF16)
    lon_back = jnp.asarray(lon.T, BF16)
    tables = lat_tables(parts)
    pick = jnp.where((sp_index == 0) & (jnp.arange(pairs) == 0), 0, 1).astype(jnp.int32)

    filter_rows = filter_master.shape[0]
    small_row = jnp.pad(small_master, (0, 4 * block - small_share)).reshape(1, -1)
    in_gather, out_gather = IN_ORDER[::-1], IN_ORDER[::-1]
    in_part, in_held = gather_steps(in_master.astype(BF16), [], in_gather[:1])
    out_part, out_held = gather_steps(out_master.astype(BF16), [], out_gather[:1])
    sent = spread(tokens, lon_table, filter_master, small_row, parts)
    arrived_low = exchange(sent[0], (in_part, out_part))
    arrived_high = exchange(sent[1], arrived_low)

    units = groups * pairs
    near = arrived_low[:, units:].reshape(parts, -1, 4 * block)
    packed_all = gather_bit(gather_bit(near, "core", 1), "y", 1)
    packed_all = packed_all.reshape((devices,) + near.shape[1:])
    filter_work = packed_all[:, :filter_rows].reshape(width, 4 * block)
    small_work = packed_all[:, filter_rows, :small_share].reshape(-1)

    in_rows, hidden = in_master.shape
    params = small_work.astype(F32).reshape(13, width)
    scale = storm_weight.astype(F32)[0] / 64.0
    in_bias = params[9:13].reshape(1, -1)
    params = jnp.concatenate(
        [params, jnp.full((1, width), scale, F32), jnp.zeros((2, width), F32)], axis=0
    )
    one, two = block_matrices(filter_work)
    params, in_bias = lax.optimization_barrier((params, in_bias))

    in_part, in_held = gather_steps(in_part, in_held, in_gather[1:2])
    out_part, out_held = gather_steps(out_part, out_held, out_gather[1:2])
    in_part, out_part = in_turn((in_part, out_part), arrived_low)
    forward_low = filter_forward(pick, arrived_low, tables, params, one, two, 0, (groups,))
    in_part, in_held = gather_steps(in_part, in_held, in_gather[2:3], forward_low[0])
    out_part, out_held = gather_steps(out_part, out_held, out_gather[2:3], forward_low[0])
    returned_low = exchange(forward_low[0], arrived_high)
    high_pieces = (1, groups - 1) if groups > 1 else (1,)
    forward_high = filter_forward(pick, arrived_high, tables, params, one, two, 1, high_pieces)
    last = returned_low
    returned_high = []
    for piece in range(len(high_pieces)):
        last = exchange(forward_high[piece], last)
        returned_high.append(last)
    in_part, in_held = gather_steps(in_part, in_held, in_gather[3:4], returned_high[0])
    in_work = gather_steps(in_part, in_held, in_gather[4:])[0].reshape(width, hidden)
    out_part, out_held = gather_steps(out_part, out_held, out_gather[3:4], forward_high[0])
    out_work = gather_steps(out_part, out_held, out_gather[4:])[0].reshape(hidden, width)
    kept = []
    grad_arrived = []
    dense_rows = 0.0
    in_bias_grad = 0.0
    for group in range(groups):
        piece = min(group, 1)
        *kept, sent_piece, bias_piece, rows_piece = dense(
            kept,
            tokens,
            cotangent,
            returned_low,
            returned_high[piece],
            (group, group - piece),
            lon_back,
            lon_table,
            params,
            in_bias,
            in_work,
            out_work,
            group,
        )
        in_bias_grad = in_bias_grad + bias_piece
        dense_rows = dense_rows + rows_piece
        before_last = last
        last = exchange(sent_piece, last)
        grad_arrived.append(last)
    result, mixed_grad, second, grad_low, act, grad_pre = kept
    act, grad_pre = in_turn((act, grad_pre), before_last)
    in_picks, out_picks = picks(IN_ORDER), picks(OUT_ORDER)
    out_part, in_part = in_turn(
        (
            out_weight_grad(out_picks[0], act, grad_low),
            in_weight_grad(in_picks[0], second, grad_pre),
        ),
        last,
    )
    out_part = scatter_steps(*out_part, OUT_ORDER, out_picks, 0, 1)
    in_part = scatter_steps(*in_part, IN_ORDER, in_picks, 0, 1)

    backward = []
    grad_returned = []
    for q, (normed, forward) in enumerate(
        ((arrived_low, forward_low), (arrived_high, forward_high))
    ):
        if q == 1:
            grad_arrived = in_turn(grad_arrived, (in_part, out_part))
        backward.append(
            filter_backward(pick, grad_arrived, tables, one, two, normed, *forward[-3:], q)
        )
        if q == 1:
            out_part = scatter_steps(*out_part, OUT_ORDER, out_picks, 1, 2)
            in_part = scatter_steps(*in_part, IN_ORDER, in_picks, 1, 2)
            last = (last, out_part, in_part)
            second_half = last
        last = exchange(backward[q][0], last)
        grad_returned.append(last)

    out_part = scatter_steps(*out_part, OUT_ORDER, out_picks, 2, 3)
    in_part = scatter_steps(*in_part, IN_ORDER, in_picks, 2, 3)
    out_part = scatter_steps(*out_part, OUT_ORDER, out_picks, 3, 4)
    in_part = scatter_steps(*in_part, IN_ORDER, in_picks, 3, 4)
    out_part, in_part = in_turn((out_part, in_part), last)
    out_grad = scatter_last(*out_part, OUT_ORDER)
    in_grad = scatter_last(*in_part, IN_ORDER)

    pieces = []
    for q in range(2):
        one_grad, two_grad = in_turn((backward[q][1], backward[q][2]), second_half)
        pieces.append(
            jnp.concatenate(
                [
                    own_blocks(one_grad[:, :HALF], block),
                    own_blocks(one_grad[:, HALF:], block),
                    own_blocks(two_grad[:HALF], block),
                    own_blocks(two_grad[HALF:], block),
                ],
                axis=1,
            )
        )
    filter_local = jnp.concatenate(pieces, axis=0).reshape(devices, filter_rows, 4 * block)
    bias_rows = jnp.concatenate([backward[0][3], backward[1][3]], axis=1)
    small_rows = jnp.concatenate(
        [
            dense_rows[3:5] + bias_rows[4:6],
            dense_rows[0:2],
            bias_rows[0:2],
            bias_rows[2:3] + bias_rows[2:3],
            bias_rows[3:4] - bias_rows[3:4],
            dense_rows[2:3],
            in_bias_grad.reshape(4, width),
        ],
        axis=0,
    )

    def shares(rows):
        flat = rows.reshape(-1)
        flat = jnp.pad(flat, (0, devices * small_share - flat.shape[0]))
        return jnp.pad(flat.reshape(devices, small_share), ((0, 0), (0, 4 * block - small_share)))

    early = scatter_small(
        jnp.concatenate([filter_local, shares(small_rows)[:, None]], axis=1), last
    )
    filter_grad = early[:filter_rows]
    small_grad = early[filter_rows, :small_share]

    input_grad = gather_grad(
        tokens,
        mixed_grad,
        grad_returned[0],
        grad_returned[1],
        lon_back,
        params,
    )

    filter_new, filter_m_new, filter_v_new, filter_ema_new = adam_update(
        filter_master, filter_grad, filter_m, filter_v, filter_ema, 0.2
    )
    in_new, in_m_new, in_v_new, in_ema_new = adam_update(
        in_master, in_grad, in_m, in_v, in_ema, 0.1
    )
    out_new, out_m_new, out_v_new, out_ema_new = adam_update(
        out_master, out_grad, out_m, out_v, out_ema, 0.05
    )
    small_new, small_m_new, small_v_new, small_ema_new = adam_update(
        small_master, small_grad, small_m, small_v, small_ema, 0.5
    )
    return (
        result,
        input_grad,
        filter_grad,
        in_grad,
        out_grad,
        small_grad,
        filter_new,
        in_new,
        out_new,
        small_new,
        filter_m_new,
        filter_v_new,
        in_m_new,
        in_v_new,
        out_m_new,
        out_v_new,
        small_m_new,
        small_v_new,
        filter_ema_new,
        in_ema_new,
        out_ema_new,
        small_ema_new,
    )


def solution(mesh):
    sizes = (mesh.shape["samp"], mesh.shape["sp"])
    samp = "samp"
    body = plain_shards
    if fits(sizes):
        samp = ("y", "core")
        mesh = Mesh(mesh.devices.reshape(2, 2, sizes[1]), AXES)
        body = functools.partial(fast_shards, sizes)
    every = (*samp, "sp") if isinstance(samp, tuple) else (samp, "sp")
    return jax.shard_map(
        body,
        mesh=mesh,
        in_specs=(
            P(samp, "sp", None, None),
            P(samp, "sp", None, None),
            P(samp),
            P(every, None),
            P(every, None),
            P(every, None),
            P(every),
            P(every, None),
            P(every, None),
            P(every, None),
            P(every, None),
            P(every, None),
            P(every, None),
            P(every),
            P(every),
            P(every, None),
            P(every, None),
            P(every, None),
            P(every),
        ),
        out_specs=(
            P(samp, "sp", None, None),
            P(samp, "sp", None, None),
            P(every, None),
            P(every, None),
            P(every, None),
            P(every),
            P(every, None),
            P(every, None),
            P(every, None),
            P(every),
            P(every, None),
            P(every, None),
            P(every, None),
            P(every, None),
            P(every, None),
            P(every, None),
            P(every),
            P(every),
            P(every, None),
            P(every, None),
            P(every, None),
            P(every),
        ),
        check_vma=False,
    )
```
